512 devices in a mesh: cuts: 16 (over x_hi, y), space: 32 (over z, x_lo, core).
Axes of the slice: x: 4 (x_hi: 2, x_lo: 2; x = x_hi * 2 + x_lo), y: 8, z: 8, core: 2. Of those that a mesh axis runs over, the one named last changes fastest.
Arguments:
- starts: float32 [16, 128, 64, 512], P('cuts', 'space'), may hold values from -6 to 6
- velocity: float32 [3, 128, 64, 512], P(None, 'space'), may hold values from -1 to 1
- diffusivity: float32 [128, 64, 512], P('space'), may hold values from 0.02 to 0.1
Outputs:
- new_ends: float32 [16, 128, 64, 512], P('cuts', 'space')
The draws below stay inside these ranges and needn't reach their ends.
All inputs are finite; a program needn't handle non-finite values.
Results may differ from the reference program's by a relative error of at most 0.00002.
Values sent between devices are 32-bit elements; how exact they have to be, the bound alone decides.
No kernel may reach another device: no remote copies, remote signals or barrier semaphores. Data moves between devices by JAX's collectives and lax.ppermute only.
A program may use at most 64 MiB of HBM per device.

```python
import math
import jax
import jax.numpy as jnp
from jax import lax

NY = 64
NZ = 512
RATIO = 4
FINE_STEPS = 16
COARSE_STEPS = 4
SLICES = 16
NX = 128


def block_scale(key, dims, cuts, low, top_value):
    factor_of = 1.0
    for position, blocks in cuts:
        steps = jax.random.uniform(jax.random.fold_in(jax.random.fold_in(key, 6), position), (blocks,), jnp.float32, low / len(cuts), top_value / len(cuts))
        factor_of = factor_of * jnp.repeat(jnp.exp(steps), dims[position] // blocks).reshape((-1,) + (1,) * (len(dims) - 1 - position))
    return factor_of


def scatter_about(stream_key, extent, scale, most, shards=(), kind=jnp.bfloat16):
    gain = block_scale(stream_key, extent, shards, -0.22, 0.18) if shards else 1.0
    array = jax.random.normal(stream_key, extent, jnp.float32) * scale * gain
    return jnp.minimum(jnp.maximum(array, -most), most).astype(kind)


def setup_inputs(seed: int = 0) -> dict:
    keys = jax.random.split(jax.random.key(seed), 4)
    starts = scatter_about(keys[0], (SLICES, NX, NY, NZ), 1.0, 6.0, ((0, 16), (1, 32)), jnp.float32)
    velocity = jnp.clip(jax.random.uniform(keys[1], (3, NX, NY, NZ), jnp.float32, -1.0, 1.0) * block_scale(keys[1], (3, NX, NY, NZ), ((1, 32),), -0.4, 0.0), -1.0, 1.0)
    diffusivity = jnp.clip(jnp.exp(math.log(0.1) - 1.609438 * jax.random.uniform(keys[2], (NX, NY, NZ), jnp.float32) ** block_scale(keys[2], (NX, NY, NZ), ((0, 32),), -0.2, 0.2)), 0.02, 0.1)
    return dict(starts=starts, velocity=velocity, diffusivity=diffusivity)


time_step = 0.2


def advance(extended, velocity, diffusion, step_size, spacing):
    centre = extended[1:-1]
    forward_x = extended[2:]
    backward_x = extended[:-2]
    forward_y = jnp.roll(centre, -1, 1)
    backward_y = jnp.roll(centre, 1, 1)
    forward_z = jnp.roll(centre, -1, 2)
    backward_z = jnp.roll(centre, 1, 2)
    transport = jnp.maximum(velocity[0], 0.0) * (centre - backward_x) + jnp.minimum(velocity[0], 0.0) * (forward_x - centre)
    transport = transport + jnp.maximum(velocity[1], 0.0) * (centre - backward_y) + jnp.minimum(velocity[1], 0.0) * (forward_y - centre)
    transport = transport + jnp.maximum(velocity[2], 0.0) * (centre - backward_z) + jnp.minimum(velocity[2], 0.0) * (forward_z - centre)
    laplace = forward_x + backward_x + forward_y + backward_y + forward_z + backward_z - 6.0 * centre
    return centre + step_size * (diffusion * laplace / (spacing * spacing) - transport / spacing)


def periodic(current):
    return jnp.concatenate([current[-1:], current, current[:1]], axis=0)


def restrict(current):
    extent_x, extent_y, extent_z = current.shape
    blocks = current.reshape(extent_x // RATIO, RATIO, extent_y // RATIO, RATIO, extent_z // RATIO, RATIO)
    return jnp.mean(blocks, axis=(1, 3, 5))


def prolong(current):
    extent_x, extent_y, extent_z = current.shape
    spread = jnp.broadcast_to(current[:, None, :, None, :, None], (extent_x, RATIO, extent_y, RATIO, extent_z, RATIO))
    return spread.reshape(extent_x * RATIO, extent_y * RATIO, extent_z * RATIO)


def fine_run(current, velocity, diffusion):
    def one_step(substep, state_now):
        return advance(periodic(state_now), velocity, diffusion, time_step, 1.0)
    return lax.fori_loop(0, FINE_STEPS, one_step, current)


def coarse_run(current, velocity, diffusion):
    def one_step(substep, state_now):
        return advance(periodic(state_now), velocity, diffusion, time_step * RATIO, 1.0 * RATIO)
    return lax.fori_loop(0, COARSE_STEPS, one_step, current)


def reference(starts, velocity, diffusivity):
    coarse_velocity = jnp.stack([restrict(velocity[component]) for component in range(3)])
    coarse_diffusion = restrict(diffusivity)
    fine_ends = lax.map(lambda current: fine_run(current, velocity, diffusivity), starts)
    coarse_old = lax.map(restrict, starts)
    image_old = lax.map(lambda current: coarse_run(current, coarse_velocity, coarse_diffusion), coarse_old)
    jump_terms = lax.map(restrict, fine_ends) - image_old

    def link_step(carried, jump_term):
        projected = coarse_run(carried, coarse_velocity, coarse_diffusion)
        return projected + jump_term, projected

    last_state, image_new = lax.scan(link_step, coarse_old[0], jump_terms)
    return lax.map(lambda triple: (prolong(triple[0]) + triple[1]) - prolong(triple[2]), (image_new, fine_ends, image_old))
```

```python
import functools

import jax
import jax.numpy as jnp
from jax import lax
from jax.experimental import pallas as pl
from jax.experimental.pallas import tpu as pltpu
from jax.sharding import PartitionSpec as P

RATIO = 4
LAYERS = 4
REACH = 3
TILE = (8, 4, 8, 128)
COARSE = (2, 8, 128)
ROUNDS = (1, 4, 4, 4, 3)
STEP = 0.2
VMEM = pl.BlockSpec(memory_space=pltpu.VMEM)
F32 = jnp.float32
MIB = 1024 * 1024


def call(body, outs, scratch=(), smem=0, ins=0, limit=32):
    specs = [pl.BlockSpec(memory_space=pltpu.SMEM)] * smem + [VMEM] * ins
    return pl.pallas_call(
        body,
        out_shape=[jax.ShapeDtypeStruct(s, F32) for s in outs],
        in_specs=specs,
        out_specs=[VMEM] * len(outs),
        scratch_shapes=list(scratch),
        compiler_params=pltpu.CompilerParams(vmem_limit_bytes=limit * MIB),
    )


def comb(transposed):
    a = lax.broadcasted_iota(jnp.int32, (512, 512), 0)
    b = lax.broadcasted_iota(jnp.int32, (512, 512), 1)
    natural, apart = (b, a) if transposed else (a, b)
    hit = natural == 4 * (apart & 127) + (apart >> 7)
    return jnp.where(hit, 1.0, 0.0).astype(jnp.bfloat16)


def exact_dot(rows, matrix):
    high = rows.astype(jnp.bfloat16)
    rest = rows - high.astype(F32)
    middle = rest.astype(jnp.bfloat16)
    low = (rest - middle.astype(F32)).astype(jnp.bfloat16)
    dot = functools.partial(jnp.dot, preferred_element_type=F32)
    return (dot(high, matrix) + dot(middle, matrix)) + dot(low, matrix)


def split_layer(rows, matrix, buffer):
    apart = exact_dot(rows, matrix)
    for q in range(4):
        buffer[q] = apart[:, q * 128 : (q + 1) * 128]
    return [[buffer[q, pl.ds(j, 8, stride=8), :] for q in range(4)] for j in range(8)]


def half_sum(tiles, h):
    total = None
    for j in range(4 * h, 4 * h + 4):
        for q in range(4):
            total = tiles[j][q] if total is None else total + tiles[j][q]
    return total


def state_kernel(starts, state, first, last, coarse, buffer):
    matrix = comb(False)
    sums = [None, None]
    for x in range(LAYERS):
        tiles = split_layer(starts[0, x], matrix, buffer.at[x])
        for j in range(8):
            for q in range(4):
                state[x, j, q] = tiles[j][q]
                if x == 0:
                    first[0, j, q] = tiles[j][q]
                if x == LAYERS - 1:
                    last[0, j, q] = tiles[j][q]
        for h in range(2):
            part = half_sum(tiles, h)
            sums[h] = part if sums[h] is None else sums[h] + part
    for h in range(2):
        coarse[h] = sums[h] * (1.0 / 64)


def weigh(velocity, diffusion, step, spacing):
    spread = diffusion * (step / (spacing * spacing))
    weights = [None]
    for component in velocity:
        moved = component * (step / spacing)
        weights.append(spread + jnp.maximum(moved, 0.0))
        weights.append(spread - jnp.minimum(moved, 0.0))
    total = weights[1]
    for weight in weights[2:]:
        total = total + weight
    weights[0] = 1.0 - total
    return weights


def field_kernel(velocity, diffusivity, own, head, tail, coarse, buffer):
    matrix = comb(False)
    for f in range(4):
        for h in range(2):
            coarse[f, h] = jnp.zeros((8, 128), F32)

    def layer(x, carry):
        for f in range(4):
            rows = velocity[f, x] if f < 3 else diffusivity[x]
            tiles = split_layer(rows, matrix, buffer.at[f])
            for h in range(2):
                coarse[f, h] += half_sum(tiles, h) * (1.0 / 64)
            for j in range(8):
                for q in range(4):
                    own[x, f, j, q] = tiles[j][q]
        return carry

    lax.fori_loop(0, LAYERS, layer, 0)
    head[...] = own[:REACH]
    tail[...] = own[LAYERS - REACH :]


def weight_kernel(count, fields, weights):
    def layer(x, carry):
        for j in range(8):
            for q in range(4):
                parts = [fields[x, f, j, q] for f in range(4)]
                for i, weight in enumerate(weigh(parts[:3], parts[3], STEP, 1.0)):
                    weights[x, i, j, q] = weight
        return carry

    lax.fori_loop(0, count, layer, 0)


def fine_layer(source, weights, target, x, wx, tx):
    tiles = [[source[x, j, q] for q in range(4)] for j in range(8)]
    for j in range(8):
        for q in range(4):
            behind_y = tiles[j - 1][q] if j > 0 else pltpu.roll(tiles[7][q], 1, 0)
            ahead_y = tiles[j + 1][q] if j < 7 else pltpu.roll(tiles[0][q], 7, 0)
            behind_z = tiles[j][q - 1] if q > 0 else pltpu.roll(tiles[j][3], 1, 1)
            ahead_z = tiles[j][q + 1] if q < 3 else pltpu.roll(tiles[j][0], 127, 1)
            target[tx, j, q] = (
                (weights[wx, 0, j, q] * tiles[j][q] + weights[wx, 1, j, q] * source[x - 1, j, q])
                + (weights[wx, 2, j, q] * source[x + 1, j, q] + weights[wx, 3, j, q] * behind_y)
                + (weights[wx, 4, j, q] * ahead_y + weights[wx, 5, j, q] * behind_z)
                + weights[wx, 6, j, q] * ahead_z
            )


def round_kernel(width, final, *refs):
    if width > 1:
        state, left, right, own, own_left, own_right, *refs = refs
    else:
        state, left, right, own, *refs = refs
        own_left = own_right = None
    if final:
        later, out, residual, one, two = refs
    else:
        out, one, two = refs
    for x in range(width):
        one[LAYERS - width + x] = left[x]
        one[2 * LAYERS + x] = right[x]
    for x in range(LAYERS):
        one[LAYERS + x] = state[x]
    source, target = one, two
    for step in range(1, width + 1):
        ends = step == width
        goal = out if ends else target
        shift = LAYERS if ends else 0

        def sweep(begin, end, weights, offset, source=source, goal=goal, shift=shift):
            if end <= begin:
                return

            def body(x, carry):
                fine_layer(source, weights, goal, x, x - offset, x - shift)
                return carry

            lax.fori_loop(begin, end, body, 0)

        sweep(LAYERS - width + step, LAYERS, own_left, LAYERS - REACH)
        sweep(LAYERS, 2 * LAYERS, own, LAYERS)
        sweep(2 * LAYERS, 2 * LAYERS + width - step, own_right, 2 * LAYERS)
        source, target = target, source
    if final:
        for h in range(2):
            total = None
            for x in range(LAYERS):
                part = half_sum([[out[x, j, q] for q in range(4)] for j in range(8)], h)
                total = part if total is None else total + part
            residual[h] = total * (1.0 / 64) - later[h]


def coarse_step(read, weights, write, count):
    first = read(0)
    behind, now = read(count - 1), first
    for x in range(count):
        ahead = read(x + 1) if x + 1 < count else first
        for h in range(2):
            behind_y = now[0] if h else pltpu.roll(now[1], 1, 0)
            ahead_y = pltpu.roll(now[0], 7, 0) if h else now[1]
            behind_z = pltpu.roll(now[h], 1, 1)
            ahead_z = pltpu.roll(now[h], 127, 1)
            write(
                x,
                h,
                (weights[x, 0, h] * now[h] + weights[x, 1, h] * behind[h])
                + (weights[x, 2, h] * ahead[h] + weights[x, 3, h] * behind_y)
                + (weights[x, 4, h] * ahead_y + weights[x, 5, h] * behind_z)
                + weights[x, 6, h] * ahead_z,
            )
        behind, now = now, ahead


def chain_kernel(place, residuals, fields, state, out, weights, one, two, buffer):
    count = fields.shape[0]
    slice_index = place[0]
    layer_index = place[1]

    def prepare(x, carry):
        for h in range(2):
            parts = [fields[x, f, h] for f in range(4)]
            for i, weight in enumerate(weigh(parts[:3], parts[3], STEP * RATIO, 1.0 * RATIO)):
                weights[x, i, h] = weight
            one[x, h] = jnp.zeros((8, 128), F32)
        return carry

    lax.fori_loop(0, count, prepare, 0)

    def reader(ref):
        return lambda x: [ref[x, h] for h in range(2)]

    def writer(ref):
        def write(x, h, value):
            ref[x, h] = value

        return write

    def link(m, carry):
        def entering(x):
            return [one[x, h] + residuals[x, m, h] for h in range(2)]

        coarse_step(entering, weights, writer(two), count)
        coarse_step(reader(two), weights, writer(one), count)
        coarse_step(reader(one), weights, writer(two), count)
        coarse_step(reader(two), weights, writer(one), count)
        return carry

    lax.fori_loop(0, slice_index, link, 0)
    change = [one[layer_index, h] for h in range(2)]
    matrix = comb(True)
    for x in range(LAYERS):
        for j in range(8):
            for q in range(4):
                buffer[x, q, pl.ds(j, 8, stride=8), :] = state[x, j, q] + change[j // 4]
        rows = jnp.concatenate([buffer[x, q] for q in range(4)], axis=1)
        out[0, x] = exact_dot(rows, matrix)


def shift(block, axis, distance):
    count = lax.axis_size(axis)
    return lax.ppermute(block, axis, [(i, (i + distance) % count) for i in range(count)])


def shards(starts, velocity, diffusivity):
    count = lax.axis_size("space")
    block = (LAYERS, *TILE)
    state, first, last, coarse_old = call(
        state_kernel,
        [block, (1, *TILE), (1, *TILE), COARSE],
        [pltpu.VMEM((LAYERS, 4, 64, 128), F32)],
        ins=1,
    )(starts)
    left, right = shift(last, "space", 1), shift(first, "space", -1)
    own, head, tail, coarse_fields = call(
        field_kernel,
        [(LAYERS, 4, *TILE), (REACH, 4, *TILE), (REACH, 4, *TILE), (4, *COARSE)],
        [pltpu.VMEM((4, 4, 64, 128), F32)],
        ins=2,
    )(velocity, diffusivity)
    fields_left, fields_right = shift(tail, "space", 1), shift(head, "space", -1)
    coarse_later = shift(coarse_old, "cuts", -1)
    all_fields = lax.all_gather(coarse_fields, "space")

    def weights_of(fields):
        layers = fields.shape[0]
        return call(functools.partial(weight_kernel, layers), [(layers, 7, *TILE)], ins=1)(fields)[0]

    own_weights = weights_of(own)
    scratch = [pltpu.VMEM((3 * LAYERS, *TILE), F32)] * 2
    sides = None
    for index, width in enumerate(ROUNDS):
        final = index == len(ROUNDS) - 1
        if index > 0:
            left = shift(state[LAYERS - width :], "space", 1)
            right = shift(state[:width], "space", -1)
        operands = [state, left, right, own_weights]
        if width > 1:
            if sides is None:
                sides = [weights_of(fields_left), weights_of(fields_right)]
            operands += sides
        if final:
            operands.append(coarse_later)
        outs = call(
            functools.partial(round_kernel, width, final),
            [block, COARSE] if final else [block],
            scratch,
            ins=len(operands),
        )(*operands)
        state = outs[0]
    residuals = lax.all_gather(lax.all_gather(outs[1], "cuts"), "space")
    place = jnp.stack([lax.axis_index("cuts"), lax.axis_index("space")]).astype(jnp.int32)
    return call(
        chain_kernel,
        [(1, LAYERS, 64, 512)],
        [
            pltpu.VMEM((count, 7, *COARSE), F32),
            pltpu.VMEM((count, *COARSE), F32),
            pltpu.VMEM((count, *COARSE), F32),
            pltpu.VMEM((LAYERS, 4, 64, 128), F32),
        ],
        smem=1,
        ins=3,
    )(place, residuals, all_fields, state)[0]


def solution(mesh):
    placed = (P("cuts", "space", None, None), P(None, "space", None, None), P("space", None, None))
    return jax.shard_map(
        shards,
        mesh=mesh,
        in_specs=placed,
        out_specs=P("cuts", "space", None, None),
        check_vma=False,
    )
```

```python
import functools

import jax
import jax.numpy as jnp
from jax import lax
from jax.experimental import pallas as pl
from jax.experimental.pallas import tpu as pltpu
from jax.sharding import PartitionSpec as P

RATIO = 4
LAYERS = 4
REACH = 3
TILE = (8, 4, 8, 128)
COARSE = (2, 8, 128)
ROUNDS = (1, 2, 2, 4, 4, 3)
STEP = 0.2
VMEM = pl.BlockSpec(memory_space=pltpu.VMEM)
F32 = jnp.float32
MIB = 1024 * 1024


def call(body, outs, scratch=(), smem=0, ins=0, limit=32, after=0):
    specs = [pl.BlockSpec(memory_space=pltpu.SMEM)] * smem + [VMEM] * ins
    specs += [pl.BlockSpec(memory_space=pl.ANY)] * after
    return pl.pallas_call(
        body,
        out_shape=[jax.ShapeDtypeStruct(s, F32) for s in outs],
        in_specs=specs,
        out_specs=[VMEM] * len(outs),
        scratch_shapes=list(scratch),
        compiler_params=pltpu.CompilerParams(vmem_limit_bytes=limit * MIB),
    )


def comb(transposed):
    a = lax.broadcasted_iota(jnp.int32, (512, 512), 0)
    b = lax.broadcasted_iota(jnp.int32, (512, 512), 1)
    natural, apart = (b, a) if transposed else (a, b)
    hit = natural == 4 * (apart & 127) + (apart >> 7)
    return jnp.where(hit, 1.0, 0.0).astype(jnp.bfloat16)


def exact_dot(rows, matrix):
    high = rows.astype(jnp.bfloat16)
    rest = rows - high.astype(F32)
    middle = rest.astype(jnp.bfloat16)
    low = (rest - middle.astype(F32)).astype(jnp.bfloat16)
    dot = functools.partial(jnp.dot, preferred_element_type=F32)
    return (dot(high, matrix) + dot(middle, matrix)) + dot(low, matrix)


def split_layer(rows, matrix, buffer):
    apart = exact_dot(rows, matrix)
    for q in range(4):
        buffer[q] = apart[:, q * 128 : (q + 1) * 128]
    return [[buffer[q, pl.ds(j, 8, stride=8), :] for q in range(4)] for j in range(8)]


def half_sum(tiles, h):
    total = None
    for j in range(4 * h, 4 * h + 4):
        for q in range(4):
            total = tiles[j][q] if total is None else total + tiles[j][q]
    return total


def state_kernel(starts, state, first, last, coarse, buffer):
    matrix = comb(False)
    sums = [None, None]
    for x in range(LAYERS):
        tiles = split_layer(starts[0, x], matrix, buffer.at[x])
        for j in range(8):
            for q in range(4):
                state[x, j, q] = tiles[j][q]
                if x == 0:
                    first[0, j, q] = tiles[j][q]
                if x == LAYERS - 1:
                    last[0, j, q] = tiles[j][q]
        for h in range(2):
            part = half_sum(tiles, h)
            sums[h] = part if sums[h] is None else sums[h] + part
    for h in range(2):
        coarse[h] = sums[h] * (1.0 / 64)


def weigh(velocity, diffusion, step, spacing):
    spread = diffusion * (step / (spacing * spacing))
    weights = [None]
    for component in velocity:
        moved = component * (step / spacing)
        weights.append(spread + jnp.maximum(moved, 0.0))
        weights.append(spread - jnp.minimum(moved, 0.0))
    total = weights[1]
    for weight in weights[2:]:
        total = total + weight
    weights[0] = 1.0 - total
    return weights


def field_kernel(velocity, diffusivity, earlier, own, first, head, last, tail, coarse, buffer):
    matrix = comb(False)
    for f in range(4):
        for h in range(2):
            coarse[f, h] = jnp.zeros((8, 128), F32)

    def layer(x, carry):
        for f in range(4):
            rows = velocity[f, x] if f < 3 else diffusivity[x]
            tiles = split_layer(rows, matrix, buffer.at[f])
            for h in range(2):
                coarse[f, h] += half_sum(tiles, h) * (1.0 / 64)
            for j in range(8):
                for q in range(4):
                    own[x, f, j, q] = tiles[j][q]
        return carry

    lax.fori_loop(0, LAYERS, layer, 0)
    first[...] = own[:1]
    head[...] = own[1:REACH]
    last[...] = own[LAYERS - 1 :]
    tail[...] = own[LAYERS - REACH : LAYERS - 1]


def weight_kernel(count, fields, weights):
    def layer(x, carry):
        for j in range(8):
            for q in range(4):
                parts = [fields[x, f, j, q] for f in range(4)]
                for i, weight in enumerate(weigh(parts[:3], parts[3], STEP, 1.0)):
                    weights[x, i, j, q] = weight
        return carry

    lax.fori_loop(0, count, layer, 0)


def fine_layer(source, weights, target, x, wx, tx):
    tiles = [[source[x, j, q] for q in range(4)] for j in range(8)]
    for j in range(8):
        for q in range(4):
            behind_y = tiles[j - 1][q] if j > 0 else pltpu.roll(tiles[7][q], 1, 0)
            ahead_y = tiles[j + 1][q] if j < 7 else pltpu.roll(tiles[0][q], 7, 0)
            behind_z = tiles[j][q - 1] if q > 0 else pltpu.roll(tiles[j][3], 1, 1)
            ahead_z = tiles[j][q + 1] if q < 3 else pltpu.roll(tiles[j][0], 127, 1)
            target[tx, j, q] = (
                (weights[wx, 0, j, q] * tiles[j][q] + weights[wx, 1, j, q] * source[x - 1, j, q])
                + (weights[wx, 2, j, q] * source[x + 1, j, q] + weights[wx, 3, j, q] * behind_y)
                + (weights[wx, 4, j, q] * ahead_y + weights[wx, 5, j, q] * behind_z)
                + weights[wx, 6, j, q] * ahead_z
            )


def round_kernel(width, final, *refs):
    state, left, right, own, *refs = refs
    parts = [(LAYERS, 2 * LAYERS, own)]
    if width > 1:
        near_left, near_right, *refs = refs
        parts += [(LAYERS - 1, LAYERS, near_left), (2 * LAYERS, 2 * LAYERS + 1, near_right)]
    if width > 2:
        far_left, far_right, *refs = refs
        parts += [(1, LAYERS - 1, far_left), (2 * LAYERS + 1, 3 * LAYERS - 1, far_right)]
    if final:
        later, out, residual, one, two = refs
    else:
        out, one, two = refs
    for x in range(width):
        one[LAYERS - width + x] = left[x]
        one[2 * LAYERS + x] = right[x]
    for x in range(LAYERS):
        one[LAYERS + x] = state[x]
    source, target = one, two
    for step in range(1, width + 1):
        ends = step == width
        goal = out if ends else target
        shift = LAYERS if ends else 0
        low, high = LAYERS - width + step, 2 * LAYERS + width - step
        for begin, end, weights in parts:
            if max(begin, low) < min(end, high):

                def body(x, carry, begin=begin, weights=weights, source=source, goal=goal, shift=shift):
                    fine_layer(source, weights, goal, x, x - begin, x - shift)
                    return carry

                lax.fori_loop(max(begin, low), min(end, high), body, 0)
        source, target = target, source
    if final:
        for h in range(2):
            total = None
            for x in range(LAYERS):
                part = half_sum([[out[x, j, q] for q in range(4)] for j in range(8)], h)
                total = part if total is None else total + part
            total = total * (1.0 / 64) - later[h]
            for copy in range(residual.shape[0]):
                residual[copy, h] = total


def coarse_step(read, weights, write, count):
    first = read(0)
    behind, now = read(count - 1), first
    for x in range(count):
        ahead = read(x + 1) if x + 1 < count else first
        for h in range(2):
            behind_y = now[0] if h else pltpu.roll(now[1], 1, 0)
            ahead_y = pltpu.roll(now[0], 7, 0) if h else now[1]
            behind_z = pltpu.roll(now[h], 1, 1)
            ahead_z = pltpu.roll(now[h], 127, 1)
            write(
                x,
                h,
                (weights[x, 0, h] * now[h] + weights[x, 1, h] * behind[h])
                + (weights[x, 2, h] * ahead[h] + weights[x, 3, h] * behind_y)
                + (weights[x, 4, h] * ahead_y + weights[x, 5, h] * behind_z)
                + weights[x, 6, h] * ahead_z,
            )
        behind, now = now, ahead


def chain_kernel(place, residuals, fields, shares, weights, one, two):
    count = fields.shape[0]
    slices = shares.shape[0]
    slice_index = place[0]
    layer_index = place[1]
    shares[...] = jnp.zeros(shares.shape, F32)

    def prepare(x, carry):
        for h in range(2):
            parts = [fields[x, f, h] for f in range(4)]
            for i, weight in enumerate(weigh(parts[:3], parts[3], STEP * RATIO, 1.0 * RATIO)):
                weights[x, i, h] = weight
            one[x, h] = residuals[x, h]
        return carry

    lax.fori_loop(0, count, prepare, 0)

    def reader(ref):
        return lambda x: [ref[x, h] for h in range(2)]

    def writer(ref):
        def write(x, h, value):
            ref[x, h] = value

        return write

    def link(n, carry):
        for source, target in ((one, two), (two, one)) * 2:
            coarse_step(reader(source), weights, writer(target), count)
        for h in range(2):
            shares[n, h] = one[layer_index, h]
        return carry

    lax.fori_loop(slice_index + 1, slices, link, 0)


def finish_kernel(shares, state, out, buffer):
    change = []
    for h in range(2):
        total = shares[0, h]
        for n in range(1, shares.shape[0]):
            total = total + shares[n, h]
        change.append(total)
    matrix = comb(True)
    for x in range(LAYERS):
        for j in range(8):
            for q in range(4):
                buffer[x, q, pl.ds(j, 8, stride=8), :] = state[x, j, q] + change[j // 4]
        rows = jnp.concatenate([buffer[x, q] for q in range(4)], axis=1)
        out[0, x] = exact_dot(rows, matrix)


def shift(block, axis, distance):
    count = lax.axis_size(axis)
    return lax.ppermute(block, axis, [(i, (i + distance) % count) for i in range(count)])


def shift_fields(block, distance):
    slices, count = lax.axis_size("cuts"), lax.axis_size("space")
    route = []
    for n in range(slices):
        for p in range(count):
            source = (p - distance) % count
            there = n if p // 2 == source // 2 else (n + slices // 2) % slices
            route.append((there * count + source, n * count + p))
    return lax.ppermute(block, ("cuts", "space"), route)


def shards(starts, velocity, diffusivity):
    count = lax.axis_size("space")
    slices = lax.axis_size("cuts")
    block = (LAYERS, *TILE)
    state, first, last, coarse_old = call(
        state_kernel,
        [block, (1, *TILE), (1, *TILE), COARSE],
        [pltpu.VMEM((LAYERS, 4, 64, 128), F32)],
        ins=1,
    )(starts)
    left, right = shift(last, "space", 1), shift(first, "space", -1)
    edges = [(1, 4, *TILE), (REACH - 1, 4, *TILE)]
    own, near_head, far_head, near_tail, far_tail, coarse_fields = call(
        field_kernel,
        [(LAYERS, 4, *TILE), *edges, *edges, (4, *COARSE)],
        [pltpu.VMEM((4, 4, 64, 128), F32)],
        ins=2,
        after=1,
    )(velocity, diffusivity, coarse_old)
    near = [shift_fields(near_tail, 1), shift_fields(near_head, -1)]
    far = [shift_fields(far_tail, 1), shift_fields(far_head, -1)]
    all_fields = lax.all_gather(coarse_fields, "space")
    coarse_later = shift(coarse_old, "cuts", -1)

    def weights_of(fields):
        layers = fields.shape[0]
        return call(functools.partial(weight_kernel, layers), [(layers, 7, *TILE)], ins=1)(fields)[0]

    own_weights = weights_of(own)
    near = [weights_of(fields) for fields in near]
    far = [weights_of(fields) for fields in far]
    for index, width in enumerate(ROUNDS):
        final = index == len(ROUNDS) - 1
        if index > 0:
            left = shift(state[LAYERS - width :], "space", 1)
            right = shift(state[:width], "space", -1)
        operands = [state, left, right, own_weights]
        if width > 1:
            operands += near
        if width > 2:
            operands += far
        if final:
            operands.append(coarse_later)
        outs = call(
            functools.partial(round_kernel, width, final),
            [block, (count, *COARSE)] if final else [block],
            [pltpu.VMEM((3 * LAYERS, *TILE), F32)] * 2,
            ins=len(operands),
        )(*operands)
        state = outs[0]
    residuals = lax.all_to_all(outs[1], "space", 0, 0)
    place = jnp.stack([lax.axis_index("cuts"), lax.axis_index("space")]).astype(jnp.int32)
    shares = call(
        chain_kernel,
        [(slices, *COARSE)],
        [
            pltpu.VMEM((count, 7, *COARSE), F32),
            pltpu.VMEM((count, *COARSE), F32),
            pltpu.VMEM((count, *COARSE), F32),
        ],
        smem=1,
        ins=2,
    )(place, residuals, all_fields)[0]
    shares = lax.all_to_all(shares, "cuts", 0, 0)
    return call(
        finish_kernel,
        [(1, LAYERS, 64, 512)],
        [pltpu.VMEM((LAYERS, 4, 64, 128), F32)],
        ins=2,
    )(shares, state)[0]


def solution(mesh):
    placed = (P("cuts", "space", None, None), P(None, "space", None, None), P("space", None, None))
    return jax.shard_map(
        shards,
        mesh=mesh,
        in_specs=placed,
        out_specs=P("cuts", "space", None, None),
        check_vma=False,
    )
```

```python
import functools

import jax
import jax.numpy as jnp
from jax import lax
from jax.experimental import pallas as pl
from jax.experimental.pallas import tpu as pltpu
from jax.sharding import PartitionSpec as P

RATIO = 4
LAYERS = 4
REACH = 2
TILE = (8, 4, 8, 128)
COARSE = (2, 8, 128)
ROUNDS = (1, 3, 3, 3, 3, 3)
STEP = 0.2
VMEM = pl.BlockSpec(memory_space=pltpu.VMEM)
SMEM = pl.BlockSpec(memory_space=pltpu.SMEM)
ANY = pl.BlockSpec(memory_space=pl.ANY)
F32 = jnp.float32
MIB = 1024 * 1024


def call(body, outs, ins, scratch=(), limit=32):
    return pl.pallas_call(
        body,
        out_shape=[jax.ShapeDtypeStruct(s, F32) for s in outs],
        in_specs=ins,
        out_specs=[VMEM] * len(outs),
        scratch_shapes=list(scratch),
        compiler_params=pltpu.CompilerParams(vmem_limit_bytes=limit * MIB),
    )


def comb(transposed):
    a = lax.broadcasted_iota(jnp.int32, (512, 512), 0)
    b = lax.broadcasted_iota(jnp.int32, (512, 512), 1)
    natural, apart = (b, a) if transposed else (a, b)
    hit = natural == 4 * (apart & 127) + (apart >> 7)
    return jnp.where(hit, 1.0, 0.0).astype(jnp.bfloat16)


def exact_dot(rows, matrix):
    count = rows.shape[0]
    high = rows.astype(jnp.bfloat16)
    rest = rows - high.astype(F32)
    middle = rest.astype(jnp.bfloat16)
    low = (rest - middle.astype(F32)).astype(jnp.bfloat16)
    parts = jnp.concatenate([high, middle, low], axis=0)
    moved = jnp.dot(parts, matrix, preferred_element_type=F32)
    return (moved[:count] + moved[count : 2 * count]) + moved[2 * count :]


def split_rows(rows, matrix, buffer):
    apart = exact_dot(rows, matrix)
    for q in range(4):
        buffer[q] = apart[:, q * 128 : (q + 1) * 128]


def split_tile(buffer, block, j, q):
    return buffer[q, pl.ds(64 * block + j, 8, stride=8), :]


def half_sum(tiles, h):
    total = None
    for j in range(4 * h, 4 * h + 4):
        for q in range(4):
            total = tiles[j][q] if total is None else total + tiles[j][q]
    return total


def copy_edges(state, outer, inner, core, width):
    spare = LAYERS - width
    for x in range(width):
        outer[x] = state[core * spare + x]
        inner[x] = state[(1 - core) * spare + x]


def state_kernel(place, starts, earlier, state, outer, inner, coarse, raw, buffer, ready):
    for x in range(LAYERS):
        pltpu.make_async_copy(starts.at[0, x], raw.at[x], ready.at[x]).start()
    matrix = comb(False)
    for x in range(LAYERS):
        pltpu.make_async_copy(starts.at[0, x], raw.at[x], ready.at[x]).wait()
    split_rows(raw[...].reshape(LAYERS * 64, 512), matrix, buffer)
    sums = [None, None]
    for x in range(LAYERS):
        tiles = [[split_tile(buffer, x, j, q) for q in range(4)] for j in range(8)]
        for j in range(8):
            for q in range(4):
                state[x, j, q] = tiles[j][q]
        for h in range(2):
            part = half_sum(tiles, h)
            sums[h] = part if sums[h] is None else sums[h] + part
    for h in range(2):
        coarse[h] = sums[h] * (1.0 / 64)
    copy_edges(state, outer, inner, place[2], ROUNDS[0])


def weigh(velocity, diffusion, step, spacing):
    spread = diffusion * (step / (spacing * spacing))
    weights = [None]
    for component in velocity:
        moved = component * (step / spacing)
        weights.append(spread + jnp.maximum(moved, 0.0))
        weights.append(spread - jnp.minimum(moved, 0.0))
    total = weights[1]
    for weight in weights[2:]:
        total = total + weight
    weights[0] = 1.0 - total
    return weights


def field_kernel(place, velocity, diffusivity, own, outer, inner, coarse, raw, buffer, ready):
    def copies(x):
        return (
            pltpu.make_async_copy(velocity.at[:, x], raw.at[x, pl.ds(0, 3)], ready.at[x, 0]),
            pltpu.make_async_copy(diffusivity.at[x], raw.at[x, 3], ready.at[x, 1]),
        )

    for x in range(LAYERS):
        for copy in copies(x):
            copy.start()
    matrix = comb(False)
    for f in range(4):
        for h in range(2):
            coarse[f, h] = jnp.zeros((8, 128), F32)

    def layer(x, carry):
        for copy in copies(x):
            copy.wait()
        split_rows(raw[x].reshape(4 * 64, 512), matrix, buffer)
        for f in range(4):
            tiles = [[split_tile(buffer, f, j, q) for q in range(4)] for j in range(8)]
            for h in range(2):
                coarse[f, h] += half_sum(tiles, h) * (1.0 / 64)
            for j in range(8):
                for q in range(4):
                    own[x, f, j, q] = tiles[j][q]
        return carry

    lax.fori_loop(0, LAYERS, layer, 0)
    core = place[2]
    spare = LAYERS - REACH

    def edge(x, carry):
        outer[x] = own[core * spare + x]
        inner[x] = own[(1 - core) * spare + x]
        return carry

    lax.fori_loop(0, REACH, edge, 0)


def weight_kernel(count, fields, weights):
    def layer(x, carry):
        for j in range(8):
            for q in range(4):
                parts = [fields[x, f, j, q] for f in range(4)]
                for i, weight in enumerate(weigh(parts[:3], parts[3], STEP, 1.0)):
                    weights[x, i, j, q] = weight
        return carry

    lax.fori_loop(0, count, layer, 0)


def fine_layer(source, weights, target, x, wx, tx):
    tiles = [[source[x, j, q] for q in range(4)] for j in range(8)]
    for j in range(8):
        for q in range(4):
            behind_y = tiles[j - 1][q] if j > 0 else pltpu.roll(tiles[7][q], 1, 0)
            ahead_y = tiles[j + 1][q] if j < 7 else pltpu.roll(tiles[0][q], 7, 0)
            behind_z = tiles[j][q - 1] if q > 0 else pltpu.roll(tiles[j][3], 1, 1)
            ahead_z = tiles[j][q + 1] if q < 3 else pltpu.roll(tiles[j][0], 127, 1)
            target[tx, j, q] = (
                (weights[wx, 0, j, q] * tiles[j][q] + weights[wx, 1, j, q] * source[x - 1, j, q])
                + (weights[wx, 2, j, q] * source[x + 1, j, q] + weights[wx, 3, j, q] * behind_y)
                + (weights[wx, 4, j, q] * ahead_y + weights[wx, 5, j, q] * behind_z)
                + weights[wx, 6, j, q] * ahead_z
            )


def round_kernel(width, after, final, place, *refs):
    state, outer, inner, own, *refs = refs
    if width > 1:
        own_outer, own_inner, *refs = refs
    if final:
        later, fields, out, residual, one, two = refs
    else:
        refs = refs[len(refs) - 3 - 2 * (after < LAYERS) :]
        out, *edges, one, two = refs
    core = place[2]
    low, high = LAYERS - width, 2 * LAYERS
    outer_begin = low + core * (high - low)
    inner_begin = high - core * (high - low)
    for x in range(width):
        one[outer_begin + x] = outer[x]
        one[inner_begin + x] = inner[x]
    for x in range(LAYERS):
        one[LAYERS + x] = state[x]
    source, target = one, two
    for step in range(1, width + 1):
        ends = step == width
        goal = out if ends else target
        shift = LAYERS if ends else 0
        depth = width - step

        def sweep(begin, count, weights, first, source=source, goal=goal, shift=shift):
            def body(i, carry):
                fine_layer(source, weights, goal, begin + i, first + i, begin + i - shift)
                return carry

            lax.fori_loop(0, count, body, 0)

        sweep(LAYERS, LAYERS, own, 0)
        if depth > 0:
            below, above = LAYERS - depth, 2 * LAYERS
            skip = REACH - depth
            sweep(below + core * (above - below), depth, own_outer, (1 - core) * skip)
            sweep(above - core * (above - below), depth, own_inner, core * skip)
        source, target = target, source
    if final:
        for h in range(2):
            total = None
            for x in range(LAYERS):
                part = half_sum([[out[x, j, q] for q in range(4)] for j in range(8)], h)
                total = part if total is None else total + part
            total = total * (1.0 / 64) - later[h]
            for copy in range(residual.shape[0]):
                residual[copy, h] = total
    elif after < LAYERS:
        copy_edges(out, *edges, core, after)


def coarse_step(read, weights, write, count):
    stride = 4

    def group(g, carry):
        behind, now = carry
        for i in range(stride):
            x = g * stride + i
            ahead = read(x + 1)
            for h in range(2):
                behind_y = now[0] if h else pltpu.roll(now[1], 1, 0)
                ahead_y = pltpu.roll(now[0], 7, 0) if h else now[1]
                behind_z = pltpu.roll(now[h], 1, 1)
                ahead_z = pltpu.roll(now[h], 127, 1)
                write(
                    x,
                    h,
                    (weights[x, 0, h] * now[h] + weights[x, 1, h] * behind[h])
                    + (weights[x, 2, h] * ahead[h] + weights[x, 3, h] * behind_y)
                    + (weights[x, 4, h] * ahead_y + weights[x, 5, h] * behind_z)
                    + weights[x, 6, h] * ahead_z,
                )
            behind, now = now, ahead
        return behind, now

    lax.fori_loop(0, count // stride, group, (read(count - 1), read(0)))


def chain_kernel(place, residuals, fields, shares, weights, one, two):
    count = weights.shape[0]
    slices = shares.shape[0]
    slice_index = place[0]
    layer_index = place[1]
    shares[...] = jnp.zeros(shares.shape, F32)

    def prepare(x, carry):
        for h in range(2):
            parts = [fields[x, f, h] for f in range(4)]
            for i, weight in enumerate(weigh(parts[:3], parts[3], STEP * RATIO, 1.0 * RATIO)):
                weights[x, i, h] = weight
            one[x, h] = residuals[x, h]
        return carry

    lax.fori_loop(0, count, prepare, 0)
    one[count] = one[0]

    def reader(ref):
        return lambda x: [ref[x, h] for h in range(2)]

    def writer(ref):
        def write(x, h, value):
            ref[x, h] = value

        return write

    def link(n, carry):
        for source, target in ((one, two), (two, one)) * 2:
            coarse_step(reader(source), weights, writer(target), count)
            target[count] = target[0]
        for h in range(2):
            shares[n, h] = one[layer_index, h]
        return carry

    lax.fori_loop(slice_index + 1, slices, link, 0)


def finish_kernel(shares, state, out, buffer):
    change = []
    for h in range(2):
        total = shares[0, h]
        for n in range(1, shares.shape[0]):
            total = total + shares[n, h]
        change.append(total)
    matrix = comb(True)
    for x in range(LAYERS):
        for j in range(8):
            for q in range(4):
                buffer[q, pl.ds(64 * x + j, 8, stride=8), :] = state[x, j, q] + change[j // 4]
    rows = jnp.concatenate([buffer[q] for q in range(4)], axis=1)
    out[0] = exact_dot(rows, matrix).reshape(LAYERS, 64, 512)


def swap_inner(block):
    count = lax.axis_size("space")
    return lax.ppermute(block, "space", [(p, p ^ 1) for p in range(count)])


def outer_partner(p, count):
    return (p + 1) % count if p % 2 else (p - 1) % count


def swap_outer(block):
    count = lax.axis_size("space")
    return lax.ppermute(block, "space", [(p, outer_partner(p, count)) for p in range(count)])


def swap_outer_fields(block):
    slices, count = lax.axis_size("cuts"), lax.axis_size("space")
    route = []
    for n in range(slices):
        there = (n + slices // 2) % slices
        route += [(n * count + p, there * count + outer_partner(p, count)) for p in range(count)]
    return lax.ppermute(block, ("cuts", "space"), route)


def shards(starts, velocity, diffusivity):
    count = lax.axis_size("space")
    slices = lax.axis_size("cuts")
    block = (LAYERS, *TILE)
    row = lax.axis_index("space")
    place = jnp.stack([lax.axis_index("cuts"), row, row % 2]).astype(jnp.int32)
    split_scratch = pltpu.VMEM((4, 256, 128), F32)
    own, field_outer, field_inner, coarse_fields = call(
        field_kernel,
        [(LAYERS, 4, *TILE), (REACH, 4, *TILE), (REACH, 4, *TILE), (4, *COARSE)],
        [SMEM, ANY, ANY],
        [pltpu.VMEM((LAYERS, 4, 64, 512), F32), split_scratch, pltpu.SemaphoreType.DMA((LAYERS, 2))],
        limit=60,
    )(place, velocity, diffusivity)
    field_outer = swap_outer_fields(field_outer)
    field_inner = swap_inner(field_inner)
    group = 4
    some_fields = lax.all_gather(
        coarse_fields,
        "space",
        axis_index_groups=[[g * group + i for i in range(group)] for g in range(count // group)],
    )
    all_fields = lax.all_gather(
        some_fields,
        "space",
        axis_index_groups=[[g * group + i for g in range(count // group)] for i in range(group)],
    ).reshape(count, 4, *COARSE)
    edge = (ROUNDS[0], *TILE)
    state, outer, inner, coarse_old = call(
        state_kernel,
        [block, edge, edge, COARSE],
        [SMEM, ANY, ANY],
        [pltpu.VMEM((LAYERS, 64, 512), F32), split_scratch, pltpu.SemaphoreType.DMA((LAYERS,))],
    )(place, starts, coarse_fields)
    coarse_later = lax.ppermute(coarse_old, "cuts", [((n + 1) % slices, n) for n in range(slices)])

    def weights_of(fields):
        layers = fields.shape[0]
        return call(functools.partial(weight_kernel, layers), [(layers, 7, *TILE)], [VMEM])(fields)[0]

    own_weights = weights_of(own)
    sides = [weights_of(field_outer), weights_of(field_inner)]
    for index, width in enumerate(ROUNDS):
        final = index == len(ROUNDS) - 1
        after = LAYERS if final else ROUNDS[index + 1]
        operands = [place, state, swap_outer(outer), swap_inner(inner), own_weights]
        specs = [SMEM] + [VMEM] * 4
        if width > 1:
            operands += sides
            specs += [VMEM] * 2
        outs = [block]
        if final:
            operands += [coarse_later, all_fields]
            specs += [VMEM, ANY]
            outs.append((count, *COARSE))
        elif index == 2:
            operands.append(some_fields)
            specs.append(ANY)
        if after < LAYERS:
            outs += [(after, *TILE)] * 2
        outs = call(
            functools.partial(round_kernel, width, after, final),
            outs,
            specs,
            [pltpu.VMEM((3 * LAYERS, *TILE), F32)] * 2,
        )(*operands)
        state = outs[0]
        outer, inner = outs[1:] if after < LAYERS else (state, state)
    residuals = lax.all_to_all(outs[1], "space", 0, 0)
    shares = call(
        chain_kernel,
        [(slices, *COARSE)],
        [SMEM, VMEM, VMEM],
        [
            pltpu.VMEM((count, 7, *COARSE), F32),
            pltpu.VMEM((count + 1, *COARSE), F32),
            pltpu.VMEM((count + 1, *COARSE), F32),
        ],
    )(place, residuals, all_fields)[0]
    shares = lax.all_to_all(shares, "cuts", 0, 0)
    return call(finish_kernel, [(1, LAYERS, 64, 512)], [VMEM, VMEM], [split_scratch])(shares, state)[0]


def solution(mesh):
    placed = (P("cuts", "space", None, None), P(None, "space", None, None), P("space", None, None))
    return jax.shard_map(
        shards,
        mesh=mesh,
        in_specs=placed,
        out_specs=P("cuts", "space", None, None),
        check_vma=False,
    )
```

```python
import functools

import jax
import jax.numpy as jnp
from jax import lax
from jax.experimental import pallas as pl
from jax.experimental.pallas import tpu as pltpu
from jax.sharding import PartitionSpec as P

RATIO = 4
LAYERS = 4
REACH = 3
ROUNDS = 4
TILE = (8, 8, 512)
COARSE = (2, 8, 128)
STEP = 0.2
VMEM = pl.BlockSpec(memory_space=pltpu.VMEM)
SMEM = pl.BlockSpec(memory_space=pltpu.SMEM)
ANY = pl.BlockSpec(memory_space=pl.ANY)
F32 = jnp.float32
MIB = 1024 * 1024


def call(body, outs, ins, scratch=(), limit=24):
    return pl.pallas_call(
        body,
        out_shape=[jax.ShapeDtypeStruct(s, F32) for s in outs],
        in_specs=ins,
        out_specs=[VMEM] * len(outs),
        scratch_shapes=list(scratch),
        compiler_params=pltpu.CompilerParams(vmem_limit_bytes=limit * MIB),
    )


def fours(shape, fine):
    z = lax.broadcasted_iota(jnp.int32, shape, fine)
    block = lax.broadcasted_iota(jnp.int32, shape, 1 - fine)
    return jnp.where((z >> 2) == block, 1.0, 0.0).astype(jnp.bfloat16)


def exact_dot(rows, matrix):
    count = rows.shape[0]
    high = rows.astype(jnp.bfloat16)
    rest = rows - high.astype(F32)
    middle = rest.astype(jnp.bfloat16)
    low = (rest - middle.astype(F32)).astype(jnp.bfloat16)
    parts = jnp.concatenate([high, middle, low], axis=0)
    moved = jnp.dot(parts, matrix, preferred_element_type=F32)
    return (moved[:count] + moved[count : 2 * count]) + moved[2 * count :]


def spread(rows, buffer):
    for c in range(4):
        buffer[c] = rows[:, 128 * c : 128 * c + 128]


def spread_tile(buffer, j):
    return jnp.concatenate([buffer[c, pl.ds(j, 8, stride=8), :] for c in range(4)], axis=1)


def half_sums(read):
    sums = []
    for h in range(2):
        total = read(4 * h)
        for j in range(4 * h + 1, 4 * h + 4):
            total = total + read(j)
        sums.append(total)
    return sums


def weigh(velocity, diffusion, step, spacing):
    spread = diffusion * (step / (spacing * spacing))
    weights = [None]
    for component in velocity:
        moved = component * (step / spacing)
        weights.append(spread + jnp.maximum(moved, 0.0))
        weights.append(spread - jnp.minimum(moved, 0.0))
    total = weights[1]
    for weight in weights[2:]:
        total = total + weight
    weights[0] = 1.0 - total
    return weights


def own_kernel(velocity, diffusivity, starts, weights, coarse_fields, coarse_old, buffer):
    def layer(x, carry):
        for f in range(3):
            spread(velocity[f, x], buffer.at[f])
        spread(diffusivity[x], buffer.at[3])
        for j in range(8):
            parts = [spread_tile(buffer.at[f], j) for f in range(4)]
            for i, weight in enumerate(weigh(parts[:3], parts[3], STEP, 1.0)):
                weights[x, i, j] = weight
        return carry

    lax.fori_loop(0, LAYERS, layer, 0)
    sums = []
    for f in range(5):
        layers = [velocity[f, x] if f < 3 else (diffusivity[x], starts[x])[f - 3] for x in range(LAYERS)]
        spread((layers[0] + layers[1]) + (layers[2] + layers[3]), buffer.at[f])
        sums += half_sums(lambda j, f=f: spread_tile(buffer.at[f], j))
    means = exact_dot(jnp.concatenate(sums, axis=0), fours((512, 128), 0)) * (1.0 / 64)
    for f in range(5):
        for h in range(2):
            mean = means[16 * f + 8 * h : 16 * f + 8 * h + 8]
            if f < 4:
                coarse_fields[f, h] = mean
            else:
                coarse_old[h] = mean


def side_kernel(velocity, mixed, weights, buffer):
    def layer(x, carry):
        for f in range(3):
            spread(velocity[f, x], buffer.at[f])
        spread(mixed[LAYERS + x], buffer.at[3])
        for j in range(8):
            parts = [spread_tile(buffer.at[f], j) for f in range(4)]
            for i, weight in enumerate(weigh(parts[:3], parts[3], STEP, 1.0)):
                weights[x, i, j] = weight
        return carry

    lax.fori_loop(0, REACH, layer, 0)


def fine_layer(source, weights, target, x, wx, tx):
    tiles = [source[x, j] for j in range(8)]
    for j in range(8):
        behind_y = tiles[j - 1] if j > 0 else pltpu.roll(tiles[7], 1, 0)
        ahead_y = tiles[j + 1] if j < 7 else pltpu.roll(tiles[0], 7, 0)
        behind_z = pltpu.roll(tiles[j], 1, 1)
        ahead_z = pltpu.roll(tiles[j], 511, 1)
        target[tx, j] = (
            (weights[wx, 0, j] * tiles[j] + weights[wx, 1, j] * source[x - 1, j])
            + (weights[wx, 2, j] * source[x + 1, j] + weights[wx, 3, j] * behind_y)
            + (weights[wx, 4, j] * ahead_y + weights[wx, 5, j] * behind_z)
            + weights[wx, 6, j] * ahead_z
        )


def round_kernel(raw, final, place, state, inner, outer, own, own_inner, own_outer, *refs):
    if final:
        later, fields, out, residual, one, two, buffer = refs
    else:
        out, one, two, buffer = refs[-4:]
    core = place[2]

    def enter(x, carry):
        blocks = ((state, LAYERS), (outer, 2 * LAYERS * core), (inner, 2 * LAYERS * (1 - core)))
        for i, (ref, begin) in enumerate(blocks):
            if raw:
                spread(ref[x], buffer.at[i])
            for j in range(8):
                one[begin + x, j] = spread_tile(buffer.at[i], j) if raw else ref[x, j]
        return carry

    lax.fori_loop(0, LAYERS, enter, 0)
    source, target = one, two
    for step in range(1, LAYERS + 1):
        ends = step == LAYERS
        goal = out if ends else target
        shift = LAYERS if ends else 0
        depth = LAYERS - step

        def sweep(begin, count, weights, first, source=source, goal=goal, shift=shift):
            def body(i, carry):
                fine_layer(source, weights, goal, begin + i, first + i, begin + i - shift)
                return carry

            lax.fori_loop(0, count, body, 0)

        sweep(LAYERS, LAYERS, own, 0)
        if depth > 0:
            below, above = LAYERS - depth, 2 * LAYERS
            skip = REACH - depth
            sweep(below + core * (above - below), depth, own_outer, (1 - core) * skip)
            sweep(above - core * (above - below), depth, own_inner, core * skip)
        source, target = target, source
    if final:
        sums = half_sums(lambda j: (out[0, j] + out[1, j]) + (out[2, j] + out[3, j]))
        means = exact_dot(jnp.concatenate(sums, axis=0), fours((512, 128), 0)) * (1.0 / 64)
        for h in range(2):
            left = means[8 * h : 8 * h + 8] - later[h]
            for copy in range(residual.shape[0]):
                residual[copy, h] = left


def coarse_step(read, weights, write, count):
    first = read(0)
    behind, now = read(count - 1), first
    for x in range(count):
        ahead = read(x + 1) if x + 1 < count else first
        for h in range(2):
            behind_y = now[0] if h else pltpu.roll(now[1], 1, 0)
            ahead_y = pltpu.roll(now[0], 7, 0) if h else now[1]
            behind_z = pltpu.roll(now[h], 1, 1)
            ahead_z = pltpu.roll(now[h], 127, 1)
            write(
                x,
                h,
                (weights[x, 0, h] * now[h] + weights[x, 1, h] * behind[h])
                + (weights[x, 2, h] * ahead[h] + weights[x, 3, h] * behind_y)
                + (weights[x, 4, h] * ahead_y + weights[x, 5, h] * behind_z)
                + weights[x, 6, h] * ahead_z,
            )
        behind, now = now, ahead


def chain_kernel(place, residuals, fields, shares, weights, one, two):
    count = weights.shape[0]
    slices = shares.shape[0]
    slice_index = place[0]
    layer_index = place[1]
    shares[...] = jnp.zeros(shares.shape, F32)

    def prepare(x, carry):
        for h in range(2):
            parts = [fields[x, f, h] for f in range(4)]
            for i, weight in enumerate(weigh(parts[:3], parts[3], STEP * RATIO, 1.0 * RATIO)):
                weights[x, i, h] = weight
            one[x, h] = residuals[x, h]
        return carry

    lax.fori_loop(0, count, prepare, 0)

    def reader(ref):
        return lambda x: [ref[x, h] for h in range(2)]

    def writer(ref):
        def write(x, h, value):
            ref[x, h] = value

        return write

    def link(n, carry):
        for source, target in ((one, two), (two, one)) * 2:
            coarse_step(reader(source), weights, writer(target), count)
        for h in range(2):
            shares[n, h] = one[layer_index, h]
        return carry

    lax.fori_loop(slice_index + 1, slices, link, 0)


def finish_kernel(shares, state, out, buffer):
    change = []
    for h in range(2):
        total = shares[0, h]
        for n in range(1, shares.shape[0]):
            total = total + shares[n, h]
        change.append(total)
    wide = exact_dot(jnp.concatenate(change, axis=0), fours((128, 512), 1))
    for x in range(LAYERS):
        for j in range(8):
            h = j // 4
            tile = state[x, j] + wide[8 * h : 8 * h + 8]
            for c in range(4):
                buffer[x, c, pl.ds(j, 8, stride=8), :] = tile[:, 128 * c : 128 * c + 128]
        for c in range(4):
            out[0, x, :, 128 * c : 128 * c + 128] = buffer[x, c]


def swap_inner(block):
    count = lax.axis_size("space")
    return lax.ppermute(block, "space", [(p, p ^ 1) for p in range(count)])


def outer_partner(p, count):
    return (p + 1) % count if p % 2 else (p - 1) % count


def swap_outer(block):
    count = lax.axis_size("space")
    return lax.ppermute(block, "space", [(p, outer_partner(p, count)) for p in range(count)])


def swap_outer_fields(block):
    slices, count = lax.axis_size("cuts"), lax.axis_size("space")
    route = []
    for n in range(slices):
        there = (n + slices // 2) % slices
        route += [(n * count + p, there * count + outer_partner(p, count)) for p in range(count)]
    return lax.ppermute(block, ("cuts", "space"), route)


def shards(starts, velocity, diffusivity):
    count = lax.axis_size("space")
    slices = lax.axis_size("cuts")
    block = (LAYERS, *TILE)
    row = lax.axis_index("space")
    core = row & 1
    columns = pltpu.VMEM((5, 4, 64, 128), F32)
    place = jnp.stack([lax.axis_index("cuts"), row, core]).astype(jnp.int32)

    def halo(begin):
        cut = functools.partial(lax.dynamic_slice_in_dim, start_index=begin, slice_size=REACH)
        mixed = jnp.concatenate([starts[0], cut(diffusivity, axis=0)], axis=0)
        return cut(velocity, axis=1), mixed

    velocity_outer, mixed_outer = halo(core)
    velocity_inner, mixed_inner = halo(1 - core)
    velocity_inner = swap_inner(velocity_inner)
    mixed_inner = swap_inner(mixed_inner)
    velocity_outer = swap_outer_fields(velocity_outer)
    mixed_outer = swap_outer(mixed_outer)
    own_weights, coarse_fields, coarse_old = call(
        own_kernel,
        [(LAYERS, 7, *TILE), (4, *COARSE), COARSE],
        [VMEM] * 3,
        [columns],
    )(velocity, diffusivity, starts[0])
    group = 4
    some_fields = lax.all_gather(
        coarse_fields,
        "space",
        axis_index_groups=[[g * group + i for i in range(group)] for g in range(count // group)],
    )
    all_fields = lax.all_gather(
        some_fields,
        "space",
        axis_index_groups=[[g * group + i for g in range(count // group)] for i in range(group)],
    ).reshape(count, 4, *COARSE)
    coarse_later = lax.ppermute(coarse_old, "cuts", [((n + 1) % slices, n) for n in range(slices)])
    sides = [
        call(side_kernel, [(REACH, 7, *TILE)], [VMEM] * 2, [columns])(*halos)[0]
        for halos in ((velocity_inner, mixed_inner), (velocity_outer, mixed_outer))
    ]
    state, outer, inner = starts[0], mixed_outer, mixed_inner
    for index in range(ROUNDS):
        final = index == ROUNDS - 1
        if index > 0:
            inner, outer = swap_inner(state), swap_outer(state)
        operands = [place, state, inner, outer, own_weights, *sides]
        specs = [SMEM] + [VMEM] * 6
        outs = [block]
        if final:
            operands += [coarse_later, all_fields]
            specs += [VMEM, ANY]
            outs.append((count, *COARSE))
        elif index == 0:
            operands.append(some_fields)
            specs.append(ANY)
        outs = call(
            functools.partial(round_kernel, index == 0, final),
            outs,
            specs,
            [pltpu.VMEM((3 * LAYERS, *TILE), F32)] * 2 + [columns],
        )(*operands)
        state = outs[0]
    residuals = lax.all_to_all(outs[1], "space", 0, 0)
    shares = call(
        chain_kernel,
        [(slices, *COARSE)],
        [SMEM, VMEM, VMEM],
        [
            pltpu.VMEM((count, 7, *COARSE), F32),
            pltpu.VMEM((count, *COARSE), F32),
            pltpu.VMEM((count, *COARSE), F32),
        ],
    )(place, residuals, all_fields)[0]
    shares = lax.all_to_all(shares, "cuts", 0, 0)
    return call(finish_kernel, [(1, LAYERS, 64, 512)], [VMEM, VMEM], [columns])(shares, state)[0]


def solution(mesh):
    placed = (P("cuts", "space", None, None), P(None, "space", None, None), P("space", None, None))
    return jax.shard_map(
        shards,
        mesh=mesh,
        in_specs=placed,
        out_specs=P("cuts", "space", None, None),
        check_vma=False,
    )
```

```python
import functools

import jax
import jax.numpy as jnp
from jax import lax
from jax.experimental import pallas as pl
from jax.experimental.pallas import tpu as pltpu
from jax.sharding import PartitionSpec as P

RATIO = 4
LAYERS = 4
REACH = 3
ROUNDS = 4
TILE = (8, 8, 512)
COARSE = (2, 8, 128)
STEP = 0.2
VMEM = pl.BlockSpec(memory_space=pltpu.VMEM)
SMEM = pl.BlockSpec(memory_space=pltpu.SMEM)
ANY = pl.BlockSpec(memory_space=pl.ANY)
F32 = jnp.float32
MIB = 1024 * 1024


def call(body, outs, ins, scratch=(), limit=24, out=VMEM):
    return pl.pallas_call(
        body,
        out_shape=[jax.ShapeDtypeStruct(s, F32) for s in outs],
        in_specs=ins,
        out_specs=[out] * len(outs),
        scratch_shapes=list(scratch),
        compiler_params=pltpu.CompilerParams(vmem_limit_bytes=limit * MIB),
    )


def fours(shape, fine):
    z = lax.broadcasted_iota(jnp.int32, shape, fine)
    block = lax.broadcasted_iota(jnp.int32, shape, 1 - fine)
    return jnp.where((z >> 2) == block, 1.0, 0.0).astype(jnp.bfloat16)


def exact_dot(rows, matrix):
    count = rows.shape[0]
    high = rows.astype(jnp.bfloat16)
    rest = rows - high.astype(F32)
    middle = rest.astype(jnp.bfloat16)
    low = (rest - middle.astype(F32)).astype(jnp.bfloat16)
    parts = jnp.concatenate([high, middle, low], axis=0)
    moved = jnp.dot(parts, matrix, preferred_element_type=F32)
    return (moved[:count] + moved[count : 2 * count]) + moved[2 * count :]


def spread(rows, buffer):
    for c in range(4):
        buffer[c] = rows[:, 128 * c : 128 * c + 128]


def spread_tile(buffer, j):
    return jnp.concatenate([buffer[c, pl.ds(j, 8, stride=8), :] for c in range(4)], axis=1)


def half_sums(read):
    sums = []
    for h in range(2):
        total = read(4 * h)
        for j in range(4 * h + 1, 4 * h + 4):
            total = total + read(j)
        sums.append(total)
    return sums


def weigh(velocity, diffusion, step, spacing):
    spread = diffusion * (step / (spacing * spacing))
    weights = [None]
    for component in velocity:
        moved = component * (step / spacing)
        weights.append(spread + jnp.maximum(moved, 0.0))
        weights.append(spread - jnp.minimum(moved, 0.0))
    total = weights[1]
    for weight in weights[2:]:
        total = total + weight
    weights[0] = 1.0 - total
    return weights


def cut_kernel(place, velocity, diffusivity, starts, fields, mixed, ready, *, outer):
    begin = place[2] if outer else 1 - place[2]
    copies = [
        pltpu.make_async_copy(velocity.at[:, pl.ds(begin, REACH)], fields, ready.at[0]),
        pltpu.make_async_copy(diffusivity.at[pl.ds(begin, REACH)], mixed.at[pl.ds(LAYERS, REACH)], ready.at[1]),
        pltpu.make_async_copy(starts.at[0], mixed.at[pl.ds(0, LAYERS)], ready.at[2]),
    ]
    for copy in copies:
        copy.start()
    for copy in copies:
        copy.wait()


def own_kernel(velocity, diffusivity, starts, weights, coarse_fields, coarse_old, buffer):
    def layer(x, carry):
        for f in range(3):
            spread(velocity[f, x], buffer.at[f])
        spread(diffusivity[x], buffer.at[3])
        for j in range(8):
            parts = [spread_tile(buffer.at[f], j) for f in range(4)]
            for i, weight in enumerate(weigh(parts[:3], parts[3], STEP, 1.0)):
                weights[x, i, j] = weight
        return carry

    lax.fori_loop(0, LAYERS, layer, 0)
    sums = []
    for f in range(5):
        layers = [velocity[f, x] if f < 3 else (diffusivity[x], starts[x])[f - 3] for x in range(LAYERS)]
        spread((layers[0] + layers[1]) + (layers[2] + layers[3]), buffer.at[f])
        sums += half_sums(lambda j, f=f: spread_tile(buffer.at[f], j))
    means = exact_dot(jnp.concatenate(sums, axis=0), fours((512, 128), 0)) * (1.0 / 64)
    for f in range(5):
        for h in range(2):
            mean = means[16 * f + 8 * h : 16 * f + 8 * h + 8]
            if f < 4:
                coarse_fields[f, h] = mean
            else:
                coarse_old[h] = mean


def side_kernel(velocity, mixed, weights, buffer):
    def layer(x, carry):
        for f in range(3):
            spread(velocity[f, x], buffer.at[f])
        spread(mixed[LAYERS + x], buffer.at[3])
        for j in range(8):
            parts = [spread_tile(buffer.at[f], j) for f in range(4)]
            for i, weight in enumerate(weigh(parts[:3], parts[3], STEP, 1.0)):
                weights[x, i, j] = weight
        return carry

    lax.fori_loop(0, REACH, layer, 0)


def fine_layer(source, weights, target, x, wx, tx):
    first, last = source[x, 0], source[x, 7]
    behind, now = pltpu.roll(last, 1, 0), first
    for j in range(8):
        ahead = pltpu.roll(first, 7, 0) if j == 7 else last if j == 6 else source[x, j + 1]
        target[tx, j] = (
            (weights[wx, 0, j] * now + weights[wx, 1, j] * source[x - 1, j])
            + (weights[wx, 2, j] * source[x + 1, j] + weights[wx, 3, j] * behind)
            + (weights[wx, 4, j] * ahead + weights[wx, 5, j] * pltpu.roll(now, 1, 1))
            + weights[wx, 6, j] * pltpu.roll(now, 511, 1)
        )
        behind, now = now, ahead


def enter(one, blocks, raw, buffer):
    def layer(x, carry):
        for i, (ref, begin) in enumerate(blocks):
            if raw:
                spread(ref[x], buffer.at[i])
            for j in range(8):
                one[begin + x, j] = spread_tile(buffer.at[i], j) if raw else ref[x, j]
        return carry

    lax.fori_loop(0, LAYERS, layer, 0)


def sweep(source, goal, begin, count, weights, first, shift=0):
    def body(i, carry):
        fine_layer(source, weights, goal, begin + i, first + i, begin + i - shift)
        return carry

    lax.fori_loop(0, count, body, 0)


def inner_kernel(raw, place, state, inner, own, own_inner, passed, one, two, buffer):
    core = place[2]
    enter(one, ((state, LAYERS), (inner, 2 * LAYERS * (1 - core))), raw, buffer)
    source, target = one, two
    for step in range(1, LAYERS):
        count = LAYERS - step
        sweep(source, target, LAYERS + (1 - core) * step, count, own, (1 - core) * step)
        above, below = 2 * LAYERS, step
        sweep(source, target, above - core * (above - below), count, own_inner, core * (step - 1))
        for i in range(2):
            on_first, on_second = LAYERS + step + i, 2 * LAYERS - 1 - step - i
            passed[step - 1, i] = target[on_first - core * (on_first - on_second)]
        source, target = target, source


def outer_kernel(raw, final, place, state, outer, own, own_outer, passed, *refs):
    if final:
        later, *refs, out, residual, one, two, buffer = refs
    else:
        out, one, two, buffer = refs[-4:]
    core = place[2]
    enter(one, ((state, LAYERS), (outer, 2 * LAYERS * core)), raw, buffer)
    source, target = one, two
    for step in range(1, LAYERS + 1):
        ends = step == LAYERS
        goal = out if ends else target
        shift = LAYERS if ends else 0
        count = LAYERS - step
        if count:
            below, above = step, 2 * LAYERS
            sweep(source, goal, below + core * (above - below), count, own_outer, (1 - core) * (step - 1))
        sweep(source, goal, LAYERS + core * count, step, own, core * count, shift)
        if not ends:
            for i in range(2):
                on_first, on_second = LAYERS + step + i, 2 * LAYERS - 1 - step - i
                target[on_first - core * (on_first - on_second)] = passed[step - 1, i]
        source, target = target, source
    if final:
        sums = half_sums(lambda j: (out[0, j] + out[1, j]) + (out[2, j] + out[3, j]))
        means = exact_dot(jnp.concatenate(sums, axis=0), fours((512, 128), 0)) * (1.0 / 64)
        for h in range(2):
            left = means[8 * h : 8 * h + 8] - later[h]
            for copy in range(residual.shape[0]):
                residual[copy, h] = left


def coarse_step(read, weights, write, count):
    first = read(0)
    behind, now = read(count - 1), first
    for x in range(count):
        ahead = read(x + 1) if x + 1 < count else first
        for h in range(2):
            behind_y = now[0] if h else pltpu.roll(now[1], 1, 0)
            ahead_y = pltpu.roll(now[0], 7, 0) if h else now[1]
            behind_z = pltpu.roll(now[h], 1, 1)
            ahead_z = pltpu.roll(now[h], 127, 1)
            write(
                x,
                h,
                (weights[x, 0, h] * now[h] + weights[x, 1, h] * behind[h])
                + (weights[x, 2, h] * ahead[h] + weights[x, 3, h] * behind_y)
                + (weights[x, 4, h] * ahead_y + weights[x, 5, h] * behind_z)
                + weights[x, 6, h] * ahead_z,
            )
        behind, now = now, ahead


def chain_kernel(place, residuals, fields, shares, weights, one, two):
    count = weights.shape[0]
    slices = shares.shape[0]
    slice_index = place[0]
    layer_index = place[1]
    shares[...] = jnp.zeros(shares.shape, F32)

    bits = count.bit_length() - 1
    for i in range(count):
        x = layer_index ^ sum(((i >> b) & 1) << (bits - 1 - b) for b in range(bits))
        for h in range(2):
            parts = [fields[i, f, h] for f in range(4)]
            for k, weight in enumerate(weigh(parts[:3], parts[3], STEP * RATIO, 1.0 * RATIO)):
                weights[x, k, h] = weight
            one[i, h] = residuals[i, h]

    def reader(ref):
        return lambda x: [ref[x, h] for h in range(2)]

    def writer(ref):
        def write(x, h, value):
            ref[x, h] = value

        return write

    def link(n, carry):
        for source, target in ((one, two), (two, one)) * 2:
            coarse_step(reader(source), weights, writer(target), count)
        for h in range(2):
            shares[n, h] = one[layer_index, h]
        return carry

    lax.fori_loop(slice_index + 1, slices, link, 0)


def finish_kernel(shares, state, out, buffer):
    change = []
    for h in range(2):
        total = shares[0, h]
        for n in range(1, shares.shape[0]):
            total = total + shares[n, h]
        change.append(total)
    wide = exact_dot(jnp.concatenate(change, axis=0), fours((128, 512), 1))
    for x in range(LAYERS):
        for j in range(8):
            h = j // 4
            tile = state[x, j] + wide[8 * h : 8 * h + 8]
            for c in range(4):
                buffer[x, c, pl.ds(j, 8, stride=8), :] = tile[:, 128 * c : 128 * c + 128]
        for c in range(4):
            out[0, x, :, 128 * c : 128 * c + 128] = buffer[x, c]


def swap_inner(block):
    count = lax.axis_size("space")
    return lax.ppermute(block, "space", [(p, p ^ 1) for p in range(count)])


def outer_partner(p, count):
    return (p + 1) % count if p % 2 else (p - 1) % count


def swap_outer(block):
    count = lax.axis_size("space")
    return lax.ppermute(block, "space", [(p, outer_partner(p, count)) for p in range(count)])


def swap_outer_fields(block):
    slices, count = lax.axis_size("cuts"), lax.axis_size("space")
    route = []
    for n in range(slices):
        there = (n + slices // 2) % slices
        route += [(n * count + p, there * count + outer_partner(p, count)) for p in range(count)]
    return lax.ppermute(block, ("cuts", "space"), route)


def double(block, bit):
    slices, count = lax.axis_size("cuts"), lax.axis_size("space")
    if bit == 2:
        axes = ("cuts", "space")
        route = [
            (n * count + p, (n + slices // 2) % slices * count + (p ^ bit)) for n in range(slices) for p in range(count)
        ]
    else:
        axes = "space"
        route = [(p, p ^ bit) for p in range(count)]
    return jnp.concatenate([block, lax.ppermute(block, axes, route)], axis=0)


def shards(starts, velocity, diffusivity):
    count = lax.axis_size("space")
    slices = lax.axis_size("cuts")
    block = (LAYERS, *TILE)
    row = lax.axis_index("space")
    place = jnp.stack([lax.axis_index("cuts"), row, row & 1]).astype(jnp.int32)
    columns = pltpu.VMEM((5, 4, 64, 128), F32)

    def cut(outer):
        return call(
            functools.partial(cut_kernel, outer=outer),
            [(3, REACH, 64, 512), (LAYERS + REACH, 64, 512)],
            [SMEM, ANY, ANY, ANY],
            [pltpu.SemaphoreType.DMA((3,))],
            limit=60,
            out=ANY,
        )(place, velocity, diffusivity, starts)

    fields_outer, mixed_outer = cut(True)
    fields_inner, mixed_inner = cut(False)
    mixed_inner = swap_inner(mixed_inner)
    mixed_outer = swap_outer(mixed_outer)
    fields_inner = swap_inner(fields_inner)
    fields_outer = swap_outer_fields(fields_outer)
    own_weights, coarse_fields, coarse_old = call(
        own_kernel,
        [(LAYERS, 7, *TILE), (4, *COARSE), COARSE],
        [VMEM] * 3,
        [columns],
    )(velocity, diffusivity, starts[0])
    coarse_later = lax.ppermute(coarse_old, "cuts", [((n + 1) % slices, n) for n in range(slices)])
    gathered = [coarse_fields[None]]
    for bit in (16, 8, 4, 2, 1):
        gathered.append(double(gathered[-1], bit))
    inner_weights, outer_weights = [
        call(side_kernel, [(REACH, 7, *TILE)], [VMEM] * 2, [columns])(*halos)[0]
        for halos in ((fields_inner, mixed_inner), (fields_outer, mixed_outer))
    ]
    state, inner, outer = starts[0], mixed_inner, mixed_outer
    scratch = [pltpu.VMEM((3 * LAYERS, *TILE), F32)] * 2 + [columns]
    for index in range(ROUNDS):
        raw, final = index == 0, index == ROUNDS - 1
        if index > 0:
            inner, outer = swap_inner(state), swap_outer(state)
        passed = call(
            functools.partial(inner_kernel, raw),
            [(LAYERS - 1, 2, *TILE)],
            [SMEM] + [VMEM] * 4,
            scratch,
        )(place, state, inner, own_weights, inner_weights)[0]
        operands = [place, state, outer, own_weights, outer_weights, passed]
        specs = [SMEM] + [VMEM] * 5
        outs = [block]
        if final:
            operands.append(coarse_later)
            specs.append(VMEM)
            outs.append((count, *COARSE))
        operands.append(gathered[index + 2])
        specs.append(ANY)
        outs = call(functools.partial(outer_kernel, raw, final), outs, specs, scratch)(*operands)
        state = outs[0]
    residuals = lax.all_to_all(outs[1], "space", 0, 0)
    shares = call(
        chain_kernel,
        [(slices, *COARSE)],
        [SMEM, VMEM, VMEM],
        [
            pltpu.VMEM((count, 7, *COARSE), F32),
            pltpu.VMEM((count, *COARSE), F32),
            pltpu.VMEM((count, *COARSE), F32),
        ],
    )(place, residuals, gathered[-1])[0]
    shares = lax.all_to_all(shares, "cuts", 0, 0)
    return call(finish_kernel, [(1, LAYERS, 64, 512)], [VMEM, VMEM], [columns])(shares, state)[0]


def solution(mesh):
    placed = (P("cuts", "space", None, None), P(None, "space", None, None), P("space", None, None))
    return jax.shard_map(
        shards,
        mesh=mesh,
        in_specs=placed,
        out_specs=P("cuts", "space", None, None),
        check_vma=False,
    )
```

```python
import functools

import jax
import jax.numpy as jnp
from jax import lax
from jax.experimental import pallas as pl
from jax.experimental.pallas import tpu as pltpu
from jax.sharding import PartitionSpec as P

RATIO = 4
LAYERS = 4
REACH = 3
ROUNDS = 4
TILE = (8, 8, 512)
COARSE = (2, 8, 128)
STEP = 0.2
VMEM = pl.BlockSpec(memory_space=pltpu.VMEM)
SMEM = pl.BlockSpec(memory_space=pltpu.SMEM)
ANY = pl.BlockSpec(memory_space=pl.ANY)
F32 = jnp.float32
MIB = 1024 * 1024


def call(body, outs, ins, scratch=(), limit=24, out=VMEM):
    return pl.pallas_call(
        body,
        out_shape=[jax.ShapeDtypeStruct(s, F32) for s in outs],
        in_specs=ins,
        out_specs=[out] * len(outs),
        scratch_shapes=list(scratch),
        compiler_params=pltpu.CompilerParams(vmem_limit_bytes=limit * MIB),
    )


def fours(shape, fine):
    z = lax.broadcasted_iota(jnp.int32, shape, fine)
    block = lax.broadcasted_iota(jnp.int32, shape, 1 - fine)
    return jnp.where((z >> 2) == block, 1.0, 0.0).astype(jnp.bfloat16)


def exact_dot(rows, matrix):
    count = rows.shape[0]
    high = rows.astype(jnp.bfloat16)
    rest = rows - high.astype(F32)
    middle = rest.astype(jnp.bfloat16)
    low = (rest - middle.astype(F32)).astype(jnp.bfloat16)
    parts = jnp.concatenate([high, middle, low], axis=0)
    moved = jnp.dot(parts, matrix, preferred_element_type=F32)
    return (moved[:count] + moved[count : 2 * count]) + moved[2 * count :]


def spread(rows, buffer):
    for c in range(4):
        buffer[c] = rows[:, 128 * c : 128 * c + 128]


def spread_tile(buffer, j):
    return jnp.concatenate([buffer[c, pl.ds(j, 8, stride=8), :] for c in range(4)], axis=1)


def half_sums(read):
    sums = []
    for h in range(2):
        total = read(4 * h)
        for j in range(4 * h + 1, 4 * h + 4):
            total = total + read(j)
        sums.append(total)
    return sums


def weigh(velocity, diffusion, step, spacing):
    spread = diffusion * (step / (spacing * spacing))
    weights = [None]
    for component in velocity:
        moved = component * (step / spacing)
        weights.append(spread + jnp.maximum(moved, 0.0))
        weights.append(spread - jnp.minimum(moved, 0.0))
    total = weights[1]
    for weight in weights[2:]:
        total = total + weight
    weights[0] = 1.0 - total
    return weights


def cut_kernel(place, velocity, diffusivity, starts, fields, mixed, ready, *, outer):
    begin = place[2] if outer else 1 - place[2]
    copies = [
        pltpu.make_async_copy(velocity.at[:, pl.ds(begin, REACH)], fields, ready.at[0]),
        pltpu.make_async_copy(diffusivity.at[pl.ds(begin, REACH)], mixed.at[pl.ds(LAYERS, REACH)], ready.at[1]),
        pltpu.make_async_copy(starts.at[0], mixed.at[pl.ds(0, LAYERS)], ready.at[2]),
    ]
    for copy in copies:
        copy.start()
    for copy in copies:
        copy.wait()


def own_kernel(velocity, diffusivity, starts, weights, coarse_fields, coarse_old, buffer):
    def layer(x, carry):
        for f in range(3):
            spread(velocity[f, x], buffer.at[f])
        spread(diffusivity[x], buffer.at[3])
        for j in range(8):
            parts = [spread_tile(buffer.at[f], j) for f in range(4)]
            for i, weight in enumerate(weigh(parts[:3], parts[3], STEP, 1.0)):
                weights[x, i, j] = weight
        return carry

    lax.fori_loop(0, LAYERS, layer, 0)
    sums = []
    for f in range(5):
        layers = [velocity[f, x] if f < 3 else (diffusivity[x], starts[x])[f - 3] for x in range(LAYERS)]
        spread((layers[0] + layers[1]) + (layers[2] + layers[3]), buffer.at[f])
        sums += half_sums(lambda j, f=f: spread_tile(buffer.at[f], j))
    means = exact_dot(jnp.concatenate(sums, axis=0), fours((512, 128), 0)) * (1.0 / 64)
    for f in range(5):
        for h in range(2):
            mean = means[16 * f + 8 * h : 16 * f + 8 * h + 8]
            if f < 4:
                coarse_fields[f, h] = mean
            else:
                coarse_old[h] = mean


def side_kernel(velocity, mixed, earlier, weights, buffer):
    def layer(x, carry):
        for f in range(3):
            spread(velocity[f, x], buffer.at[f])
        spread(mixed[LAYERS + x], buffer.at[3])
        for j in range(8):
            parts = [spread_tile(buffer.at[f], j) for f in range(4)]
            for i, weight in enumerate(weigh(parts[:3], parts[3], STEP, 1.0)):
                weights[x, i, j] = weight
        return carry

    lax.fori_loop(0, REACH, layer, 0)


def fine_layer(source, weights, target, x, wx, tx):
    first, last = source[x, 0], source[x, 7]
    behind, now = pltpu.roll(last, 1, 0), first
    for j in range(8):
        ahead = pltpu.roll(first, 7, 0) if j == 7 else last if j == 6 else source[x, j + 1]
        target[tx, j] = (
            (weights[wx, 0, j] * now + weights[wx, 1, j] * source[x - 1, j])
            + (weights[wx, 2, j] * source[x + 1, j] + weights[wx, 3, j] * behind)
            + (weights[wx, 4, j] * ahead + weights[wx, 5, j] * pltpu.roll(now, 1, 1))
            + weights[wx, 6, j] * pltpu.roll(now, 511, 1)
        )
        behind, now = now, ahead


def enter(one, blocks, raw, buffer):
    def layer(x, carry):
        for i, (ref, begin) in enumerate(blocks):
            if raw:
                spread(ref[x], buffer.at[i])
            for j in range(8):
                one[begin + x, j] = spread_tile(buffer.at[i], j) if raw else ref[x, j]
        return carry

    lax.fori_loop(0, LAYERS, layer, 0)


def sweep(source, goal, begin, count, weights, first, shift=0):
    def body(i, carry):
        fine_layer(source, weights, goal, begin + i, first + i, begin + i - shift)
        return carry

    lax.fori_loop(0, count, body, 0)


def inner_kernel(raw, place, state, inner, own, own_inner, passed, one, two, buffer):
    core = place[2]
    enter(one, ((state, LAYERS), (inner, 2 * LAYERS * (1 - core))), raw, buffer)
    source, target = one, two
    for step in range(1, LAYERS):
        count = LAYERS - step
        sweep(source, target, LAYERS + (1 - core) * step, count, own, (1 - core) * step)
        above, below = 2 * LAYERS, step
        sweep(source, target, above - core * (above - below), count, own_inner, core * (step - 1))
        for i in range(2):
            on_first, on_second = LAYERS + step + i, 2 * LAYERS - 1 - step - i
            passed[step - 1, i] = target[on_first - core * (on_first - on_second)]
        source, target = target, source


def outer_kernel(raw, final, place, state, passed, outer, own, own_outer, *refs):
    if final:
        later, after, out, residual, one, two, buffer = refs
    else:
        *parts, early, out, joined, one, two, buffer = refs
        begin = 0
        for part in parts:
            joined[begin : begin + part.shape[0]] = part[...]
            begin += part.shape[0]
    core = place[2]
    enter(one, ((state, LAYERS), (outer, 2 * LAYERS * core)), raw, buffer)
    source, target = one, two
    for step in range(1, LAYERS + 1):
        ends = step == LAYERS
        goal = out if ends else target
        shift = LAYERS if ends else 0
        count = LAYERS - step
        if count:
            below, above = step, 2 * LAYERS
            sweep(source, goal, below + core * (above - below), count, own_outer, (1 - core) * (step - 1))
        sweep(source, goal, LAYERS + core * count, step, own, core * count, shift)
        if not ends:
            for i in range(2):
                on_first, on_second = LAYERS + step + i, 2 * LAYERS - 1 - step - i
                target[on_first - core * (on_first - on_second)] = passed[step - 1, i]
        source, target = target, source
    if final:
        sums = half_sums(lambda j: (out[0, j] + out[1, j]) + (out[2, j] + out[3, j]))
        means = exact_dot(jnp.concatenate(sums, axis=0), fours((512, 128), 0)) * (1.0 / 64)
        for h in range(2):
            left = means[8 * h : 8 * h + 8] - later[h]
            for copy in range(residual.shape[0]):
                residual[copy, h] = left


def coarse_step(read, weights, write, count):
    first = read(0)
    behind, now = read(count - 1), first
    for x in range(count):
        ahead = read(x + 1) if x + 1 < count else first
        for h in range(2):
            behind_y = now[0] if h else pltpu.roll(now[1], 1, 0)
            ahead_y = pltpu.roll(now[0], 7, 0) if h else now[1]
            behind_z = pltpu.roll(now[h], 1, 1)
            ahead_z = pltpu.roll(now[h], 127, 1)
            write(
                x,
                h,
                (weights[x, 0, h] * now[h] + weights[x, 1, h] * behind[h])
                + (weights[x, 2, h] * ahead[h] + weights[x, 3, h] * behind_y)
                + (weights[x, 4, h] * ahead_y + weights[x, 5, h] * behind_z)
                + weights[x, 6, h] * ahead_z,
            )
        behind, now = now, ahead


def mask_of(i):
    return 8 * (i & 3) | (i & 4) | ((i >> 2) & 2) | (i >> 4)


def coarse_weight_kernel(place, some, others, weights):
    row = place[1]
    half = some.shape[0]
    for i in range(2 * half):
        x = row ^ mask_of(i)
        for h in range(2):
            parts = [(some if i < half else others)[i % half, f, h] for f in range(4)]
            for k, weight in enumerate(weigh(parts[:3], parts[3], STEP * RATIO, 1.0 * RATIO)):
                weights[x, k, h] = weight


def chain_kernel(place, residuals, weights, shares, one, two):
    count = weights.shape[0]
    slices = shares.shape[0]
    slice_index = place[0]
    layer_index = place[1]
    shares[...] = jnp.zeros(shares.shape, F32)
    one[...] = residuals[...]

    def reader(ref):
        return lambda x: [ref[x, h] for h in range(2)]

    def writer(ref):
        def write(x, h, value):
            ref[x, h] = value

        return write

    def link(n, carry):
        for source, target in ((one, two), (two, one)) * 2:
            coarse_step(reader(source), weights, writer(target), count)
        for h in range(2):
            shares[n, h] = one[layer_index, h]
        return carry

    lax.fori_loop(slice_index + 1, slices, link, 0)


def finish_kernel(shares, state, out, buffer):
    change = []
    for h in range(2):
        total = shares[0, h]
        for n in range(1, shares.shape[0]):
            total = total + shares[n, h]
        change.append(total)
    wide = exact_dot(jnp.concatenate(change, axis=0), fours((128, 512), 1))
    for x in range(LAYERS):
        for j in range(8):
            h = j // 4
            tile = state[x, j] + wide[8 * h : 8 * h + 8]
            for c in range(4):
                buffer[x, c, pl.ds(j, 8, stride=8), :] = tile[:, 128 * c : 128 * c + 128]
        for c in range(4):
            out[0, x, :, 128 * c : 128 * c + 128] = buffer[x, c]


def swap_inner(block):
    count = lax.axis_size("space")
    return lax.ppermute(block, "space", [(p, p ^ 1) for p in range(count)])


def outer_partner(p, count):
    return (p + 1) % count if p % 2 else (p - 1) % count


def swap_outer(block):
    count = lax.axis_size("space")
    return lax.ppermute(block, "space", [(p, outer_partner(p, count)) for p in range(count)])


def swap_outer_fields(block):
    slices, count = lax.axis_size("cuts"), lax.axis_size("space")
    route = []
    for n in range(slices):
        there = (n + slices // 2) % slices
        route += [(n * count + p, there * count + outer_partner(p, count)) for p in range(count)]
    return lax.ppermute(block, ("cuts", "space"), route)


def across(block, bits):
    slices, count = lax.axis_size("cuts"), lax.axis_size("space")
    if bits == 2:
        route = [
            (n * count + p, (n + slices // 2) % slices * count + (p ^ bits)) for n in range(slices) for p in range(count)
        ]
        return lax.ppermute(block, ("cuts", "space"), route)
    return lax.ppermute(block, "space", [(p, p ^ bits) for p in range(count)])


def shards(starts, velocity, diffusivity):
    count = lax.axis_size("space")
    slices = lax.axis_size("cuts")
    block = (LAYERS, *TILE)
    row = lax.axis_index("space")
    place = jnp.stack([lax.axis_index("cuts"), row, row & 1]).astype(jnp.int32)
    columns = pltpu.VMEM((5, 4, 64, 128), F32)

    def cut(outer):
        return call(
            functools.partial(cut_kernel, outer=outer),
            [(3, REACH, 64, 512), (LAYERS + REACH, 64, 512)],
            [SMEM, ANY, ANY, ANY],
            [pltpu.SemaphoreType.DMA((3,))],
            limit=60,
        )(place, velocity, diffusivity, starts)

    fields_outer, mixed_outer = cut(True)
    fields_inner, mixed_inner = cut(False)
    mixed_inner = swap_inner(mixed_inner)
    mixed_outer = swap_outer(mixed_outer)
    fields_inner = swap_inner(fields_inner)
    fields_outer = swap_outer_fields(fields_outer)
    own_weights, coarse_fields, coarse_old = call(
        own_kernel,
        [(LAYERS, 7, *TILE), (4, *COARSE), COARSE],
        [VMEM] * 3,
        [columns],
    )(velocity, diffusivity, starts[0])
    coarse_later = lax.ppermute(coarse_old, "cuts", [((n + 1) % slices, n) for n in range(slices)])
    gathered = coarse_fields[None]
    weigh_side = call(side_kernel, [(REACH, 7, *TILE)], [VMEM, VMEM, ANY], [columns])
    inner_weights = weigh_side(fields_inner, mixed_inner, coarse_old)[0]
    state, inner, outer = starts[0], mixed_inner, mixed_outer
    scratch = [pltpu.VMEM((3 * LAYERS, *TILE), F32)] * 2 + [columns]
    for index in range(ROUNDS):
        raw, final = index == 0, index == ROUNDS - 1
        if index > 0:
            inner, outer = swap_inner(state), swap_outer(state)
        passed = call(
            functools.partial(inner_kernel, raw),
            [(LAYERS - 1, 2, *TILE)],
            [SMEM] + [VMEM] * 4,
            scratch,
        )(place, state, inner, own_weights, inner_weights)[0]
        if raw:
            outer_weights = weigh_side(fields_outer, mixed_outer, passed)[0]
        operands = [place, state, passed, outer, own_weights, outer_weights]
        if final:
            weights = call(
                coarse_weight_kernel,
                [(count, 7, *COARSE)],
                [SMEM, VMEM, VMEM],
            )(place, gathered, across(gathered, 1))[0]
            operands += [coarse_later, weights]
            specs = [SMEM] + [VMEM] * 6 + [ANY]
            outs = [block, (count, *COARSE)]
        else:
            bits = ((8, 16, 24), (4,), (2,))[index]
            parts = [gathered] + [across(gathered, b) for b in bits]
            operands += parts + [coarse_later if index == 1 else coarse_old]
            specs = [SMEM] + [VMEM] * (5 + len(parts)) + [ANY]
            outs = [block, (len(parts) * gathered.shape[0], 4, *COARSE)]
        state, gathered = call(functools.partial(outer_kernel, raw, final), outs, specs, scratch)(*operands)
    residuals = lax.all_to_all(gathered, "space", 0, 0)
    shares = call(
        chain_kernel,
        [(slices, *COARSE)],
        [SMEM, VMEM, VMEM],
        [pltpu.VMEM((count, *COARSE), F32)] * 2,
    )(place, residuals, weights)[0]
    shares = lax.all_to_all(shares, "cuts", 0, 0)
    return call(finish_kernel, [(1, LAYERS, 64, 512)], [VMEM, VMEM], [columns])(shares, state)[0]


def solution(mesh):
    placed = (P("cuts", "space", None, None), P(None, "space", None, None), P("space", None, None))
    return jax.shard_map(
        shards,
        mesh=mesh,
        in_specs=placed,
        out_specs=P("cuts", "space", None, None),
        check_vma=False,
    )
```

```python
import functools

import jax
import jax.numpy as jnp
from jax import lax
from jax.experimental import pallas as pl
from jax.experimental.pallas import tpu as pltpu
from jax.sharding import PartitionSpec as P

RATIO = 4
LAYERS = 4
REACH = 3
ROUNDS = 4
TILE = (8, 8, 512)
COARSE = (2, 8, 128)
STEP = 0.2
VMEM = pl.BlockSpec(memory_space=pltpu.VMEM)
SMEM = pl.BlockSpec(memory_space=pltpu.SMEM)
ANY = pl.BlockSpec(memory_space=pl.ANY)
F32 = jnp.float32
MIB = 1024 * 1024


def call(body, outs, ins, scratch=(), limit=24, out=VMEM):
    return pl.pallas_call(
        body,
        out_shape=[jax.ShapeDtypeStruct(s, F32) for s in outs],
        in_specs=ins,
        out_specs=[out] * len(outs),
        scratch_shapes=list(scratch),
        compiler_params=pltpu.CompilerParams(vmem_limit_bytes=limit * MIB),
    )


def fours(shape, fine):
    z = lax.broadcasted_iota(jnp.int32, shape, fine)
    block = lax.broadcasted_iota(jnp.int32, shape, 1 - fine)
    return jnp.where((z >> 2) == block, 1.0, 0.0).astype(jnp.bfloat16)


def exact_dot(rows, matrix):
    count = rows.shape[0]
    high = rows.astype(jnp.bfloat16)
    rest = rows - high.astype(F32)
    middle = rest.astype(jnp.bfloat16)
    low = (rest - middle.astype(F32)).astype(jnp.bfloat16)
    parts = jnp.concatenate([high, middle, low], axis=0)
    moved = jnp.dot(parts, matrix, preferred_element_type=F32)
    return (moved[:count] + moved[count : 2 * count]) + moved[2 * count :]


def spread(rows, buffer):
    for c in range(4):
        buffer[c] = rows[:, 128 * c : 128 * c + 128]


def spread_tile(buffer, j):
    return jnp.concatenate([buffer[c, pl.ds(j, 8, stride=8), :] for c in range(4)], axis=1)


def half_sums(read):
    sums = []
    for h in range(2):
        total = read(4 * h)
        for j in range(4 * h + 1, 4 * h + 4):
            total = total + read(j)
        sums.append(total)
    return sums


def weigh(velocity, diffusion, step, spacing):
    spread = diffusion * (step / (spacing * spacing))
    weights = [None]
    for component in velocity:
        moved = component * (step / spacing)
        weights.append(spread + jnp.maximum(moved, 0.0))
        weights.append(spread - jnp.minimum(moved, 0.0))
    total = weights[1]
    for weight in weights[2:]:
        total = total + weight
    weights[0] = 1.0 - total
    return weights


def cut_kernel(place, velocity, diffusivity, starts, fields, mixed, ready, *, outer):
    begin = place[2] if outer else 1 - place[2]
    copies = [
        pltpu.make_async_copy(velocity.at[:, pl.ds(begin, REACH)], fields, ready.at[0]),
        pltpu.make_async_copy(diffusivity.at[pl.ds(begin, REACH)], mixed.at[pl.ds(LAYERS, REACH)], ready.at[1]),
        pltpu.make_async_copy(starts.at[0], mixed.at[pl.ds(0, LAYERS)], ready.at[2]),
    ]
    for copy in copies:
        copy.start()
    for copy in copies:
        copy.wait()


def own_kernel(velocity, diffusivity, starts, weights, coarse_fields, coarse_old, buffer):
    def layer(x, carry):
        for f in range(3):
            spread(velocity[f, x], buffer.at[f])
        spread(diffusivity[x], buffer.at[3])
        for j in range(8):
            parts = [spread_tile(buffer.at[f], j) for f in range(4)]
            for i, weight in enumerate(weigh(parts[:3], parts[3], STEP, 1.0)):
                weights[x, i, j] = weight
        return carry

    lax.fori_loop(0, LAYERS, layer, 0)
    sums = []
    for f in range(5):
        layers = [velocity[f, x] if f < 3 else (diffusivity[x], starts[x])[f - 3] for x in range(LAYERS)]
        spread((layers[0] + layers[1]) + (layers[2] + layers[3]), buffer.at[f])
        sums += half_sums(lambda j, f=f: spread_tile(buffer.at[f], j))
    means = exact_dot(jnp.concatenate(sums, axis=0), fours((512, 128), 0)) * (1.0 / 64)
    for f in range(5):
        for h in range(2):
            mean = means[16 * f + 8 * h : 16 * f + 8 * h + 8]
            if f < 4:
                coarse_fields[f, h] = mean
            else:
                coarse_old[h] = mean


def side_kernel(velocity, mixed, weights, buffer):
    def layer(x, carry):
        for f in range(3):
            spread(velocity[f, x], buffer.at[f])
        spread(mixed[LAYERS + x], buffer.at[3])
        for j in range(8):
            parts = [spread_tile(buffer.at[f], j) for f in range(4)]
            for i, weight in enumerate(weigh(parts[:3], parts[3], STEP, 1.0)):
                weights[x, i, j] = weight
        return carry

    lax.fori_loop(0, REACH, layer, 0)


def fine_layers(source, weights, target, x, wx, tx, depth):
    firsts = [source[x + i, 0] for i in range(depth)]
    lasts = [source[x + i, 7] for i in range(depth)]
    behind = [pltpu.roll(last, 1, 0) for last in lasts]
    now = firsts
    for j in range(8):
        below, above = source[x - 1, j], source[x + depth, j]
        column = [below, *now, above]
        ahead = []
        for i in range(depth):
            if j == 7:
                ahead.append(pltpu.roll(firsts[i], 7, 0))
            else:
                ahead.append(lasts[i] if j == 6 else source[x + i, j + 1])
        for i in range(depth):
            target[tx + i, j] = (
                (weights[wx + i, 0, j] * now[i] + weights[wx + i, 1, j] * column[i])
                + (weights[wx + i, 2, j] * column[i + 2] + weights[wx + i, 3, j] * behind[i])
                + (weights[wx + i, 4, j] * ahead[i] + weights[wx + i, 5, j] * pltpu.roll(now[i], 1, 1))
                + weights[wx + i, 6, j] * pltpu.roll(now[i], 511, 1)
            )
        behind, now = now, ahead


def sweep(source, goal, begin, count, weights, first, shift=0):
    def pair(i, carry):
        fine_layers(source, weights, goal, begin + 2 * i, first + 2 * i, begin + 2 * i - shift, 2)
        return carry

    if count > 1:
        lax.fori_loop(0, count // 2, pair, 0)
    if count % 2:
        last = count - 1
        fine_layers(source, weights, goal, begin + last, first + last, begin + last - shift, 1)


def round_kernel(raw, final, place, state, outer, inner, own, own_outer, own_inner, *refs):
    if final:
        later, after, out, residual, one, two, buffer = refs
    else:
        *parts, early, out, joined, one, two, buffer = refs
        begin = 0
        for part in parts:
            joined[begin : begin + part.shape[0]] = part[...]
            begin += part.shape[0]
    core = place[2]

    def enter(x, carry):
        blocks = ((state, LAYERS), (outer, 2 * LAYERS * core), (inner, 2 * LAYERS * (1 - core)))
        for i, (ref, begin) in enumerate(blocks):
            if raw:
                spread(ref[x], buffer.at[i])
            for j in range(8):
                one[begin + x, j] = spread_tile(buffer.at[i], j) if raw else ref[x, j]
        return carry

    lax.fori_loop(0, LAYERS, enter, 0)
    source, target = one, two
    for step in range(1, LAYERS + 1):
        ends = step == LAYERS
        goal = out if ends else target
        depth = LAYERS - step
        sweep(source, goal, LAYERS, LAYERS, own, 0, LAYERS if ends else 0)
        if depth > 0:
            below, above = step, 2 * LAYERS
            sweep(source, goal, below + core * (above - below), depth, own_outer, (1 - core) * (step - 1))
            sweep(source, goal, above - core * (above - below), depth, own_inner, core * (step - 1))
        source, target = target, source
    if final:
        sums = half_sums(lambda j: (out[0, j] + out[1, j]) + (out[2, j] + out[3, j]))
        means = exact_dot(jnp.concatenate(sums, axis=0), fours((512, 128), 0)) * (1.0 / 64)
        for h in range(2):
            left = means[8 * h : 8 * h + 8] - later[h]
            for copy in range(residual.shape[0]):
                residual[copy, h] = left


def coarse_step(read, weights, write, count):
    first = read(0)
    behind, now = read(count - 1), first
    for x in range(count):
        ahead = read(x + 1) if x + 1 < count else first
        for h in range(2):
            behind_y = now[0] if h else pltpu.roll(now[1], 1, 0)
            ahead_y = pltpu.roll(now[0], 7, 0) if h else now[1]
            behind_z = pltpu.roll(now[h], 1, 1)
            ahead_z = pltpu.roll(now[h], 127, 1)
            write(
                x,
                h,
                (weights[x, 0, h] * now[h] + weights[x, 1, h] * behind[h])
                + (weights[x, 2, h] * ahead[h] + weights[x, 3, h] * behind_y)
                + (weights[x, 4, h] * ahead_y + weights[x, 5, h] * behind_z)
                + weights[x, 6, h] * ahead_z,
            )
        behind, now = now, ahead


def mask_of(i):
    return 8 * (i & 3) | (i & 4) | ((i >> 2) & 2) | (i >> 4)


def coarse_weight_kernel(place, some, others, weights):
    row = place[1]
    half = some.shape[0]
    for i in range(2 * half):
        x = row ^ mask_of(i)
        for h in range(2):
            parts = [(some if i < half else others)[i % half, f, h] for f in range(4)]
            for k, weight in enumerate(weigh(parts[:3], parts[3], STEP * RATIO, 1.0 * RATIO)):
                weights[x, k, h] = weight


def chain_kernel(place, residuals, weights, shares, one, two):
    count = weights.shape[0]
    slices = shares.shape[0]
    slice_index = place[0]
    layer_index = place[1]
    shares[...] = jnp.zeros(shares.shape, F32)
    one[...] = residuals[...]

    def reader(ref):
        return lambda x: [ref[x, h] for h in range(2)]

    def writer(ref):
        def write(x, h, value):
            ref[x, h] = value

        return write

    def link(n, carry):
        for source, target in ((one, two), (two, one)) * 2:
            coarse_step(reader(source), weights, writer(target), count)
        for h in range(2):
            shares[n, h] = one[layer_index, h]
        return carry

    lax.fori_loop(slice_index + 1, slices, link, 0)


def finish_kernel(shares, state, out, buffer):
    change = []
    for h in range(2):
        total = shares[0, h]
        for n in range(1, shares.shape[0]):
            total = total + shares[n, h]
        change.append(total)
    wide = exact_dot(jnp.concatenate(change, axis=0), fours((128, 512), 1))
    for x in range(LAYERS):
        for j in range(8):
            h = j // 4
            tile = state[x, j] + wide[8 * h : 8 * h + 8]
            for c in range(4):
                buffer[x, c, pl.ds(j, 8, stride=8), :] = tile[:, 128 * c : 128 * c + 128]
        for c in range(4):
            out[0, x, :, 128 * c : 128 * c + 128] = buffer[x, c]


def swap_inner(block):
    count = lax.axis_size("space")
    return lax.ppermute(block, "space", [(p, p ^ 1) for p in range(count)])


def outer_partner(p, count):
    return (p + 1) % count if p % 2 else (p - 1) % count


def swap_outer(block):
    count = lax.axis_size("space")
    return lax.ppermute(block, "space", [(p, outer_partner(p, count)) for p in range(count)])


def swap_outer_fields(block):
    slices, count = lax.axis_size("cuts"), lax.axis_size("space")
    route = []
    for n in range(slices):
        there = (n + slices // 2) % slices
        route += [(n * count + p, there * count + outer_partner(p, count)) for p in range(count)]
    return lax.ppermute(block, ("cuts", "space"), route)


def across(block, bits):
    slices, count = lax.axis_size("cuts"), lax.axis_size("space")
    if bits == 2:
        route = [
            (n * count + p, (n + slices // 2) % slices * count + (p ^ bits)) for n in range(slices) for p in range(count)
        ]
        return lax.ppermute(block, ("cuts", "space"), route)
    return lax.ppermute(block, "space", [(p, p ^ bits) for p in range(count)])


def shards(starts, velocity, diffusivity):
    count = lax.axis_size("space")
    slices = lax.axis_size("cuts")
    block = (LAYERS, *TILE)
    row = lax.axis_index("space")
    place = jnp.stack([lax.axis_index("cuts"), row, row & 1]).astype(jnp.int32)
    columns = pltpu.VMEM((5, 4, 64, 128), F32)

    def cut(outer):
        return call(
            functools.partial(cut_kernel, outer=outer),
            [(3, REACH, 64, 512), (LAYERS + REACH, 64, 512)],
            [SMEM, ANY, ANY, ANY],
            [pltpu.SemaphoreType.DMA((3,))],
        )(place, velocity, diffusivity, starts)

    fields_outer, mixed_outer = cut(True)
    fields_inner, mixed_inner = cut(False)
    mixed_inner = swap_inner(mixed_inner)
    mixed_outer = swap_outer(mixed_outer)
    fields_inner = swap_inner(fields_inner)
    fields_outer = swap_outer_fields(fields_outer)
    own_weights, coarse_fields, coarse_old = call(
        own_kernel,
        [(LAYERS, 7, *TILE), (4, *COARSE), COARSE],
        [VMEM] * 3,
        [columns],
    )(velocity, diffusivity, starts[0])
    coarse_later = lax.ppermute(coarse_old, "cuts", [((n + 1) % slices, n) for n in range(slices)])
    gathered = coarse_fields[None]
    outer_weights, inner_weights = [
        call(side_kernel, [(REACH, 7, *TILE)], [VMEM, VMEM], [columns])(*halos)[0]
        for halos in ((fields_outer, mixed_outer), (fields_inner, mixed_inner))
    ]
    state, inner, outer = starts[0], mixed_inner, mixed_outer
    scratch = [pltpu.VMEM((3 * LAYERS, *TILE), F32)] * 2 + [columns]
    for index in range(ROUNDS):
        raw, final = index == 0, index == ROUNDS - 1
        if index > 0:
            inner, outer = swap_inner(state), swap_outer(state)
        operands = [place, state, outer, inner, own_weights, outer_weights, inner_weights]
        specs = [SMEM] + [VMEM] * 6
        if final:
            weights = call(
                coarse_weight_kernel,
                [(count, 7, *COARSE)],
                [SMEM, VMEM, VMEM],
            )(place, gathered, across(gathered, 1))[0]
            operands += [coarse_later, weights]
            specs += [VMEM, ANY]
            outs = [block, (count, *COARSE)]
        else:
            bits = ((8, 16, 24), (4,), (2,))[index]
            parts = [gathered] + [across(gathered, b) for b in bits]
            operands += parts + [coarse_later if index == 1 else coarse_old]
            specs += [VMEM] * len(parts) + [ANY]
            outs = [block, (len(parts) * gathered.shape[0], 4, *COARSE)]
        state, gathered = call(functools.partial(round_kernel, raw, final), outs, specs, scratch)(*operands)
    residuals = lax.all_to_all(gathered, "space", 0, 0)
    shares = call(
        chain_kernel,
        [(slices, *COARSE)],
        [SMEM, VMEM, VMEM],
        [pltpu.VMEM((count, *COARSE), F32)] * 2,
    )(place, residuals, weights)[0]
    shares = lax.all_to_all(shares, "cuts", 0, 0)
    return call(finish_kernel, [(1, LAYERS, 64, 512)], [VMEM, VMEM], [columns])(shares, state)[0]


def solution(mesh):
    placed = (P("cuts", "space", None, None), P(None, "space", None, None), P("space", None, None))
    return jax.shard_map(
        shards,
        mesh=mesh,
        in_specs=placed,
        out_specs=P("cuts", "space", None, None),
        check_vma=False,
    )
```

```python
import functools

import jax
import jax.numpy as jnp
from jax import lax
from jax.experimental import pallas as pl
from jax.experimental.pallas import tpu as pltpu
from jax.sharding import PartitionSpec as P

RATIO = 4
LAYERS = 4
REACH = 3
ROUNDS = 4
TILE = (8, 8, 512)
COARSE = (2, 8, 128)
STEP = 0.2
VMEM = pl.BlockSpec(memory_space=pltpu.VMEM)
SMEM = pl.BlockSpec(memory_space=pltpu.SMEM)
ANY = pl.BlockSpec(memory_space=pl.ANY)
F32 = jnp.float32
MIB = 1024 * 1024


def call(body, outs, ins, scratch=(), limit=24, out=VMEM):
    return pl.pallas_call(
        body,
        out_shape=[jax.ShapeDtypeStruct(s, F32) for s in outs],
        in_specs=ins,
        out_specs=[out] * len(outs),
        scratch_shapes=list(scratch),
        compiler_params=pltpu.CompilerParams(vmem_limit_bytes=limit * MIB),
    )


def fours(shape, fine):
    z = lax.broadcasted_iota(jnp.int32, shape, fine)
    block = lax.broadcasted_iota(jnp.int32, shape, 1 - fine)
    return jnp.where((z >> 2) == block, 1.0, 0.0).astype(jnp.bfloat16)


def exact_dot(rows, matrix):
    count = rows.shape[0]
    high = rows.astype(jnp.bfloat16)
    rest = rows - high.astype(F32)
    middle = rest.astype(jnp.bfloat16)
    low = (rest - middle.astype(F32)).astype(jnp.bfloat16)
    parts = jnp.concatenate([high, middle, low], axis=0)
    moved = jnp.dot(parts, matrix, preferred_element_type=F32)
    return (moved[:count] + moved[count : 2 * count]) + moved[2 * count :]


def spread(rows, buffer):
    for c in range(4):
        buffer[c] = rows[:, 128 * c : 128 * c + 128]


def spread_tile(buffer, j):
    return jnp.concatenate([buffer[c, pl.ds(j, 8, stride=8), :] for c in range(4)], axis=1)


def half_sums(read):
    sums = []
    for h in range(2):
        total = read(4 * h)
        for j in range(4 * h + 1, 4 * h + 4):
            total = total + read(j)
        sums.append(total)
    return sums


def weigh(velocity, diffusion, step, spacing):
    spread = diffusion * (step / (spacing * spacing))
    weights = [None]
    for component in velocity:
        moved = component * (step / spacing)
        weights.append(spread + jnp.maximum(moved, 0.0))
        weights.append(spread - jnp.minimum(moved, 0.0))
    total = weights[1]
    for weight in weights[2:]:
        total = total + weight
    weights[0] = 1.0 - total
    return weights


STATE_AT = 3 * REACH
INNER = STATE_AT + LAYERS + REACH


def cut_kernel(place, velocity, diffusivity, starts, fields, mixed, inner, ready):
    core = place[2]
    pairs = [
        (diffusivity.at[pl.ds(core, REACH)], mixed.at[pl.ds(LAYERS, REACH)]),
        (starts.at[0], mixed.at[pl.ds(0, LAYERS)]),
        (diffusivity.at[pl.ds(1 - core, REACH)], inner.at[pl.ds(STATE_AT + LAYERS, REACH)]),
        (starts.at[0], inner.at[pl.ds(STATE_AT, LAYERS)]),
    ]
    for f in range(3):
        pairs.append((velocity.at[f, pl.ds(core, REACH)], fields.at[pl.ds(f * REACH, REACH)]))
        pairs.append((velocity.at[f, pl.ds(1 - core, REACH)], inner.at[pl.ds(f * REACH, REACH)]))
    copies = [pltpu.make_async_copy(*pair, ready.at[i]) for i, pair in enumerate(pairs)]
    for copy in copies:
        copy.start()
    for copy in copies:
        copy.wait()


def own_kernel(velocity, diffusivity, starts, weights, coarse_fields, coarse_old, buffer):
    def layer(x, carry):
        for f in range(3):
            spread(velocity[f, x], buffer.at[f])
        spread(diffusivity[x], buffer.at[3])
        for j in range(8):
            parts = [spread_tile(buffer.at[f], j) for f in range(4)]
            for i, weight in enumerate(weigh(parts[:3], parts[3], STEP, 1.0)):
                weights[x, i, j] = weight
        return carry

    lax.fori_loop(0, LAYERS, layer, 0)
    sums = []
    for f in range(5):
        layers = [velocity[f, x] if f < 3 else (diffusivity[x], starts[x])[f - 3] for x in range(LAYERS)]
        spread((layers[0] + layers[1]) + (layers[2] + layers[3]), buffer.at[f])
        sums += half_sums(lambda j, f=f: spread_tile(buffer.at[f], j))
    means = exact_dot(jnp.concatenate(sums, axis=0), fours((512, 128), 0)) * (1.0 / 64)
    for f in range(5):
        for h in range(2):
            mean = means[16 * f + 8 * h : 16 * f + 8 * h + 8]
            if f < 4:
                coarse_fields[f, h] = mean
            else:
                coarse_old[h] = mean


def side_kernel(at, *refs):
    *fields, earlier, weights, buffer = refs

    def layer(x, carry):
        for f in range(3):
            spread(fields[0][f * REACH + x], buffer.at[f])
        spread(fields[-1][at + x], buffer.at[3])
        for j in range(8):
            parts = [spread_tile(buffer.at[f], j) for f in range(4)]
            for i, weight in enumerate(weigh(parts[:3], parts[3], STEP, 1.0)):
                weights[x, i, j] = weight
        return carry

    lax.fori_loop(0, REACH, layer, 0)


def fine_layers(source, weights, target, x, wx, tx, depth):
    firsts = [source[x + i, 0] for i in range(depth)]
    lasts = [source[x + i, 7] for i in range(depth)]
    behind = [pltpu.roll(last, 1, 0) for last in lasts]
    now = firsts
    done = []
    for j in range(8):
        below, above = source[x - 1, j], source[x + depth, j]
        column = [below, *now, above]
        ahead = []
        for i in range(depth):
            if j == 7:
                ahead.append(pltpu.roll(firsts[i], 7, 0))
            else:
                ahead.append(lasts[i] if j == 6 else source[x + i, j + 1])
        for i in range(depth):
            value = (
                (weights[wx + i, 0, j] * now[i] + weights[wx + i, 1, j] * column[i])
                + (weights[wx + i, 2, j] * column[i + 2] + weights[wx + i, 3, j] * behind[i])
                + (weights[wx + i, 4, j] * ahead[i] + weights[wx + i, 5, j] * pltpu.roll(now[i], 1, 1))
                + weights[wx + i, 6, j] * pltpu.roll(now[i], 511, 1)
            )
            done.append((tx + i, j, value))
        behind, now = now, ahead
        if j % 2:
            for at, tile, value in done:
                target[at, tile] = value
            done = []


def sweep(source, goal, begin, count, weights, first, shift=0):
    def pair(i, carry):
        fine_layers(source, weights, goal, begin + 2 * i, first + 2 * i, begin + 2 * i - shift, 2)
        return carry

    if count > 1:
        lax.fori_loop(0, count // 2, pair, 0)
    if count % 2:
        last = count - 1
        fine_layers(source, weights, goal, begin + last, first + last, begin + last - shift, 1)


def round_kernel(raw, final, place, state, outer, inner, own, own_outer, own_inner, *refs):
    if final:
        later, after, out, residual, one, two, buffer = refs
    else:
        *parts, out, joined, one, two, buffer = refs
        begin = 0
        for part in parts:
            joined[begin : begin + part.shape[0]] = part[...]
            begin += part.shape[0]
    core = place[2]

    def enter(x, carry):
        blocks = ((state, LAYERS), (outer, 2 * LAYERS * core), (inner, 2 * LAYERS * (1 - core)))
        for i, (ref, begin) in enumerate(blocks):
            if raw:
                spread(ref[(STATE_AT if ref is inner else 0) + x], buffer.at[i])
            for j in range(8):
                one[begin + x, j] = spread_tile(buffer.at[i], j) if raw else ref[x, j]
        return carry

    lax.fori_loop(0, LAYERS, enter, 0)
    source, target = one, two
    for step in range(1, LAYERS + 1):
        ends = step == LAYERS
        goal = out if ends else target
        depth = LAYERS - step
        sweep(source, goal, LAYERS, LAYERS, own, 0, LAYERS if ends else 0)
        if depth > 0:
            below, above = step, 2 * LAYERS
            sweep(source, goal, below + core * (above - below), depth, own_outer, (1 - core) * (step - 1))
            sweep(source, goal, above - core * (above - below), depth, own_inner, core * (step - 1))
        source, target = target, source
    if final:
        sums = half_sums(lambda j: (out[0, j] + out[1, j]) + (out[2, j] + out[3, j]))
        means = exact_dot(jnp.concatenate(sums, axis=0), fours((512, 128), 0)) * (1.0 / 64)
        for h in range(2):
            left = means[8 * h : 8 * h + 8] - later[h]
            for copy in range(residual.shape[0]):
                residual[copy, h] = left


def coarse_step(read, weights, write, count):
    first = read(0)
    behind, now = read(count - 1), first
    for x in range(count):
        ahead = read(x + 1) if x + 1 < count else first
        for h in range(2):
            behind_y = now[0] if h else pltpu.roll(now[1], 1, 0)
            ahead_y = pltpu.roll(now[0], 7, 0) if h else now[1]
            behind_z = pltpu.roll(now[h], 1, 1)
            ahead_z = pltpu.roll(now[h], 127, 1)
            write(
                x,
                h,
                (weights[x, 0, h] * now[h] + weights[x, 1, h] * behind[h])
                + (weights[x, 2, h] * ahead[h] + weights[x, 3, h] * behind_y)
                + (weights[x, 4, h] * ahead_y + weights[x, 5, h] * behind_z)
                + weights[x, 6, h] * ahead_z,
            )
        behind, now = now, ahead


def mask_of(i):
    return 8 * (i & 3) | ((i >> 1) & 2) | ((i >> 1) & 4) | (i >> 4)


def coarse_weight_kernel(place, some, others, weights):
    row = place[1]
    half = some.shape[0]
    for i in range(2 * half):
        x = row ^ mask_of(i)
        for h in range(2):
            parts = [(some if i < half else others)[i % half, f, h] for f in range(4)]
            for k, weight in enumerate(weigh(parts[:3], parts[3], STEP * RATIO, 1.0 * RATIO)):
                weights[x, k, h] = weight


def chain_kernel(place, residuals, given, shares, weights, one, two):
    count = weights.shape[0]
    slices = shares.shape[0]
    weights[...] = given[...]
    slice_index = place[0]
    layer_index = place[1]
    shares[...] = jnp.zeros(shares.shape, F32)
    one[...] = residuals[...]

    def reader(ref):
        return lambda x: [ref[x, h] for h in range(2)]

    def writer(ref):
        def write(x, h, value):
            ref[x, h] = value

        return write

    def link(n, carry):
        for source, target in ((one, two), (two, one)) * 2:
            coarse_step(reader(source), weights, writer(target), count)
        for h in range(2):
            shares[n, h] = one[layer_index, h]
        return carry

    lax.fori_loop(slice_index + 1, slices, link, 0)


def finish_kernel(shares, state, out, buffer):
    change = []
    for h in range(2):
        total = shares[0, h]
        for n in range(1, shares.shape[0]):
            total = total + shares[n, h]
        change.append(total)
    wide = exact_dot(jnp.concatenate(change, axis=0), fours((128, 512), 1))
    for x in range(LAYERS):
        for j in range(8):
            h = j // 4
            tile = state[x, j] + wide[8 * h : 8 * h + 8]
            for c in range(4):
                buffer[x, c, pl.ds(j, 8, stride=8), :] = tile[:, 128 * c : 128 * c + 128]
        for c in range(4):
            out[0, x, :, 128 * c : 128 * c + 128] = buffer[x, c]


def swap_inner(block):
    count = lax.axis_size("space")
    return lax.ppermute(block, "space", [(p, p ^ 1) for p in range(count)])


def outer_partner(p, count):
    return (p + 1) % count if p % 2 else (p - 1) % count


def swap_outer(block):
    count = lax.axis_size("space")
    return lax.ppermute(block, "space", [(p, outer_partner(p, count)) for p in range(count)])


def swap_outer_fields(block):
    slices, count = lax.axis_size("cuts"), lax.axis_size("space")
    route = []
    for n in range(slices):
        there = (n + slices // 2) % slices
        route += [(n * count + p, there * count + outer_partner(p, count)) for p in range(count)]
    return lax.ppermute(block, ("cuts", "space"), route)


def across(block, bits):
    slices, count = lax.axis_size("cuts"), lax.axis_size("space")
    if bits == 2:
        route = [
            (n * count + p, (n + slices // 2) % slices * count + (p ^ bits)) for n in range(slices) for p in range(count)
        ]
        return lax.ppermute(block, ("cuts", "space"), route)
    return lax.ppermute(block, "space", [(p, p ^ bits) for p in range(count)])


def shards(starts, velocity, diffusivity):
    count = lax.axis_size("space")
    slices = lax.axis_size("cuts")
    block = (LAYERS, *TILE)
    row = lax.axis_index("space")
    place = jnp.stack([lax.axis_index("cuts"), row, row & 1]).astype(jnp.int32)
    columns = pltpu.VMEM((5, 4, 64, 128), F32)

    fields_outer, mixed_outer, all_inner = call(
        cut_kernel,
        [(3 * REACH, 64, 512), (LAYERS + REACH, 64, 512), (INNER, 64, 512)],
        [SMEM, ANY, ANY, ANY],
        [pltpu.SemaphoreType.DMA((10,))],
    )(place, velocity, diffusivity, starts)
    fields_outer = swap_outer_fields(fields_outer)
    mixed_outer = swap_outer(mixed_outer)
    all_inner = swap_inner(all_inner)
    own_weights, coarse_fields, coarse_old = call(
        own_kernel,
        [(LAYERS, 7, *TILE), (4, *COARSE), COARSE],
        [VMEM] * 3,
        [columns],
    )(velocity, diffusivity, starts[0])
    coarse_later = lax.ppermute(coarse_old, "cuts", [((n + 1) % slices, n) for n in range(slices)])
    gathered = coarse_fields[None]
    side = [(REACH, 7, *TILE)]
    inner_weights = call(functools.partial(side_kernel, STATE_AT + LAYERS), side, [VMEM, ANY], [columns])(
        all_inner, coarse_old
    )[0]
    outer_weights = call(functools.partial(side_kernel, LAYERS), side, [VMEM, VMEM, ANY], [columns])(
        fields_outer, mixed_outer, inner_weights
    )[0]
    state, inner, outer = starts[0], all_inner, mixed_outer
    scratch = [pltpu.VMEM((3 * LAYERS, *TILE), F32)] * 2 + [columns]
    for index in range(ROUNDS):
        raw, final = index == 0, index == ROUNDS - 1
        if index > 0:
            inner, outer = swap_inner(state), swap_outer(state)
        operands = [place, state, outer, inner, own_weights, outer_weights, inner_weights]
        specs = [SMEM] + [VMEM] * 6
        if final:
            weights = call(
                coarse_weight_kernel,
                [(count, 7, *COARSE)],
                [SMEM, VMEM, VMEM],
            )(place, gathered, across(gathered, 1))[0]
            operands += [coarse_later, weights]
            specs += [VMEM, ANY]
            outs = [block, (count, *COARSE)]
        else:
            parts = [gathered] + [across(gathered, b) for b in ((8, 16, 24), (2,), (4,))[index]]
            operands += parts
            specs += [VMEM] * len(parts)
            outs = [block, (len(parts) * gathered.shape[0], 4, *COARSE)]
        state, gathered = call(functools.partial(round_kernel, raw, final), outs, specs, scratch)(*operands)
    residuals = lax.all_to_all(gathered, "space", 0, 0)
    shares = call(
        chain_kernel,
        [(slices, *COARSE)],
        [SMEM, VMEM, VMEM],
        [pltpu.VMEM((count, 7, *COARSE), F32)] + [pltpu.VMEM((count, *COARSE), F32)] * 2,
    )(place, residuals, weights)[0]
    shares = lax.all_to_all(shares, "cuts", 0, 0)
    return call(finish_kernel, [(1, LAYERS, 64, 512)], [VMEM, VMEM], [columns])(shares, state)[0]


def solution(mesh):
    placed = (P("cuts", "space", None, None), P(None, "space", None, None), P("space", None, None))
    return jax.shard_map(
        shards,
        mesh=mesh,
        in_specs=placed,
        out_specs=P("cuts", "space", None, None),
        check_vma=False,
    )
```

```python
import functools

import jax
import jax.numpy as jnp
from jax import lax
from jax.experimental import pallas as pl
from jax.experimental.pallas import tpu as pltpu
from jax.sharding import PartitionSpec as P

RATIO = 4
LAYERS = 4
REACH = 3
ROUNDS = 4
TILE = (8, 8, 512)
COARSE = (2, 8, 128)
STEP = 0.2
VMEM = pl.BlockSpec(memory_space=pltpu.VMEM)
SMEM = pl.BlockSpec(memory_space=pltpu.SMEM)
ANY = pl.BlockSpec(memory_space=pl.ANY)
F32 = jnp.float32
MIB = 1024 * 1024
SMALL = pl.CostEstimate(flops=1, bytes_accessed=1, transcendentals=0)


def call(body, outs, ins, scratch=(), limit=24, cost=None):
    return pl.pallas_call(
        body,
        out_shape=[jax.ShapeDtypeStruct(s, F32) for s in outs],
        in_specs=ins,
        out_specs=[VMEM] * len(outs),
        scratch_shapes=list(scratch),
        cost_estimate=cost,
        compiler_params=pltpu.CompilerParams(vmem_limit_bytes=limit * MIB),
    )


def fours(shape, fine):
    z = lax.broadcasted_iota(jnp.int32, shape, fine)
    block = lax.broadcasted_iota(jnp.int32, shape, 1 - fine)
    return jnp.where((z >> 2) == block, 1.0, 0.0).astype(jnp.bfloat16)


def exact_dot(rows, matrix):
    count = rows.shape[0]
    high = rows.astype(jnp.bfloat16)
    rest = rows - high.astype(F32)
    middle = rest.astype(jnp.bfloat16)
    low = (rest - middle.astype(F32)).astype(jnp.bfloat16)
    parts = jnp.concatenate([high, middle, low], axis=0)
    moved = jnp.dot(parts, matrix, preferred_element_type=F32)
    return (moved[:count] + moved[count : 2 * count]) + moved[2 * count :]


def spread(rows, buffer):
    for c in range(4):
        buffer[c] = rows[:, 128 * c : 128 * c + 128]


def spread_tile(buffer, j):
    return jnp.concatenate([buffer[c, pl.ds(j, 8, stride=8), :] for c in range(4)], axis=1)


def half_sums(read):
    sums = []
    for h in range(2):
        total = read(4 * h)
        for j in range(4 * h + 1, 4 * h + 4):
            total = total + read(j)
        sums.append(total)
    return sums


def weigh(velocity, diffusion, step, spacing):
    spread = diffusion * (step / (spacing * spacing))
    weights = [None]
    for component in velocity:
        moved = component * (step / spacing)
        weights.append(spread + jnp.maximum(moved, 0.0))
        weights.append(spread - jnp.minimum(moved, 0.0))
    total = weights[1]
    for weight in weights[2:]:
        total = total + weight
    weights[0] = 1.0 - total
    return weights


def run(pairs, ready):
    copies = [pltpu.make_async_copy(*pair, ready.at[i]) for i, pair in enumerate(pairs)]
    for copy in copies:
        copy.start()
    for copy in copies:
        copy.wait()


def cut_fields_kernel(place, velocity, fields, ready):
    run([(velocity.at[f, pl.ds(place[2], REACH)], fields.at[pl.ds(f * REACH, REACH)]) for f in range(3)], ready)


STATE_AT = 3 * REACH
INNER = STATE_AT + LAYERS + REACH


def cut_kernel(place, velocity, diffusivity, starts, earlier, mixed, inner, ready):
    core = place[2]
    pairs = [
        (diffusivity.at[pl.ds(core, REACH)], mixed.at[pl.ds(LAYERS, REACH)]),
        (starts.at[0], mixed.at[pl.ds(0, LAYERS)]),
        (diffusivity.at[pl.ds(1 - core, REACH)], inner.at[pl.ds(STATE_AT + LAYERS, REACH)]),
        (starts.at[0], inner.at[pl.ds(STATE_AT, LAYERS)]),
    ]
    for f in range(3):
        pairs.append((velocity.at[f, pl.ds(1 - core, REACH)], inner.at[pl.ds(f * REACH, REACH)]))
    run(pairs, ready)


def own_kernel(velocity, diffusivity, starts, weights, coarse_fields, coarse_old, buffer):
    def layer(x, carry):
        for f in range(3):
            spread(velocity[f, x], buffer.at[f])
        spread(diffusivity[x], buffer.at[3])
        for j in range(8):
            parts = [spread_tile(buffer.at[f], j) for f in range(4)]
            for i, weight in enumerate(weigh(parts[:3], parts[3], STEP, 1.0)):
                weights[x, i, j] = weight
        return carry

    lax.fori_loop(0, LAYERS, layer, 0)
    sums = []
    for f in range(5):
        layers = [velocity[f, x] if f < 3 else (diffusivity[x], starts[x])[f - 3] for x in range(LAYERS)]
        spread((layers[0] + layers[1]) + (layers[2] + layers[3]), buffer.at[f])
        sums += half_sums(lambda j, f=f: spread_tile(buffer.at[f], j))
    means = exact_dot(jnp.concatenate(sums, axis=0), fours((512, 128), 0)) * (1.0 / 64)
    for f in range(5):
        for h in range(2):
            mean = means[16 * f + 8 * h : 16 * f + 8 * h + 8]
            if f < 4:
                coarse_fields[f, h] = mean
            else:
                coarse_old[h] = mean


def side_kernel(at, *refs):
    *fields, earlier, weights, buffer = refs

    def layer(x, carry):
        for f in range(3):
            spread(fields[0][f * REACH + x], buffer.at[f])
        spread(fields[-1][at + x], buffer.at[3])
        for j in range(8):
            parts = [spread_tile(buffer.at[f], j) for f in range(4)]
            for i, weight in enumerate(weigh(parts[:3], parts[3], STEP, 1.0)):
                weights[x, i, j] = weight
        return carry

    lax.fori_loop(0, REACH, layer, 0)


def fine_layers(source, weights, target, x, wx, tx, depth):
    firsts = [source[x + i, 0] for i in range(depth)]
    lasts = [source[x + i, 7] for i in range(depth)]
    behind = [pltpu.roll(last, 1, 0) for last in lasts]
    now = firsts
    done = []
    for j in range(8):
        below, above = source[x - 1, j], source[x + depth, j]
        column = [below, *now, above]
        ahead = []
        for i in range(depth):
            if j == 7:
                ahead.append(pltpu.roll(firsts[i], 7, 0))
            else:
                ahead.append(lasts[i] if j == 6 else source[x + i, j + 1])
        for i in range(depth):
            value = (
                (weights[wx + i, 0, j] * now[i] + weights[wx + i, 1, j] * column[i])
                + (weights[wx + i, 2, j] * column[i + 2] + weights[wx + i, 3, j] * behind[i])
                + (weights[wx + i, 4, j] * ahead[i] + weights[wx + i, 5, j] * pltpu.roll(now[i], 1, 1))
                + weights[wx + i, 6, j] * pltpu.roll(now[i], 511, 1)
            )
            done.append((tx + i, j, value))
        behind, now = now, ahead
        if j % 2:
            for at, tile, value in done:
                target[at, tile] = value
            done = []


def sweep(source, goal, begin, count, weights, first, shift=0):
    def pair(i, carry):
        fine_layers(source, weights, goal, begin + 2 * i, first + 2 * i, begin + 2 * i - shift, 2)
        return carry

    if count > 1:
        lax.fori_loop(0, count // 2, pair, 0)
    if count % 2:
        last = count - 1
        fine_layers(source, weights, goal, begin + last, first + last, begin + last - shift, 1)


def join(parts, joined):
    begin = 0
    for part in parts:
        joined[begin : begin + part.shape[0]] = part[...]
        begin += part.shape[0]


def first_kernel(place, state, outer, inner, own, own_outer, own_inner, *refs):
    *parts, out, near, far, joined, one, two, buffer = refs
    join(parts, joined)
    core = place[2]

    def enter(x, carry):
        blocks = ((state, LAYERS), (outer, 2 * LAYERS * core), (inner, 2 * LAYERS * (1 - core)))
        for i, (ref, begin) in enumerate(blocks):
            spread(ref[(STATE_AT if ref is inner else 0) + x], buffer.at[i])
            for j in range(8):
                one[begin + x, j] = spread_tile(buffer.at[i], j)
        return carry

    lax.fori_loop(0, LAYERS, enter, 0)
    source, target = one, two
    for step in range(1, LAYERS + 1):
        ends = step == LAYERS
        goal = out if ends else target
        depth = LAYERS - step
        sweep(source, goal, LAYERS, LAYERS, own, 0, LAYERS if ends else 0)
        if depth > 0:
            below, above = step, 2 * LAYERS
            sweep(source, goal, below + core * (above - below), depth, own_outer, (1 - core) * (step - 1))
            sweep(source, goal, above - core * (above - below), depth, own_inner, core * (step - 1))
        source, target = target, source
    for i in range(2):
        near[i] = out[2 * core + i]
        far[i] = out[2 - 2 * core + i]


def passed_at(step, core):
    return 2 + step + core * (6 - 2 * step)


def near_kernel(place, state, inner, near, own, own_inner, own_outer, passed, rest, one, two):
    core = place[2]

    def enter(x, carry):
        for j in range(8):
            one[LAYERS + x, j] = state[x, j]
            one[2 * LAYERS * (1 - core) + x, j] = inner[x, j]
        return carry

    lax.fori_loop(0, LAYERS, enter, 0)
    for i in range(2):
        one[2 + 6 * core + i] = near[i]
    sweep(one, two, 3 + 5 * core, 1, own_outer, 2 - 2 * core)
    sweep(one, two, 4, 4, own, 0)
    sweep(one, two, 8 - 7 * core, 3, own_inner, 0)
    for i in range(2):
        passed[0, i] = two[passed_at(1, core) + i]
    sweep(two, one, 4, 4, own, 0)
    sweep(two, one, 8 - 6 * core, 2, own_inner, core)
    for i in range(2):
        passed[1, i] = one[passed_at(2, core) + i]
    sweep(one, two, 5 - core, 3, own, 1 - core)
    sweep(one, two, 8 - 5 * core, 1, own_inner, 2 * core)
    for i in range(2):
        passed[2, i] = two[passed_at(3, core) + i]
    sweep(two, rest, 6 - 2 * core, 2, own, 2 - 2 * core, 6 - 2 * core)


def far_kernel(final, place, near, far, own, own_outer, passed, rest, *refs):
    if final:
        later, after, out, residual, one, two = refs
    else:
        *parts, out, next_near, joined, one, two = refs
        join(parts, joined)
    core = place[2]
    for i in range(2):
        one[10 * core + i] = far[i]
        one[2 + 6 * core + i] = near[i]
    sweep(one, two, 1 + 8 * core, 2, own_outer, core)
    for i in range(2):
        two[passed_at(1, core) + i] = passed[0, i]
    sweep(two, one, 2 + 6 * core, 2, own_outer, 1 - core)
    for i in range(2):
        one[passed_at(2, core) + i] = passed[1, i]
    sweep(one, two, 3 + 5 * core, 1, own_outer, 2 - 2 * core)
    sweep(one, two, 4 + 3 * core, 1, own, 3 * core)
    for i in range(2):
        two[passed_at(3, core) + i] = passed[2, i]
    sweep(two, out, 4 + 2 * core, 2, own, 2 * core, LAYERS)
    for i in range(2):
        out[2 - 2 * core + i] = rest[i]
    if final:
        sums = half_sums(lambda j: (out[0, j] + out[1, j]) + (out[2, j] + out[3, j]))
        means = exact_dot(jnp.concatenate(sums, axis=0), fours((512, 128), 0)) * (1.0 / 64)
        for h in range(2):
            left = means[8 * h : 8 * h + 8] - later[h]
            for copy in range(residual.shape[0]):
                residual[copy, h] = left
    else:
        for i in range(2):
            next_near[i] = out[2 * core + i]


def coarse_step(read, weights, write, count):
    first = read(0)
    behind, now = read(count - 1), first
    for x in range(count):
        ahead = read(x + 1) if x + 1 < count else first
        for h in range(2):
            behind_y = now[0] if h else pltpu.roll(now[1], 1, 0)
            ahead_y = pltpu.roll(now[0], 7, 0) if h else now[1]
            behind_z = pltpu.roll(now[h], 1, 1)
            ahead_z = pltpu.roll(now[h], 127, 1)
            write(
                x,
                h,
                (weights[x, 0, h] * now[h] + weights[x, 1, h] * behind[h])
                + (weights[x, 2, h] * ahead[h] + weights[x, 3, h] * behind_y)
                + (weights[x, 4, h] * ahead_y + weights[x, 5, h] * behind_z)
                + weights[x, 6, h] * ahead_z,
            )
        behind, now = now, ahead


def mask_of(i):
    return 8 * (i & 3) | ((i >> 1) & 2) | ((i >> 1) & 4) | (i >> 4)


def coarse_weight_kernel(place, some, others, weights):
    row = place[1]
    half = some.shape[0]
    for i in range(2 * half):
        x = row ^ mask_of(i)
        for h in range(2):
            parts = [(some if i < half else others)[i % half, f, h] for f in range(4)]
            for k, weight in enumerate(weigh(parts[:3], parts[3], STEP * RATIO, 1.0 * RATIO)):
                weights[x, k, h] = weight


def chain_kernel(place, residuals, given, shares, weights, one, two):
    count = weights.shape[0]
    slices = shares.shape[0]
    weights[...] = given[...]
    slice_index = place[0]
    layer_index = place[1]
    shares[...] = jnp.zeros(shares.shape, F32)
    one[...] = residuals[...]

    def reader(ref):
        return lambda x: [ref[x, h] for h in range(2)]

    def writer(ref):
        def write(x, h, value):
            ref[x, h] = value

        return write

    def link(n, carry):
        for source, target in ((one, two), (two, one)) * 2:
            coarse_step(reader(source), weights, writer(target), count)
        for h in range(2):
            shares[n, h] = one[layer_index, h]
        return carry

    lax.fori_loop(slice_index + 1, slices, link, 0)


def finish_kernel(shares, state, out, buffer):
    change = []
    for h in range(2):
        total = shares[0, h]
        for n in range(1, shares.shape[0]):
            total = total + shares[n, h]
        change.append(total)
    wide = exact_dot(jnp.concatenate(change, axis=0), fours((128, 512), 1))
    for x in range(LAYERS):
        for j in range(8):
            h = j // 4
            tile = state[x, j] + wide[8 * h : 8 * h + 8]
            for c in range(4):
                buffer[x, c, pl.ds(j, 8, stride=8), :] = tile[:, 128 * c : 128 * c + 128]
        for c in range(4):
            out[0, x, :, 128 * c : 128 * c + 128] = buffer[x, c]


def swap_inner(block):
    count = lax.axis_size("space")
    return lax.ppermute(block, "space", [(p, p ^ 1) for p in range(count)])


def outer_partner(p, count):
    return (p + 1) % count if p % 2 else (p - 1) % count


def swap_outer(block):
    count = lax.axis_size("space")
    return lax.ppermute(block, "space", [(p, outer_partner(p, count)) for p in range(count)])


def swap_outer_fields(block):
    slices, count = lax.axis_size("cuts"), lax.axis_size("space")
    route = []
    for n in range(slices):
        there = (n + slices // 2) % slices
        route += [(n * count + p, there * count + outer_partner(p, count)) for p in range(count)]
    return lax.ppermute(block, ("cuts", "space"), route)


def across(block, bits):
    slices, count = lax.axis_size("cuts"), lax.axis_size("space")
    if bits == 2:
        route = [
            (n * count + p, (n + slices // 2) % slices * count + (p ^ bits)) for n in range(slices) for p in range(count)
        ]
        return lax.ppermute(block, ("cuts", "space"), route)
    return lax.ppermute(block, "space", [(p, p ^ bits) for p in range(count)])


def shards(starts, velocity, diffusivity):
    count = lax.axis_size("space")
    slices = lax.axis_size("cuts")
    block = (LAYERS, *TILE)
    row = lax.axis_index("space")
    place = jnp.stack([lax.axis_index("cuts"), row, row & 1]).astype(jnp.int32)
    columns = pltpu.VMEM((5, 4, 64, 128), F32)

    fields_outer = call(
        cut_fields_kernel,
        [(3 * REACH, 64, 512)],
        [SMEM, ANY],
        [pltpu.SemaphoreType.DMA((3,))],
        cost=SMALL,
    )(place, velocity)[0]
    mixed_outer, all_inner = call(
        cut_kernel,
        [(LAYERS + REACH, 64, 512), (INNER, 64, 512)],
        [SMEM, ANY, ANY, ANY, ANY],
        [pltpu.SemaphoreType.DMA((7,))],
        cost=SMALL,
    )(place, velocity, diffusivity, starts, fields_outer)
    fields_outer = swap_outer_fields(fields_outer)
    mixed_outer = swap_outer(mixed_outer)
    all_inner = swap_inner(all_inner)
    own_weights, coarse_fields, coarse_old = call(
        own_kernel,
        [(LAYERS, 7, *TILE), (4, *COARSE), COARSE],
        [VMEM] * 3,
        [columns],
        cost=SMALL,
    )(velocity, diffusivity, starts[0])
    coarse_later = lax.ppermute(coarse_old, "cuts", [((n + 1) % slices, n) for n in range(slices)])
    gathered = coarse_fields[None]
    side = [(REACH, 7, *TILE)]
    inner_weights = call(functools.partial(side_kernel, STATE_AT + LAYERS), side, [VMEM, ANY], [columns], cost=SMALL)(
        all_inner, coarse_old
    )[0]
    outer_weights = call(functools.partial(side_kernel, LAYERS), side, [VMEM, VMEM, ANY], [columns], cost=SMALL)(
        fields_outer, mixed_outer, inner_weights
    )[0]
    pair = (2, *TILE)
    scratch = [pltpu.VMEM((3 * LAYERS, *TILE), F32)] * 2
    parts = [gathered] + [across(gathered, bits) for bits in (8, 16, 24)]
    state, near, far, gathered = call(
        first_kernel,
        [block, pair, pair, (4, 4, *COARSE)],
        [SMEM] + [VMEM] * (6 + len(parts)),
        scratch + [columns],
    )(place, starts[0], mixed_outer, all_inner, own_weights, outer_weights, inner_weights, *parts)
    for index in range(1, ROUNDS):
        final = index == ROUNDS - 1
        near, inner, far = swap_outer(near), swap_inner(state), swap_outer(far)
        passed, rest = call(
            near_kernel,
            [(LAYERS - 1, *pair), pair],
            [SMEM] + [VMEM] * 6,
            scratch,
        )(place, state, inner, near, own_weights, inner_weights, outer_weights)
        operands = [place, near, far, own_weights, outer_weights, passed, rest]
        specs = [SMEM] + [VMEM] * 6
        if final:
            weights = call(
                coarse_weight_kernel,
                [(count, 7, *COARSE)],
                [SMEM, VMEM, VMEM],
            )(place, gathered, across(gathered, 1))[0]
            operands += [coarse_later, weights]
            specs += [VMEM, ANY]
            outs = [block, (count, *COARSE)]
        else:
            parts = [gathered, across(gathered, (2, 4)[index - 1])]
            operands += parts
            specs += [VMEM] * len(parts)
            outs = [block, pair, (2 * gathered.shape[0], 4, *COARSE)]
        state, *near, gathered = call(functools.partial(far_kernel, final), outs, specs, scratch)(*operands)
        near, far = near[0] if near else None, rest
    residuals = lax.all_to_all(gathered, "space", 0, 0)
    shares = call(
        chain_kernel,
        [(slices, *COARSE)],
        [SMEM, VMEM, VMEM],
        [pltpu.VMEM((count, 7, *COARSE), F32)] + [pltpu.VMEM((count, *COARSE), F32)] * 2,
    )(place, residuals, weights)[0]
    shares = lax.all_to_all(shares, "cuts", 0, 0)
    return call(finish_kernel, [(1, LAYERS, 64, 512)], [VMEM, VMEM], [columns])(shares, state)[0]


def solution(mesh):
    placed = (P("cuts", "space", None, None), P(None, "space", None, None), P("space", None, None))
    return jax.shard_map(
        shards,
        mesh=mesh,
        in_specs=placed,
        out_specs=P("cuts", "space", None, None),
        check_vma=False,
    )
```

```python
import functools

import jax
import jax.numpy as jnp
from jax import lax
from jax.experimental import pallas as pl
from jax.experimental.pallas import tpu as pltpu
from jax.sharding import PartitionSpec as P

RATIO = 4
LAYERS = 4
COARSE_STEPS = 4
REACH = 3
ROUNDS = 4
TILE = (8, 8, 512)
COARSE = (2, 8, 128)
STEP = 0.2
VMEM = pl.BlockSpec(memory_space=pltpu.VMEM)
SMEM = pl.BlockSpec(memory_space=pltpu.SMEM)
ANY = pl.BlockSpec(memory_space=pl.ANY)
F32 = jnp.float32
MIB = 1024 * 1024
SMALL = pl.CostEstimate(flops=1, bytes_accessed=1, transcendentals=0)


def call(body, outs, ins, scratch=(), limit=24, cost=None):
    return pl.pallas_call(
        body,
        out_shape=[jax.ShapeDtypeStruct(s, F32) for s in outs],
        in_specs=ins,
        out_specs=[VMEM] * len(outs),
        scratch_shapes=list(scratch),
        cost_estimate=cost,
        compiler_params=pltpu.CompilerParams(vmem_limit_bytes=limit * MIB),
    )


def fours(shape, fine):
    z = lax.broadcasted_iota(jnp.int32, shape, fine)
    block = lax.broadcasted_iota(jnp.int32, shape, 1 - fine)
    return jnp.where((z >> 2) == block, 1.0, 0.0).astype(jnp.bfloat16)


def exact_dot(rows, matrix):
    count = rows.shape[0]
    high = rows.astype(jnp.bfloat16)
    rest = rows - high.astype(F32)
    middle = rest.astype(jnp.bfloat16)
    low = (rest - middle.astype(F32)).astype(jnp.bfloat16)
    parts = jnp.concatenate([high, middle, low], axis=0)
    moved = jnp.dot(parts, matrix, preferred_element_type=F32)
    return (moved[:count] + moved[count : 2 * count]) + moved[2 * count :]


def spread(rows, buffer):
    for c in range(4):
        buffer[c] = rows[:, 128 * c : 128 * c + 128]


def spread_tile(buffer, j):
    return jnp.concatenate([buffer[c, pl.ds(j, 8, stride=8), :] for c in range(4)], axis=1)


def half_sums(read):
    sums = []
    for h in range(2):
        total = read(4 * h)
        for j in range(4 * h + 1, 4 * h + 4):
            total = total + read(j)
        sums.append(total)
    return sums


def weigh(velocity, diffusion, step, spacing):
    spread = diffusion * (step / (spacing * spacing))
    weights = [None]
    for component in velocity:
        moved = component * (step / spacing)
        weights.append(spread + jnp.maximum(moved, 0.0))
        weights.append(spread - jnp.minimum(moved, 0.0))
    total = weights[1]
    for weight in weights[2:]:
        total = total + weight
    weights[0] = 1.0 - total
    return weights


def run(pairs, ready):
    copies = [pltpu.make_async_copy(*pair, ready.at[i]) for i, pair in enumerate(pairs)]
    for copy in copies:
        copy.start()
    for copy in copies:
        copy.wait()


def cut_fields_kernel(place, velocity, fields, ready):
    run([(velocity.at[f, pl.ds(place[2], REACH)], fields.at[pl.ds(f * REACH, REACH)]) for f in range(3)], ready)


STATE_AT = 3 * REACH
INNER = STATE_AT + LAYERS + REACH


def cut_kernel(place, velocity, diffusivity, starts, earlier, mixed, inner, ready):
    core = place[2]
    pairs = [
        (diffusivity.at[pl.ds(core, REACH)], mixed.at[pl.ds(LAYERS, REACH)]),
        (starts.at[0], mixed.at[pl.ds(0, LAYERS)]),
        (diffusivity.at[pl.ds(1 - core, REACH)], inner.at[pl.ds(STATE_AT + LAYERS, REACH)]),
        (starts.at[0], inner.at[pl.ds(STATE_AT, LAYERS)]),
    ]
    for f in range(3):
        pairs.append((velocity.at[f, pl.ds(1 - core, REACH)], inner.at[pl.ds(f * REACH, REACH)]))
    run(pairs, ready)


def own_kernel(velocity, diffusivity, starts, weights, coarse_fields, coarse_old, buffer):
    def layer(x, carry):
        for f in range(3):
            spread(velocity[f, x], buffer.at[f])
        spread(diffusivity[x], buffer.at[3])
        for j in range(8):
            parts = [spread_tile(buffer.at[f], j) for f in range(4)]
            for i, weight in enumerate(weigh(parts[:3], parts[3], STEP, 1.0)):
                weights[x, i, j] = weight
        return carry

    lax.fori_loop(0, LAYERS, layer, 0)
    sums = []
    for f in range(5):
        layers = [velocity[f, x] if f < 3 else (diffusivity[x], starts[x])[f - 3] for x in range(LAYERS)]
        spread((layers[0] + layers[1]) + (layers[2] + layers[3]), buffer.at[f])
        sums += half_sums(lambda j, f=f: spread_tile(buffer.at[f], j))
    means = exact_dot(jnp.concatenate(sums, axis=0), fours((512, 128), 0)) * (1.0 / 64)
    for f in range(5):
        for h in range(2):
            mean = means[16 * f + 8 * h : 16 * f + 8 * h + 8]
            if f < 4:
                coarse_fields[f, h] = mean
            else:
                coarse_old[h] = mean


def side_kernel(at, *refs):
    *fields, earlier, weights, buffer = refs

    def layer(x, carry):
        for f in range(3):
            spread(fields[0][f * REACH + x], buffer.at[f])
        spread(fields[-1][at + x], buffer.at[3])
        for j in range(8):
            parts = [spread_tile(buffer.at[f], j) for f in range(4)]
            for i, weight in enumerate(weigh(parts[:3], parts[3], STEP, 1.0)):
                weights[x, i, j] = weight
        return carry

    lax.fori_loop(0, REACH, layer, 0)


def fine_layers(source, weights, target, x, wx, tx, depth):
    firsts = [source[x + i, 0] for i in range(depth)]
    lasts = [source[x + i, 7] for i in range(depth)]
    behind = [pltpu.roll(last, 1, 0) for last in lasts]
    now = firsts
    done = []
    for j in range(8):
        below, above = source[x - 1, j], source[x + depth, j]
        column = [below, *now, above]
        ahead = []
        for i in range(depth):
            if j == 7:
                ahead.append(pltpu.roll(firsts[i], 7, 0))
            else:
                ahead.append(lasts[i] if j == 6 else source[x + i, j + 1])
        for i in range(depth):
            value = (
                (weights[wx + i, 0, j] * now[i] + weights[wx + i, 1, j] * column[i])
                + (weights[wx + i, 2, j] * column[i + 2] + weights[wx + i, 3, j] * behind[i])
                + (weights[wx + i, 4, j] * ahead[i] + weights[wx + i, 5, j] * pltpu.roll(now[i], 1, 1))
                + weights[wx + i, 6, j] * pltpu.roll(now[i], 511, 1)
            )
            done.append((tx + i, j, value))
        behind, now = now, ahead
        if j % 2:
            for at, tile, value in done:
                target[at, tile] = value
            done = []


def sweep(source, goal, begin, count, weights, first, shift=0):
    def pair(i, carry):
        fine_layers(source, weights, goal, begin + 2 * i, first + 2 * i, begin + 2 * i - shift, 2)
        return carry

    if count > 1:
        lax.fori_loop(0, count // 2, pair, 0)
    if count % 2:
        last = count - 1
        fine_layers(source, weights, goal, begin + last, first + last, begin + last - shift, 1)


def join(parts, joined):
    begin = 0
    for part in parts:
        joined[begin : begin + part.shape[0]] = part[...]
        begin += part.shape[0]


def first_kernel(place, state, outer, inner, own, own_outer, own_inner, *refs):
    *parts, out, near, far, joined, one, two, buffer = refs
    join(parts, joined)
    core = place[2]

    def enter(x, carry):
        blocks = ((state, LAYERS), (outer, 2 * LAYERS * core), (inner, 2 * LAYERS * (1 - core)))
        for i, (ref, begin) in enumerate(blocks):
            spread(ref[(STATE_AT if ref is inner else 0) + x], buffer.at[i])
            for j in range(8):
                one[begin + x, j] = spread_tile(buffer.at[i], j)
        return carry

    lax.fori_loop(0, LAYERS, enter, 0)
    source, target = one, two
    for step in range(1, LAYERS + 1):
        ends = step == LAYERS
        goal = out if ends else target
        depth = LAYERS - step
        sweep(source, goal, LAYERS, LAYERS, own, 0, LAYERS if ends else 0)
        if depth > 0:
            below, above = step, 2 * LAYERS
            sweep(source, goal, below + core * (above - below), depth, own_outer, (1 - core) * (step - 1))
            sweep(source, goal, above - core * (above - below), depth, own_inner, core * (step - 1))
        source, target = target, source
    for i in range(2):
        near[i] = out[2 * core + i]
        far[i] = out[2 - 2 * core + i]


def passed_at(step, core):
    return 2 + step + core * (6 - 2 * step)


def near_kernel(place, state, inner, near, own, own_inner, own_outer, passed, rest, one, two):
    core = place[2]

    def enter(x, carry):
        for j in range(8):
            one[LAYERS + x, j] = state[x, j]
            one[2 * LAYERS * (1 - core) + x, j] = inner[x, j]
        return carry

    lax.fori_loop(0, LAYERS, enter, 0)
    for i in range(2):
        one[2 + 6 * core + i] = near[i]
    sweep(one, two, 3 + 5 * core, 1, own_outer, 2 - 2 * core)
    sweep(one, two, 4, 4, own, 0)
    sweep(one, two, 8 - 7 * core, 3, own_inner, 0)
    for i in range(2):
        passed[0, i] = two[passed_at(1, core) + i]
    sweep(two, one, 4, 4, own, 0)
    sweep(two, one, 8 - 6 * core, 2, own_inner, core)
    for i in range(2):
        passed[1, i] = one[passed_at(2, core) + i]
    sweep(one, two, 5 - core, 3, own, 1 - core)
    sweep(one, two, 8 - 5 * core, 1, own_inner, 2 * core)
    for i in range(2):
        passed[2, i] = two[passed_at(3, core) + i]
    sweep(two, rest, 6 - 2 * core, 2, own, 2 - 2 * core, 6 - 2 * core)


def far_kernel(final, place, near, far, own, own_outer, passed, rest, *refs):
    if final:
        later, after, out, residual, one, two = refs
    else:
        *parts, early, out, next_near, joined, one, two = refs
        join(parts, joined)
    core = place[2]
    for i in range(2):
        one[10 * core + i] = far[i]
        one[2 + 6 * core + i] = near[i]
    sweep(one, two, 1 + 8 * core, 2, own_outer, core)
    for i in range(2):
        two[passed_at(1, core) + i] = passed[0, i]
    sweep(two, one, 2 + 6 * core, 2, own_outer, 1 - core)
    for i in range(2):
        one[passed_at(2, core) + i] = passed[1, i]
    sweep(one, two, 3 + 5 * core, 1, own_outer, 2 - 2 * core)
    sweep(one, two, 4 + 3 * core, 1, own, 3 * core)
    for i in range(2):
        two[passed_at(3, core) + i] = passed[2, i]
    sweep(two, out, 4 + 2 * core, 2, own, 2 * core, LAYERS)
    for i in range(2):
        out[2 - 2 * core + i] = rest[i]
    if final:
        sums = half_sums(lambda j: (out[0, j] + out[1, j]) + (out[2, j] + out[3, j]))
        means = exact_dot(jnp.concatenate(sums, axis=0), fours((512, 128), 0)) * (1.0 / 64)
        for h in range(2):
            left = means[8 * h : 8 * h + 8] - later[h]
            for copy in range(residual.shape[0]):
                residual[copy, h] = left
    else:
        for i in range(2):
            next_near[i] = out[2 * core + i]


def coarse_step(read, weights, write, begin, end, count):
    behind, now = read((begin - 1) % count), read(begin)
    for x in range(begin, end):
        ahead = read((x + 1) % count)
        for h in range(2):
            behind_y = now[0] if h else pltpu.roll(now[1], 1, 0)
            ahead_y = pltpu.roll(now[0], 7, 0) if h else now[1]
            behind_z = pltpu.roll(now[h], 1, 1)
            ahead_z = pltpu.roll(now[h], 127, 1)
            write(
                x,
                h,
                (weights[x, 0, h] * now[h] + weights[x, 1, h] * behind[h])
                + (weights[x, 2, h] * ahead[h] + weights[x, 3, h] * behind_y)
                + (weights[x, 4, h] * ahead_y + weights[x, 5, h] * behind_z)
                + weights[x, 6, h] * ahead_z,
            )
        behind, now = now, ahead


def mask_of(i):
    return 8 * (i & 3) | ((i >> 1) & 2) | ((i >> 1) & 4) | (i >> 4)


def coarse_weight_kernel(place, some, others, weights):
    row = place[1]
    half = some.shape[0]
    for i in range(2 * half):
        x = row ^ mask_of(i)
        for h in range(2):
            parts = [(some if i < half else others)[i % half, f, h] for f in range(4)]
            for k, weight in enumerate(weigh(parts[:3], parts[3], STEP * RATIO, 1.0 * RATIO)):
                weights[x, k, h] = weight


def chain_kernel(place, residuals, given, shares, weights, one, two):
    count = weights.shape[0]
    slices = shares.shape[0]
    slice_index = place[0]
    layer_index = place[1]
    middle = count // 2
    shares[...] = jnp.zeros(shares.shape, F32)
    for x in range(count):
        at = (x - layer_index + middle) & (count - 1)
        weights[at] = given[x]
        one[at] = residuals[x]

    def reader(ref):
        return lambda x: [ref[x, h] for h in range(2)]

    def writer(ref):
        def write(x, h, value):
            ref[x, h] = value

        return write

    def propagate(ranges):
        for (source, target), (begin, end) in zip(((one, two), (two, one)) * 2, ranges, strict=True):
            coarse_step(reader(source), weights, writer(target), begin, end, count)

    def share(n):
        for h in range(2):
            shares[n, h] = one[middle, h]

    def link(n, carry):
        propagate([(0, count)] * 4)
        share(n)
        return carry

    narrow = 4
    lax.fori_loop(slice_index + 1, slices - narrow, link, 0)
    for left in range(narrow - 1, -1, -1):

        @pl.when(slices - 1 - slice_index > left)
        def _(left=left):
            reach = [COARSE_STEPS * left + COARSE_STEPS - 1 - step for step in range(COARSE_STEPS)]
            propagate([(middle - r, middle + r + 1) for r in reach])
            share(slices - 1 - left)


def finish_kernel(shares, state, out, buffer):
    change = []
    for h in range(2):
        total = shares[0, h]
        for n in range(1, shares.shape[0]):
            total = total + shares[n, h]
        change.append(total)
    wide = exact_dot(jnp.concatenate(change, axis=0), fours((128, 512), 1))
    for x in range(LAYERS):
        for j in range(8):
            h = j // 4
            tile = state[x, j] + wide[8 * h : 8 * h + 8]
            for c in range(4):
                buffer[x, c, pl.ds(j, 8, stride=8), :] = tile[:, 128 * c : 128 * c + 128]
        for c in range(4):
            out[0, x, :, 128 * c : 128 * c + 128] = buffer[x, c]


def swap_inner(block):
    count = lax.axis_size("space")
    return lax.ppermute(block, "space", [(p, p ^ 1) for p in range(count)])


def outer_partner(p, count):
    return (p + 1) % count if p % 2 else (p - 1) % count


def swap_outer(block):
    count = lax.axis_size("space")
    return lax.ppermute(block, "space", [(p, outer_partner(p, count)) for p in range(count)])


def swap_outer_fields(block):
    slices, count = lax.axis_size("cuts"), lax.axis_size("space")
    route = []
    for n in range(slices):
        there = (n + slices // 2) % slices
        route += [(n * count + p, there * count + outer_partner(p, count)) for p in range(count)]
    return lax.ppermute(block, ("cuts", "space"), route)


def across(block, bits):
    slices, count = lax.axis_size("cuts"), lax.axis_size("space")
    if bits == 2:
        route = [
            (n * count + p, (n + slices // 2) % slices * count + (p ^ bits)) for n in range(slices) for p in range(count)
        ]
        return lax.ppermute(block, ("cuts", "space"), route)
    return lax.ppermute(block, "space", [(p, p ^ bits) for p in range(count)])


def shards(starts, velocity, diffusivity):
    count = lax.axis_size("space")
    slices = lax.axis_size("cuts")
    block = (LAYERS, *TILE)
    row = lax.axis_index("space")
    place = jnp.stack([lax.axis_index("cuts"), row, row & 1]).astype(jnp.int32)
    columns = pltpu.VMEM((5, 4, 64, 128), F32)

    fields_outer = call(
        cut_fields_kernel,
        [(3 * REACH, 64, 512)],
        [SMEM, ANY],
        [pltpu.SemaphoreType.DMA((3,))],
        cost=SMALL,
    )(place, velocity)[0]
    mixed_outer, all_inner = call(
        cut_kernel,
        [(LAYERS + REACH, 64, 512), (INNER, 64, 512)],
        [SMEM, ANY, ANY, ANY, ANY],
        [pltpu.SemaphoreType.DMA((7,))],
        cost=SMALL,
    )(place, velocity, diffusivity, starts, fields_outer)
    fields_outer = swap_outer_fields(fields_outer)
    mixed_outer = swap_outer(mixed_outer)
    all_inner = swap_inner(all_inner)
    own_weights, coarse_fields, coarse_old = call(
        own_kernel,
        [(LAYERS, 7, *TILE), (4, *COARSE), COARSE],
        [VMEM] * 3,
        [columns],
        cost=SMALL,
    )(velocity, diffusivity, starts[0])
    coarse_later = lax.ppermute(coarse_old, "cuts", [((n + 1) % slices, n) for n in range(slices)])
    gathered = coarse_fields[None]
    side = [(REACH, 7, *TILE)]
    inner_weights = call(functools.partial(side_kernel, STATE_AT + LAYERS), side, [VMEM, ANY], [columns], cost=SMALL)(
        all_inner, coarse_old
    )[0]
    outer_weights = call(functools.partial(side_kernel, LAYERS), side, [VMEM, VMEM, ANY], [columns], cost=SMALL)(
        fields_outer, mixed_outer, inner_weights
    )[0]
    pair = (2, *TILE)
    scratch = [pltpu.VMEM((3 * LAYERS, *TILE), F32)] * 2
    parts = [gathered] + [across(gathered, bits) for bits in (8, 16, 24)]
    state, near, far, gathered = call(
        first_kernel,
        [block, pair, pair, (4, 4, *COARSE)],
        [SMEM] + [VMEM] * (6 + len(parts)),
        scratch + [columns],
    )(place, starts[0], mixed_outer, all_inner, own_weights, outer_weights, inner_weights, *parts)
    for index in range(1, ROUNDS):
        final = index == ROUNDS - 1
        near, inner, far = swap_outer(near), swap_inner(state), swap_outer(far)
        passed, rest = call(
            near_kernel,
            [(LAYERS - 1, *pair), pair],
            [SMEM] + [VMEM] * 6,
            scratch,
        )(place, state, inner, near, own_weights, inner_weights, outer_weights)
        operands = [place, near, far, own_weights, outer_weights, passed, rest]
        specs = [SMEM] + [VMEM] * 6
        if final:
            weights = call(
                coarse_weight_kernel,
                [(count, 7, *COARSE)],
                [SMEM, VMEM, VMEM],
            )(place, gathered, across(gathered, 1))[0]
            operands += [coarse_later, weights]
            specs += [VMEM, ANY]
            outs = [block, (count, *COARSE)]
        else:
            parts = [gathered, across(gathered, (2, 4)[index - 1])]
            operands += parts + [coarse_later if index == 2 else coarse_old]
            specs += [VMEM] * len(parts) + [ANY]
            outs = [block, pair, (2 * gathered.shape[0], 4, *COARSE)]
        state, *near, gathered = call(functools.partial(far_kernel, final), outs, specs, scratch)(*operands)
        near, far = near[0] if near else None, rest
    residuals = lax.all_to_all(gathered, "space", 0, 0)
    shares = call(
        chain_kernel,
        [(slices, *COARSE)],
        [SMEM, VMEM, VMEM],
        [pltpu.VMEM((count, 7, *COARSE), F32)] + [pltpu.VMEM((count, *COARSE), F32)] * 2,
    )(place, residuals, weights)[0]
    shares = lax.all_to_all(shares, "cuts", 0, 0)
    return call(finish_kernel, [(1, LAYERS, 64, 512)], [VMEM, VMEM], [columns])(shares, state)[0]


def solution(mesh):
    placed = (P("cuts", "space", None, None), P(None, "space", None, None), P("space", None, None))
    return jax.shard_map(
        shards,
        mesh=mesh,
        in_specs=placed,
        out_specs=P("cuts", "space", None, None),
        check_vma=False,
    )
```

```python
import functools

import jax
import jax.numpy as jnp
from jax import lax
from jax.experimental import pallas as pl
from jax.experimental.pallas import tpu as pltpu
from jax.sharding import PartitionSpec as P

RATIO = 4
LAYERS = 4
COARSE_STEPS = 4
REACH = 3
ROUNDS = 4
TILE = (8, 8, 512)
COARSE = (2, 8, 128)
STEP = 0.2
VMEM = pl.BlockSpec(memory_space=pltpu.VMEM)
SMEM = pl.BlockSpec(memory_space=pltpu.SMEM)
ANY = pl.BlockSpec(memory_space=pl.ANY)
F32 = jnp.float32
MIB = 1024 * 1024
SMALL = pl.CostEstimate(flops=1, bytes_accessed=1, transcendentals=0)


def call(body, outs, ins, scratch=(), limit=24, cost=None):
    return pl.pallas_call(
        body,
        out_shape=[jax.ShapeDtypeStruct(s, F32) for s in outs],
        in_specs=ins,
        out_specs=[VMEM] * len(outs),
        scratch_shapes=list(scratch),
        cost_estimate=cost,
        compiler_params=pltpu.CompilerParams(vmem_limit_bytes=limit * MIB),
    )


def fours(shape, fine):
    z = lax.broadcasted_iota(jnp.int32, shape, fine)
    block = lax.broadcasted_iota(jnp.int32, shape, 1 - fine)
    return jnp.where((z >> 2) == block, 1.0, 0.0).astype(jnp.bfloat16)


def exact_dot(rows, matrix):
    count = rows.shape[0]
    high = rows.astype(jnp.bfloat16)
    rest = rows - high.astype(F32)
    middle = rest.astype(jnp.bfloat16)
    low = (rest - middle.astype(F32)).astype(jnp.bfloat16)
    parts = jnp.concatenate([high, middle, low], axis=0)
    moved = jnp.dot(parts, matrix, preferred_element_type=F32)
    return (moved[:count] + moved[count : 2 * count]) + moved[2 * count :]


def spread(rows, buffer):
    for c in range(4):
        buffer[c] = rows[:, 128 * c : 128 * c + 128]


def spread_tile(buffer, j):
    return jnp.concatenate([buffer[c, pl.ds(j, 8, stride=8), :] for c in range(4)], axis=1)


def half_sums(read):
    sums = []
    for h in range(2):
        total = read(4 * h)
        for j in range(4 * h + 1, 4 * h + 4):
            total = total + read(j)
        sums.append(total)
    return sums


def weigh(velocity, diffusion, step, spacing):
    spread = diffusion * (step / (spacing * spacing))
    weights = [None]
    for component in velocity:
        moved = component * (step / spacing)
        weights.append(spread + jnp.maximum(moved, 0.0))
        weights.append(spread - jnp.minimum(moved, 0.0))
    total = weights[1]
    for weight in weights[2:]:
        total = total + weight
    weights[0] = 1.0 - total
    return weights


def run(pairs, ready):
    copies = [pltpu.make_async_copy(*pair, ready.at[i]) for i, pair in enumerate(pairs)]
    for copy in copies:
        copy.start()
    for copy in copies:
        copy.wait()


def cut_fields_kernel(place, velocity, fields, ready):
    run([(velocity.at[f, pl.ds(place[2], REACH)], fields.at[pl.ds(f * REACH, REACH)]) for f in range(3)], ready)


STATE_AT = 3 * REACH
INNER = STATE_AT + LAYERS + REACH


def cut_kernel(place, velocity, diffusivity, starts, earlier, mixed, inner, ready):
    core = place[2]
    pairs = [
        (diffusivity.at[pl.ds(core, REACH)], mixed.at[pl.ds(LAYERS, REACH)]),
        (starts.at[0], mixed.at[pl.ds(0, LAYERS)]),
        (diffusivity.at[pl.ds(1 - core, REACH)], inner.at[pl.ds(STATE_AT + LAYERS, REACH)]),
        (starts.at[0], inner.at[pl.ds(STATE_AT, LAYERS)]),
    ]
    for f in range(3):
        pairs.append((velocity.at[f, pl.ds(1 - core, REACH)], inner.at[pl.ds(f * REACH, REACH)]))
    run(pairs, ready)


def own_kernel(velocity, diffusivity, starts, weights, coarse_fields, coarse_old, buffer):
    def layer(x, carry):
        for f in range(3):
            spread(velocity[f, x], buffer.at[f])
        spread(diffusivity[x], buffer.at[3])
        for j in range(8):
            parts = [spread_tile(buffer.at[f], j) for f in range(4)]
            for i, weight in enumerate(weigh(parts[:3], parts[3], STEP, 1.0)):
                weights[x, i, j] = weight
        return carry

    lax.fori_loop(0, LAYERS, layer, 0)
    sums = []
    for f in range(5):
        layers = [velocity[f, x] if f < 3 else (diffusivity[x], starts[x])[f - 3] for x in range(LAYERS)]
        spread((layers[0] + layers[1]) + (layers[2] + layers[3]), buffer.at[f])
        sums += half_sums(lambda j, f=f: spread_tile(buffer.at[f], j))
    means = exact_dot(jnp.concatenate(sums, axis=0), fours((512, 128), 0)) * (1.0 / 64)
    for f in range(5):
        for h in range(2):
            mean = means[16 * f + 8 * h : 16 * f + 8 * h + 8]
            if f < 4:
                coarse_fields[f, h] = mean
            else:
                coarse_old[h] = mean


def side_kernel(at, *refs):
    *fields, earlier, weights, buffer = refs

    def layer(x, carry):
        for f in range(3):
            spread(fields[0][f * REACH + x], buffer.at[f])
        spread(fields[-1][at + x], buffer.at[3])
        for j in range(8):
            parts = [spread_tile(buffer.at[f], j) for f in range(4)]
            for i, weight in enumerate(weigh(parts[:3], parts[3], STEP, 1.0)):
                weights[x, i, j] = weight
        return carry

    lax.fori_loop(0, REACH, layer, 0)


def fine_layers(source, weights, target, x, wx, tx, depth):
    firsts = [source[x + i, 0] for i in range(depth)]
    lasts = [source[x + i, 7] for i in range(depth)]
    behind = [pltpu.roll(last, 1, 0) for last in lasts]
    now = firsts
    done = []
    for j in range(8):
        below, above = source[x - 1, j], source[x + depth, j]
        column = [below, *now, above]
        ahead = []
        for i in range(depth):
            if j == 7:
                ahead.append(pltpu.roll(firsts[i], 7, 0))
            else:
                ahead.append(lasts[i] if j == 6 else source[x + i, j + 1])
        for i in range(depth):
            value = (
                (weights[wx + i, 0, j] * now[i] + weights[wx + i, 1, j] * column[i])
                + (weights[wx + i, 2, j] * column[i + 2] + weights[wx + i, 3, j] * behind[i])
                + (weights[wx + i, 4, j] * ahead[i] + weights[wx + i, 5, j] * pltpu.roll(now[i], 1, 1))
                + weights[wx + i, 6, j] * pltpu.roll(now[i], 511, 1)
            )
            done.append((tx + i, j, value))
        behind, now = now, ahead
        if j % 2:
            for at, tile, value in done:
                target[at, tile] = value
            done = []


def sweep(source, goal, begin, count, weights, first, shift=0):
    def pair(i, carry):
        fine_layers(source, weights, goal, begin + 2 * i, first + 2 * i, begin + 2 * i - shift, 2)
        return carry

    if count > 1:
        lax.fori_loop(0, count // 2, pair, 0)
    if count % 2:
        last = count - 1
        fine_layers(source, weights, goal, begin + last, first + last, begin + last - shift, 1)


def join(parts, joined):
    begin = 0
    for part in parts:
        joined[begin : begin + part.shape[0]] = part[...]
        begin += part.shape[0]


def first_inner_kernel(place, state, inner, own, own_inner, passed, one, two, buffer):
    core = place[2]

    def enter(x, carry):
        blocks = ((state, x, LAYERS), (inner, STATE_AT + x, 2 * LAYERS * (1 - core)))
        for i, (ref, at, begin) in enumerate(blocks):
            spread(ref[at], buffer.at[i])
            for j in range(8):
                one[begin + x, j] = spread_tile(buffer.at[i], j)
        return carry

    lax.fori_loop(0, LAYERS, enter, 0)
    source, target = one, two
    for step in range(1, LAYERS):
        count = LAYERS - step
        sweep(source, target, LAYERS + (1 - core) * step, count, own, (1 - core) * step)
        above, below = 2 * LAYERS, step
        sweep(source, target, above - core * (above - below), count, own_inner, core * (step - 1))
        for i in range(2):
            on_first, on_second = LAYERS + step + i, 2 * LAYERS - 1 - step - i
            passed[step - 1, i] = target[on_first - core * (on_first - on_second)]
        source, target = target, source


def first_outer_kernel(place, state, outer, own, own_outer, passed, *refs):
    *parts, out, near, far, joined, one, two, buffer = refs
    join(parts, joined)
    core = place[2]

    def enter(x, carry):
        spread(outer[x], buffer.at[0])
        for j in range(8):
            one[2 * LAYERS * core + x, j] = spread_tile(buffer.at[0], j)
        return carry

    lax.fori_loop(0, LAYERS, enter, 0)
    for i in range(2):
        spread(state[2 * core + i], buffer.at[1 + i])
        for j in range(8):
            one[LAYERS + 2 * core + i, j] = spread_tile(buffer.at[1 + i], j)
    source, target = one, two
    for step in range(1, LAYERS + 1):
        ends = step == LAYERS
        goal = out if ends else target
        count = LAYERS - step
        if count:
            below, above = step, 2 * LAYERS
            sweep(source, goal, below + core * (above - below), count, own_outer, (1 - core) * (step - 1))
        sweep(source, goal, LAYERS + core * count, step, own, core * count, LAYERS if ends else 0)
        if not ends:
            for i in range(2):
                on_first, on_second = LAYERS + step + i, 2 * LAYERS - 1 - step - i
                target[on_first - core * (on_first - on_second)] = passed[step - 1, i]
        source, target = target, source
    for i in range(2):
        near[i] = out[2 * core + i]
        far[i] = out[2 - 2 * core + i]


def passed_at(step, core):
    return 2 + step + core * (6 - 2 * step)


def near_kernel(place, state, inner, near, own, own_inner, own_outer, passed, rest, one, two):
    core = place[2]

    def enter(x, carry):
        for j in range(8):
            one[LAYERS + x, j] = state[x, j]
            one[2 * LAYERS * (1 - core) + x, j] = inner[x, j]
        return carry

    lax.fori_loop(0, LAYERS, enter, 0)
    for i in range(2):
        one[2 + 6 * core + i] = near[i]
    sweep(one, two, 3 + 5 * core, 1, own_outer, 2 - 2 * core)
    sweep(one, two, 4, 4, own, 0)
    sweep(one, two, 8 - 7 * core, 3, own_inner, 0)
    for i in range(2):
        passed[0, i] = two[passed_at(1, core) + i]
    sweep(two, one, 4, 4, own, 0)
    sweep(two, one, 8 - 6 * core, 2, own_inner, core)
    for i in range(2):
        passed[1, i] = one[passed_at(2, core) + i]
    sweep(one, two, 5 - core, 3, own, 1 - core)
    sweep(one, two, 8 - 5 * core, 1, own_inner, 2 * core)
    for i in range(2):
        passed[2, i] = two[passed_at(3, core) + i]
    sweep(two, rest, 6 - 2 * core, 2, own, 2 - 2 * core, 6 - 2 * core)


def far_kernel(final, place, near, far, own, own_outer, passed, rest, *refs):
    if final:
        later, after, out, residual, one, two = refs
    else:
        *parts, early, out, next_near, joined, one, two = refs
        join(parts, joined)
    core = place[2]
    for i in range(2):
        one[10 * core + i] = far[i]
        one[2 + 6 * core + i] = near[i]
    sweep(one, two, 1 + 8 * core, 2, own_outer, core)
    for i in range(2):
        two[passed_at(1, core) + i] = passed[0, i]
    sweep(two, one, 2 + 6 * core, 2, own_outer, 1 - core)
    for i in range(2):
        one[passed_at(2, core) + i] = passed[1, i]
    sweep(one, two, 3 + 5 * core, 1, own_outer, 2 - 2 * core)
    sweep(one, two, 4 + 3 * core, 1, own, 3 * core)
    for i in range(2):
        two[passed_at(3, core) + i] = passed[2, i]
    sweep(two, out, 4 + 2 * core, 2, own, 2 * core, LAYERS)
    for i in range(2):
        out[2 - 2 * core + i] = rest[i]
    if final:
        sums = half_sums(lambda j: (out[0, j] + out[1, j]) + (out[2, j] + out[3, j]))
        means = exact_dot(jnp.concatenate(sums, axis=0), fours((512, 128), 0)) * (1.0 / 64)
        for h in range(2):
            left = means[8 * h : 8 * h + 8] - later[h]
            for copy in range(residual.shape[0]):
                residual[copy, h] = left
    else:
        for i in range(2):
            next_near[i] = out[2 * core + i]


def coarse_step(read, weights, write, begin, end, count):
    behind, now = read((begin - 1) % count), read(begin)
    for x in range(begin, end):
        ahead = read((x + 1) % count)
        for h in range(2):
            behind_y = now[0] if h else pltpu.roll(now[1], 1, 0)
            ahead_y = pltpu.roll(now[0], 7, 0) if h else now[1]
            behind_z = pltpu.roll(now[h], 1, 1)
            ahead_z = pltpu.roll(now[h], 127, 1)
            write(
                x,
                h,
                (weights[x, 0, h] * now[h] + weights[x, 1, h] * behind[h])
                + (weights[x, 2, h] * ahead[h] + weights[x, 3, h] * behind_y)
                + (weights[x, 4, h] * ahead_y + weights[x, 5, h] * behind_z)
                + weights[x, 6, h] * ahead_z,
            )
        behind, now = now, ahead


def mask_of(i):
    return 8 * (i & 3) | ((i >> 1) & 2) | ((i >> 1) & 4) | (i >> 4)


def coarse_weight_kernel(place, some, others, weights):
    row = place[1]
    half = some.shape[0]
    for i in range(2 * half):
        x = row ^ mask_of(i)
        for h in range(2):
            parts = [(some if i < half else others)[i % half, f, h] for f in range(4)]
            for k, weight in enumerate(weigh(parts[:3], parts[3], STEP * RATIO, 1.0 * RATIO)):
                weights[x, k, h] = weight


def chain_kernel(place, residuals, given, shares, weights, one, two):
    count = weights.shape[0]
    slices = shares.shape[0]
    slice_index = place[0]
    layer_index = place[1]
    middle = count // 2
    shares[...] = jnp.zeros(shares.shape, F32)
    for x in range(count):
        at = (x - layer_index + middle) & (count - 1)
        weights[at] = given[x]
        one[at] = residuals[x]

    def reader(ref):
        return lambda x: [ref[x, h] for h in range(2)]

    def writer(ref):
        def write(x, h, value):
            ref[x, h] = value

        return write

    def propagate(ranges):
        for (source, target), (begin, end) in zip(((one, two), (two, one)) * 2, ranges, strict=True):
            coarse_step(reader(source), weights, writer(target), begin, end, count)

    def share(n):
        for h in range(2):
            shares[n, h] = one[middle, h]

    def link(n, carry):
        propagate([(0, count)] * 4)
        share(n)
        return carry

    narrow = 4
    lax.fori_loop(slice_index + 1, slices - narrow, link, 0)
    for left in range(narrow - 1, -1, -1):

        @pl.when(slices - 1 - slice_index > left)
        def _(left=left):
            reach = [COARSE_STEPS * left + COARSE_STEPS - 1 - step for step in range(COARSE_STEPS)]
            propagate([(middle - r, middle + r + 1) for r in reach])
            share(slices - 1 - left)


def finish_kernel(shares, state, out, buffer):
    change = []
    for h in range(2):
        total = shares[0, h]
        for n in range(1, shares.shape[0]):
            total = total + shares[n, h]
        change.append(total)
    wide = exact_dot(jnp.concatenate(change, axis=0), fours((128, 512), 1))
    for x in range(LAYERS):
        for j in range(8):
            h = j // 4
            tile = state[x, j] + wide[8 * h : 8 * h + 8]
            for c in range(4):
                buffer[x, c, pl.ds(j, 8, stride=8), :] = tile[:, 128 * c : 128 * c + 128]
        for c in range(4):
            out[0, x, :, 128 * c : 128 * c + 128] = buffer[x, c]


def swap_inner(block):
    count = lax.axis_size("space")
    return lax.ppermute(block, "space", [(p, p ^ 1) for p in range(count)])


def outer_partner(p, count):
    return (p + 1) % count if p % 2 else (p - 1) % count


def swap_outer(block):
    count = lax.axis_size("space")
    return lax.ppermute(block, "space", [(p, outer_partner(p, count)) for p in range(count)])


def swap_outer_fields(block):
    slices, count = lax.axis_size("cuts"), lax.axis_size("space")
    route = []
    for n in range(slices):
        there = (n + slices // 2) % slices
        route += [(n * count + p, there * count + outer_partner(p, count)) for p in range(count)]
    return lax.ppermute(block, ("cuts", "space"), route)


def across(block, bits):
    slices, count = lax.axis_size("cuts"), lax.axis_size("space")
    if bits == 2:
        route = [
            (n * count + p, (n + slices // 2) % slices * count + (p ^ bits)) for n in range(slices) for p in range(count)
        ]
        return lax.ppermute(block, ("cuts", "space"), route)
    return lax.ppermute(block, "space", [(p, p ^ bits) for p in range(count)])


def shards(starts, velocity, diffusivity):
    count = lax.axis_size("space")
    slices = lax.axis_size("cuts")
    block = (LAYERS, *TILE)
    row = lax.axis_index("space")
    place = jnp.stack([lax.axis_index("cuts"), row, row & 1]).astype(jnp.int32)
    columns = pltpu.VMEM((5, 4, 64, 128), F32)

    fields_outer = call(
        cut_fields_kernel,
        [(3 * REACH, 64, 512)],
        [SMEM, ANY],
        [pltpu.SemaphoreType.DMA((3,))],
        cost=SMALL,
    )(place, velocity)[0]
    mixed_outer, all_inner = call(
        cut_kernel,
        [(LAYERS + REACH, 64, 512), (INNER, 64, 512)],
        [SMEM, ANY, ANY, ANY, ANY],
        [pltpu.SemaphoreType.DMA((7,))],
        cost=SMALL,
    )(place, velocity, diffusivity, starts, fields_outer)
    fields_outer = swap_outer_fields(fields_outer)
    mixed_outer = swap_outer(mixed_outer)
    all_inner = swap_inner(all_inner)
    own_weights, coarse_fields, coarse_old = call(
        own_kernel,
        [(LAYERS, 7, *TILE), (4, *COARSE), COARSE],
        [VMEM] * 3,
        [columns],
        cost=SMALL,
    )(velocity, diffusivity, starts[0])
    coarse_later = lax.ppermute(coarse_old, "cuts", [((n + 1) % slices, n) for n in range(slices)])
    gathered = coarse_fields[None]
    side = [(REACH, 7, *TILE)]
    inner_weights = call(functools.partial(side_kernel, STATE_AT + LAYERS), side, [VMEM, ANY], [columns], cost=SMALL)(
        all_inner, coarse_old
    )[0]
    pair = (2, *TILE)
    scratch = [pltpu.VMEM((3 * LAYERS, *TILE), F32)] * 2
    parts = [gathered] + [across(gathered, bits) for bits in (8, 16, 24)]
    passed = call(
        first_inner_kernel,
        [(LAYERS - 1, *pair)],
        [SMEM] + [VMEM] * 4,
        scratch + [columns],
    )(place, starts[0], all_inner, own_weights, inner_weights)[0]
    outer_weights = call(functools.partial(side_kernel, LAYERS), side, [VMEM, VMEM, ANY], [columns], cost=SMALL)(
        fields_outer, mixed_outer, passed
    )[0]
    state, near, far, gathered = call(
        first_outer_kernel,
        [block, pair, pair, (4, 4, *COARSE)],
        [SMEM] + [VMEM] * (5 + len(parts)),
        scratch + [columns],
    )(place, starts[0], mixed_outer, own_weights, outer_weights, passed, *parts)
    for index in range(1, ROUNDS):
        final = index == ROUNDS - 1
        near, inner, far = swap_outer(near), swap_inner(state), swap_outer(far)
        passed, rest = call(
            near_kernel,
            [(LAYERS - 1, *pair), pair],
            [SMEM] + [VMEM] * 6,
            scratch,
        )(place, state, inner, near, own_weights, inner_weights, outer_weights)
        operands = [place, near, far, own_weights, outer_weights, passed, rest]
        specs = [SMEM] + [VMEM] * 6
        if final:
            weights = call(
                coarse_weight_kernel,
                [(count, 7, *COARSE)],
                [SMEM, VMEM, VMEM],
            )(place, gathered, across(gathered, 1))[0]
            operands += [coarse_later, weights]
            specs += [VMEM, ANY]
            outs = [block, (count, *COARSE)]
        else:
            parts = [gathered, across(gathered, (2, 4)[index - 1])]
            operands += parts + [coarse_later if index == 2 else coarse_old]
            specs += [VMEM] * len(parts) + [ANY]
            outs = [block, pair, (2 * gathered.shape[0], 4, *COARSE)]
        state, *near, gathered = call(functools.partial(far_kernel, final), outs, specs, scratch)(*operands)
        near, far = near[0] if near else None, rest
    residuals = lax.all_to_all(gathered, "space", 0, 0)
    shares = call(
        chain_kernel,
        [(slices, *COARSE)],
        [SMEM, VMEM, VMEM],
        [pltpu.VMEM((count, 7, *COARSE), F32)] + [pltpu.VMEM((count, *COARSE), F32)] * 2,
    )(place, residuals, weights)[0]
    shares = lax.all_to_all(shares, "cuts", 0, 0)
    return call(finish_kernel, [(1, LAYERS, 64, 512)], [VMEM, VMEM], [columns])(shares, state)[0]


def solution(mesh):
    placed = (P("cuts", "space", None, None), P(None, "space", None, None), P("space", None, None))
    return jax.shard_map(
        shards,
        mesh=mesh,
        in_specs=placed,
        out_specs=P("cuts", "space", None, None),
        check_vma=False,
    )
```

```python
import functools

import jax
import jax.numpy as jnp
from jax import lax
from jax.experimental import pallas as pl
from jax.experimental.pallas import tpu as pltpu
from jax.sharding import PartitionSpec as P

RATIO = 4
LAYERS = 4
COARSE_STEPS = 4
REACH = 3
ROUNDS = 4
TILE = (8, 8, 512)
COARSE = (2, 8, 128)
STEP = 0.2
VMEM = pl.BlockSpec(memory_space=pltpu.VMEM)
SMEM = pl.BlockSpec(memory_space=pltpu.SMEM)
ANY = pl.BlockSpec(memory_space=pl.ANY)
F32 = jnp.float32
MIB = 1024 * 1024
SMALL = pl.CostEstimate(flops=1, bytes_accessed=1, transcendentals=0)


def call(body, outs, ins, scratch=(), limit=24, cost=None):
    return pl.pallas_call(
        body,
        out_shape=[jax.ShapeDtypeStruct(s, F32) for s in outs],
        in_specs=ins,
        out_specs=[VMEM] * len(outs),
        scratch_shapes=list(scratch),
        cost_estimate=cost,
        compiler_params=pltpu.CompilerParams(vmem_limit_bytes=limit * MIB),
    )


def fours(shape, fine):
    z = lax.broadcasted_iota(jnp.int32, shape, fine)
    block = lax.broadcasted_iota(jnp.int32, shape, 1 - fine)
    return jnp.where((z >> 2) == block, 1.0, 0.0).astype(jnp.bfloat16)


def exact_dot(rows, matrix):
    count = rows.shape[0]
    high = rows.astype(jnp.bfloat16)
    rest = rows - high.astype(F32)
    middle = rest.astype(jnp.bfloat16)
    low = (rest - middle.astype(F32)).astype(jnp.bfloat16)
    parts = jnp.concatenate([high, middle, low], axis=0)
    moved = jnp.dot(parts, matrix, preferred_element_type=F32)
    return (moved[:count] + moved[count : 2 * count]) + moved[2 * count :]


def spread(rows, buffer):
    for c in range(4):
        buffer[c] = rows[:, 128 * c : 128 * c + 128]


def spread_tile(buffer, j):
    return jnp.concatenate([buffer[c, pl.ds(j, 8, stride=8), :] for c in range(4)], axis=1)


def half_sums(read):
    sums = []
    for h in range(2):
        total = read(4 * h)
        for j in range(4 * h + 1, 4 * h + 4):
            total = total + read(j)
        sums.append(total)
    return sums


def weigh(velocity, diffusion, step, spacing):
    spread = diffusion * (step / (spacing * spacing))
    weights = [None]
    for component in velocity:
        moved = component * (step / spacing)
        weights.append(spread + jnp.maximum(moved, 0.0))
        weights.append(spread - jnp.minimum(moved, 0.0))
    total = weights[1]
    for weight in weights[2:]:
        total = total + weight
    weights[0] = 1.0 - total
    return weights


def run(pairs, ready):
    copies = [pltpu.make_async_copy(*pair, ready.at[i]) for i, pair in enumerate(pairs)]
    for copy in copies:
        copy.start()
    for copy in copies:
        copy.wait()


def cut_fields_kernel(place, velocity, fields, ready):
    run([(velocity.at[f, pl.ds(place[2], REACH)], fields.at[pl.ds(f * REACH, REACH)]) for f in range(3)], ready)


STATE_AT = 3 * REACH
INNER = STATE_AT + LAYERS + REACH


def cut_kernel(place, velocity, diffusivity, starts, earlier, mixed, inner, ready):
    core = place[2]
    pairs = [
        (diffusivity.at[pl.ds(core, REACH)], mixed.at[pl.ds(LAYERS, REACH)]),
        (starts.at[0], mixed.at[pl.ds(0, LAYERS)]),
        (diffusivity.at[pl.ds(1 - core, REACH)], inner.at[pl.ds(STATE_AT + LAYERS, REACH)]),
        (starts.at[0], inner.at[pl.ds(STATE_AT, LAYERS)]),
    ]
    for f in range(3):
        pairs.append((velocity.at[f, pl.ds(1 - core, REACH)], inner.at[pl.ds(f * REACH, REACH)]))
    run(pairs, ready)


def own_kernel(velocity, diffusivity, starts, weights, coarse_fields, coarse_old, buffer):
    def layer(x, carry):
        for f in range(3):
            spread(velocity[f, x], buffer.at[f])
        spread(diffusivity[x], buffer.at[3])
        for j in range(8):
            parts = [spread_tile(buffer.at[f], j) for f in range(4)]
            for i, weight in enumerate(weigh(parts[:3], parts[3], STEP, 1.0)):
                weights[x, i, j] = weight
        return carry

    lax.fori_loop(0, LAYERS, layer, 0)
    sums = []
    for f in range(5):
        layers = [velocity[f, x] if f < 3 else (diffusivity[x], starts[x])[f - 3] for x in range(LAYERS)]
        spread((layers[0] + layers[1]) + (layers[2] + layers[3]), buffer.at[f])
        sums += half_sums(lambda j, f=f: spread_tile(buffer.at[f], j))
    means = exact_dot(jnp.concatenate(sums, axis=0), fours((512, 128), 0)) * (1.0 / 64)
    for f in range(5):
        for h in range(2):
            mean = means[16 * f + 8 * h : 16 * f + 8 * h + 8]
            if f < 4:
                coarse_fields[f, h] = mean
            else:
                coarse_old[h] = mean


def side_kernel(at, *refs):
    *fields, earlier, weights, buffer = refs

    def layer(x, carry):
        for f in range(3):
            spread(fields[0][f * REACH + x], buffer.at[f])
        spread(fields[-1][at + x], buffer.at[3])
        for j in range(8):
            parts = [spread_tile(buffer.at[f], j) for f in range(4)]
            for i, weight in enumerate(weigh(parts[:3], parts[3], STEP, 1.0)):
                weights[x, i, j] = weight
        return carry

    lax.fori_loop(0, REACH, layer, 0)


def fine_layers(source, weights, target, x, wx, tx, depth):
    firsts = [source[x + i, 0] for i in range(depth)]
    lasts = [source[x + i, 7] for i in range(depth)]
    behind = [pltpu.roll(last, 1, 0) for last in lasts]
    now = firsts
    done = []
    for j in range(8):
        below, above = source[x - 1, j], source[x + depth, j]
        column = [below, *now, above]
        ahead = []
        for i in range(depth):
            if j == 7:
                ahead.append(pltpu.roll(firsts[i], 7, 0))
            else:
                ahead.append(lasts[i] if j == 6 else source[x + i, j + 1])
        for i in range(depth):
            value = (
                (weights[wx + i, 0, j] * now[i] + weights[wx + i, 1, j] * column[i])
                + (weights[wx + i, 2, j] * column[i + 2] + weights[wx + i, 3, j] * behind[i])
                + (weights[wx + i, 4, j] * ahead[i] + weights[wx + i, 5, j] * pltpu.roll(now[i], 1, 1))
                + weights[wx + i, 6, j] * pltpu.roll(now[i], 511, 1)
            )
            done.append((tx + i, j, value))
        behind, now = now, ahead
        if j % 2:
            for at, tile, value in done:
                target[at, tile] = value
            done = []


def sweep(source, goal, begin, count, weights, first, shift=0):
    def pair(i, carry):
        fine_layers(source, weights, goal, begin + 2 * i, first + 2 * i, begin + 2 * i - shift, 2)
        return carry

    if count > 1:
        lax.fori_loop(0, count // 2, pair, 0)
    if count % 2:
        last = count - 1
        fine_layers(source, weights, goal, begin + last, first + last, begin + last - shift, 1)


def join(parts, joined):
    begin = 0
    for part in parts:
        joined[begin : begin + part.shape[0]] = part[...]
        begin += part.shape[0]


def first_inner_kernel(place, state, inner, own, own_inner, passed, one, two, buffer):
    core = place[2]

    def enter(x, carry):
        blocks = ((state, x, LAYERS), (inner, STATE_AT + x, 2 * LAYERS * (1 - core)))
        for i, (ref, at, begin) in enumerate(blocks):
            spread(ref[at], buffer.at[i])
            for j in range(8):
                one[begin + x, j] = spread_tile(buffer.at[i], j)
        return carry

    lax.fori_loop(0, LAYERS, enter, 0)
    source, target = one, two
    for step in range(1, LAYERS):
        count = LAYERS - step
        sweep(source, target, LAYERS + (1 - core) * step, count, own, (1 - core) * step)
        above, below = 2 * LAYERS, step
        sweep(source, target, above - core * (above - below), count, own_inner, core * (step - 1))
        for i in range(2):
            on_first, on_second = LAYERS + step + i, 2 * LAYERS - 1 - step - i
            passed[step - 1, i] = target[on_first - core * (on_first - on_second)]
        source, target = target, source


def first_outer_kernel(place, state, outer, own, own_outer, passed, *refs):
    *parts, out, near, far, joined, one, two, buffer = refs
    join(parts, joined)
    core = place[2]

    def enter(x, carry):
        spread(outer[x], buffer.at[0])
        for j in range(8):
            one[2 * LAYERS * core + x, j] = spread_tile(buffer.at[0], j)
        return carry

    lax.fori_loop(0, LAYERS, enter, 0)
    for i in range(2):
        spread(state[2 * core + i], buffer.at[1 + i])
        for j in range(8):
            one[LAYERS + 2 * core + i, j] = spread_tile(buffer.at[1 + i], j)
    source, target = one, two
    for step in range(1, LAYERS + 1):
        ends = step == LAYERS
        goal = out if ends else target
        count = LAYERS - step
        if count:
            below, above = step, 2 * LAYERS
            sweep(source, goal, below + core * (above - below), count, own_outer, (1 - core) * (step - 1))
        sweep(source, goal, LAYERS + core * count, step, own, core * count, LAYERS if ends else 0)
        if not ends:
            for i in range(2):
                on_first, on_second = LAYERS + step + i, 2 * LAYERS - 1 - step - i
                target[on_first - core * (on_first - on_second)] = passed[step - 1, i]
        source, target = target, source
    for i in range(2):
        near[i] = out[2 * core + i]
        far[i] = out[2 - 2 * core + i]


def passed_at(step, core):
    return 2 + step + core * (6 - 2 * step)


def near_kernel(place, state, inner, near, own, own_inner, own_outer, passed, rest, one, two):
    core = place[2]

    def enter(x, carry):
        for j in range(8):
            one[LAYERS + x, j] = state[x, j]
            one[2 * LAYERS * (1 - core) + x, j] = inner[x, j]
        return carry

    lax.fori_loop(0, LAYERS, enter, 0)
    for i in range(2):
        one[2 + 6 * core + i] = near[i]
    sweep(one, two, 3 + 5 * core, 1, own_outer, 2 - 2 * core)
    sweep(one, two, 4, 4, own, 0)
    sweep(one, two, 8 - 7 * core, 3, own_inner, 0)
    for i in range(2):
        passed[0, i] = two[passed_at(1, core) + i]
    sweep(two, one, 4, 4, own, 0)
    sweep(two, one, 8 - 6 * core, 2, own_inner, core)
    for i in range(2):
        passed[1, i] = one[passed_at(2, core) + i]
    sweep(one, two, 5 - core, 3, own, 1 - core)
    sweep(one, two, 8 - 5 * core, 1, own_inner, 2 * core)
    for i in range(2):
        passed[2, i] = two[passed_at(3, core) + i]
    sweep(two, rest, 6 - 2 * core, 2, own, 2 - 2 * core, 6 - 2 * core)


def far_kernel(final, place, near, far, own, own_outer, passed, rest, *refs):
    if final:
        later, after, out, residual, one, two = refs
    else:
        *parts, early, out, next_near, joined, one, two = refs
        join(parts, joined)
    core = place[2]
    for i in range(2):
        one[10 * core + i] = far[i]
        one[2 + 6 * core + i] = near[i]
    sweep(one, two, 1 + 8 * core, 2, own_outer, core)
    for i in range(2):
        two[passed_at(1, core) + i] = passed[0, i]
    sweep(two, one, 2 + 6 * core, 2, own_outer, 1 - core)
    for i in range(2):
        one[passed_at(2, core) + i] = passed[1, i]
    sweep(one, two, 3 + 5 * core, 1, own_outer, 2 - 2 * core)
    sweep(one, two, 4 + 3 * core, 1, own, 3 * core)
    for i in range(2):
        two[passed_at(3, core) + i] = passed[2, i]
    sweep(two, out, 4 + 2 * core, 2, own, 2 * core, LAYERS)
    for i in range(2):
        out[2 - 2 * core + i] = rest[i]
    if final:
        sums = half_sums(lambda j: (out[0, j] + out[1, j]) + (out[2, j] + out[3, j]))
        means = exact_dot(jnp.concatenate(sums, axis=0), fours((512, 128), 0)) * (1.0 / 64)
        for h in range(2):
            left = means[8 * h : 8 * h + 8] - later[h]
            for copy in range(residual.shape[0]):
                residual[copy, h] = left
    else:
        for i in range(2):
            next_near[i] = out[2 * core + i]


def coarse_step(read, weights, write, begin, end, count):
    behind, now = read((begin - 1) % count), read(begin)
    for x in range(begin, end):
        ahead = read((x + 1) % count)
        for h in range(2):
            behind_y = now[0] if h else pltpu.roll(now[1], 1, 0)
            ahead_y = pltpu.roll(now[0], 7, 0) if h else now[1]
            behind_z = pltpu.roll(now[h], 1, 1)
            ahead_z = pltpu.roll(now[h], 127, 1)
            write(
                x,
                h,
                (weights[x, 0, h] * now[h] + weights[x, 1, h] * behind[h])
                + (weights[x, 2, h] * ahead[h] + weights[x, 3, h] * behind_y)
                + (weights[x, 4, h] * ahead_y + weights[x, 5, h] * behind_z)
                + weights[x, 6, h] * ahead_z,
            )
        behind, now = now, ahead


def mask_of(i):
    return 8 * (i & 3) | ((i >> 1) & 2) | ((i >> 1) & 4) | (i >> 4)


def coarse_weight_kernel(place, some, others, weights):
    row = place[1]
    half = some.shape[0]
    for i in range(2 * half):
        x = row ^ mask_of(i)
        for h in range(2):
            parts = [(some if i < half else others)[i % half, f, h] for f in range(4)]
            for k, weight in enumerate(weigh(parts[:3], parts[3], STEP * RATIO, 1.0 * RATIO)):
                weights[x, k, h] = weight


def chain_kernel(place, residuals, given, shares, weights, one, two):
    count = weights.shape[0]
    slices = shares.shape[0]
    slice_index = place[0]
    layer_index = place[1]
    middle = count // 2
    shares[...] = jnp.zeros(shares.shape, F32)
    for x in range(count):
        at = (x - layer_index + middle) & (count - 1)
        weights[at] = given[x]
        one[at] = residuals[x]

    def reader(ref):
        return lambda x: [ref[x, h] for h in range(2)]

    def writer(ref):
        def write(x, h, value):
            ref[x, h] = value

        return write

    def propagate(ranges):
        for (source, target), (begin, end) in zip(((one, two), (two, one)) * 2, ranges, strict=True):
            coarse_step(reader(source), weights, writer(target), begin, end, count)

    def share(n):
        for h in range(2):
            shares[n, h] = one[middle, h]

    def link(n, carry):
        propagate([(0, count)] * 4)
        share(n)
        return carry

    narrow = 4
    lax.fori_loop(slice_index + 1, slices - narrow, link, 0)
    for left in range(narrow - 1, -1, -1):

        @pl.when(slices - 1 - slice_index > left)
        def _(left=left):
            reach = [COARSE_STEPS * left + COARSE_STEPS - 1 - step for step in range(COARSE_STEPS)]
            propagate([(middle - r, middle + r + 1) for r in reach])
            share(slices - 1 - left)


def finish_kernel(shares, state, out, buffer):
    change = []
    for h in range(2):
        total = shares[0, h]
        for n in range(1, shares.shape[0]):
            total = total + shares[n, h]
        change.append(total)
    wide = exact_dot(jnp.concatenate(change, axis=0), fours((128, 512), 1))
    for x in range(LAYERS):
        for j in range(8):
            h = j // 4
            tile = state[x, j] + wide[8 * h : 8 * h + 8]
            for c in range(4):
                buffer[x, c, pl.ds(j, 8, stride=8), :] = tile[:, 128 * c : 128 * c + 128]
        for c in range(4):
            out[0, x, :, 128 * c : 128 * c + 128] = buffer[x, c]


def swap_inner(block):
    count = lax.axis_size("space")
    return lax.ppermute(block, "space", [(p, p ^ 1) for p in range(count)])


def outer_partner(p, count):
    return (p + 1) % count if p % 2 else (p - 1) % count


def swap_outer(block):
    count = lax.axis_size("space")
    return lax.ppermute(block, "space", [(p, outer_partner(p, count)) for p in range(count)])


def swap_outer_fields(block):
    slices, count = lax.axis_size("cuts"), lax.axis_size("space")
    route = []
    for n in range(slices):
        there = (n + slices // 2) % slices
        route += [(n * count + p, there * count + outer_partner(p, count)) for p in range(count)]
    return lax.ppermute(block, ("cuts", "space"), route)


def across(block, bits):
    slices, count = lax.axis_size("cuts"), lax.axis_size("space")
    if bits == 2:
        route = [
            (n * count + p, (n + slices // 2) % slices * count + (p ^ bits)) for n in range(slices) for p in range(count)
        ]
        return lax.ppermute(block, ("cuts", "space"), route)
    return lax.ppermute(block, "space", [(p, p ^ bits) for p in range(count)])


def shards(starts, velocity, diffusivity):
    count = lax.axis_size("space")
    slices = lax.axis_size("cuts")
    block = (LAYERS, *TILE)
    row = lax.axis_index("space")
    place = jnp.stack([lax.axis_index("cuts"), row, row & 1]).astype(jnp.int32)
    columns = pltpu.VMEM((5, 4, 64, 128), F32)

    fields_outer = call(
        cut_fields_kernel,
        [(3 * REACH, 64, 512)],
        [SMEM, ANY],
        [pltpu.SemaphoreType.DMA((3,))],
        cost=SMALL,
    )(place, velocity)[0]
    mixed_outer, all_inner = call(
        cut_kernel,
        [(LAYERS + REACH, 64, 512), (INNER, 64, 512)],
        [SMEM, ANY, ANY, ANY, ANY],
        [pltpu.SemaphoreType.DMA((7,))],
        cost=SMALL,
    )(place, velocity, diffusivity, starts, fields_outer)
    fields_outer = swap_outer_fields(fields_outer)
    mixed_outer = swap_outer(mixed_outer)
    all_inner = swap_inner(all_inner)
    own_weights, coarse_fields, coarse_old = call(
        own_kernel,
        [(LAYERS, 7, *TILE), (4, *COARSE), COARSE],
        [VMEM] * 3,
        [columns],
        cost=SMALL,
    )(velocity, diffusivity, starts[0])
    coarse_later = lax.ppermute(coarse_old, "cuts", [((n + 1) % slices, n) for n in range(slices)])
    gathered = coarse_fields[None]
    side = [(REACH, 7, *TILE)]
    inner_weights = call(functools.partial(side_kernel, STATE_AT + LAYERS), side, [VMEM, ANY], [columns], cost=SMALL)(
        all_inner, coarse_old
    )[0]
    pair = (2, *TILE)
    scratch = [pltpu.VMEM((3 * LAYERS, *TILE), F32)] * 2
    parts = [gathered] + [across(gathered, bits) for bits in (8, 16, 24)]
    passed = call(
        first_inner_kernel,
        [(LAYERS - 1, *pair)],
        [SMEM] + [VMEM] * 4,
        scratch + [columns],
    )(place, starts[0], all_inner, own_weights, inner_weights)[0]
    outer_weights = call(functools.partial(side_kernel, LAYERS), side, [VMEM, VMEM, ANY], [columns], cost=SMALL)(
        fields_outer, mixed_outer, passed
    )[0]
    state, near, far, gathered = call(
        first_outer_kernel,
        [block, pair, pair, (4, 4, *COARSE)],
        [SMEM] + [VMEM] * (5 + len(parts)),
        scratch + [columns],
    )(place, starts[0], mixed_outer, own_weights, outer_weights, passed, *parts)
    for index in range(1, ROUNDS):
        final = index == ROUNDS - 1
        near, inner, far = swap_outer(near), swap_inner(state), swap_outer(far)
        passed, rest = call(
            near_kernel,
            [(LAYERS - 1, *pair), pair],
            [SMEM] + [VMEM] * 6,
            scratch,
        )(place, state, inner, near, own_weights, inner_weights, outer_weights)
        operands = [place, near, far, own_weights, outer_weights, passed, rest]
        specs = [SMEM] + [VMEM] * 6
        if final:
            weights = call(
                coarse_weight_kernel,
                [(count, 7, *COARSE)],
                [SMEM, VMEM, VMEM],
            )(place, gathered, across(gathered, 1))[0]
            operands += [coarse_later, weights]
            specs += [VMEM, ANY]
            outs = [block, (count, *COARSE)]
        else:
            parts = [gathered, across(gathered, (2, 4)[index - 1])]
            operands += parts + [coarse_later if index == 1 else coarse_old]
            specs += [VMEM] * len(parts) + [ANY]
            outs = [block, pair, (2 * gathered.shape[0], 4, *COARSE)]
        state, *near, gathered = call(functools.partial(far_kernel, final), outs, specs, scratch)(*operands)
        near, far = near[0] if near else None, rest
    residuals = lax.all_to_all(gathered, "space", 0, 0)
    shares = call(
        chain_kernel,
        [(slices, *COARSE)],
        [SMEM, VMEM, VMEM],
        [pltpu.VMEM((count, 7, *COARSE), F32)] + [pltpu.VMEM((count, *COARSE), F32)] * 2,
    )(place, residuals, weights)[0]
    shares = lax.all_to_all(shares, "cuts", 0, 0)
    return call(finish_kernel, [(1, LAYERS, 64, 512)], [VMEM, VMEM], [columns])(shares, state)[0]


def solution(mesh):
    placed = (P("cuts", "space", None, None), P(None, "space", None, None), P("space", None, None))
    return jax.shard_map(
        shards,
        mesh=mesh,
        in_specs=placed,
        out_specs=P("cuts", "space", None, None),
        check_vma=False,
    )
```
